32 devices in a mesh: wide: 8 (over z, x), narrow: 4 (over y, core).
Axes of the slice: x: 2, y: 2, z: 4, core: 2. Of those that a mesh axis runs over, the one named last changes fastest.
Arguments:
- tokens: bfloat16 [16, 1024, 768], P('wide', 'narrow'), may hold values from -6 to 6
- lengths: int32 [16], P('wide'), may hold values from 640 to 1024, as said below
- tissues: int32 [16], P('wide'), may hold values from 0 to 7
- ln1_gain: float32 [768], replicated, may hold values from 0.5 to 1.5
- ln1_bias: float32 [768], replicated, may hold values from -1 to 1
- qkv_weight: bfloat16 [768, 2304], P(None, 'narrow'), may hold values from -0.21875 to 0.21875
- qkv_bias: float32 [2304], P('narrow'), may hold values from -1 to 1
- dense_weight: bfloat16 [768, 768], P('narrow'), may hold values from -3.5 to 3.5
- dense_bias: float32 [768], replicated, may hold values from -2.5 to 2.5
- ln2_gain: float32 [768], replicated, may hold values from 0.5 to 1.5
- ln2_bias: float32 [768], replicated, may hold values from -1 to 1
- up_weight: bfloat16 [768, 3072], P(None, 'narrow'), may hold values from -0.21875 to 0.21875
- up_bias: float32 [3072], P('narrow'), may hold values from -1.5 to 1.5
- down_weight: bfloat16 [3072, 768], P('narrow'), may hold values from -0.109375 to 0.109375
- down_bias: float32 [768], replicated, may hold values from -2.5 to 2.5
- out_probe: bfloat16 [16, 1024, 768], P('wide', 'narrow'), may hold values from -6 to 6
Outputs:
- block_out: bfloat16 [16, 1024, 768], P('wide', 'narrow')
- grad_tokens: float32 [16, 1024, 768], P('wide', 'narrow')
- grad_ln1_gain: float32 [768], P('narrow')
- grad_ln1_bias: float32 [768], P('narrow')
- grad_qkv_weight: float32 [768, 2304], P(None, 'narrow')
- grad_qkv_bias: float32 [2304], P('narrow')
- grad_dense_weight: float32 [768, 768], P('narrow')
- grad_dense_bias: float32 [768], P('narrow')
- grad_ln2_gain: float32 [768], P('narrow')
- grad_ln2_bias: float32 [768], P('narrow')
- grad_up_weight: float32 [768, 3072], P(None, 'narrow')
- grad_up_bias: float32 [3072], P('narrow')
- grad_down_weight: float32 [3072, 768], P('narrow')
- grad_down_bias: float32 [768], P('narrow')
The draws below stay inside these ranges and needn't reach their ends.
Inputs may be any that keep to these rules, and one draw needn't show every extreme that they name: `lengths`: in each aligned block of 2 rows, one row has all 1024 slots in use.
All inputs are finite; a program needn't handle non-finite values.
Results may differ from the reference program's by a relative error of at most 0.017.
Values may be sent and summed in bfloat16 or wider, within the bound.
No kernel may reach another device: no remote copies, remote signals or barrier semaphores. Data moves between devices by JAX's collectives and lax.ppermute only.
A program may use at most 128 MiB of HBM per device.

```python
import math
import jax
import jax.numpy as jnp
from jax import lax

D = 768
HEADS = 12
HEAD = 64
FF = 3072
ROT = 16
SLOTS = 1024
TISSUES = 8
ROWS_DEV = 2
ROWS = 16
N_NARROW = 4


def draw_lengths(key, part):
    key = jax.random.fold_in(key, 1)
    first_key, second_key = jax.random.split(key)
    base_lengths = jax.random.randint(first_key, (ROWS,), 5 * SLOTS // 8, SLOTS + 1)
    chosen = jax.random.randint(second_key, (ROWS // ROWS_DEV, 1), 0, ROWS_DEV)
    full_rows = (jnp.arange(ROWS_DEV)[None, :] == chosen).reshape(ROWS)
    return jnp.where(full_rows, SLOTS, base_lengths).astype(jnp.int32)


def place_ends(entries, stream_key, smallest, high):
    longest = entries.shape.index(max(entries.shape))
    spots = []
    for shift in (0, 1):
        where = [jax.random.randint(jax.random.fold_in(stream_key, axis), (), 0, length) for axis, length in enumerate(entries.shape)]
        where[longest] = (where[longest] + shift) % entries.shape[longest]
        spots.append(tuple(where))
    return entries.at[spots[0]].set(smallest).at[spots[1]].set(high)


def block_levels(key, dims, shards, smallest, largest):
    def one(dim, shards_of):
        steps = jax.random.uniform(jax.random.fold_in(jax.random.fold_in(key, 6), dim), (shards_of,), jnp.float32, smallest / len(shards), largest / len(shards))
        return jnp.repeat(jnp.exp(steps), dims[dim] // shards_of).reshape((-1,) + (1,) * (len(dims) - dim - 1))

    factor_of = one(*shards[0])
    for cut in shards[1:]:
        factor_of = factor_of * one(*cut)
    return factor_of


def centred(stream_key, extent, deviation, most, cuts=(), dtype=jnp.bfloat16):
    values = jax.random.normal(stream_key, extent, jnp.float32) * deviation
    if len(cuts) > 0:
        values = block_levels(stream_key, extent, cuts, -0.22, 0.18) * values
    return jnp.clip(values, min=-most, max=most).astype(dtype)


def setup_inputs(seed: int = 0) -> dict:
    splits = jax.random.split(jax.random.key(seed), 17)
    tokens = centred(splits[0], (ROWS, SLOTS, D), 1.0, 6.0, ((0, 8), (1, 4)))
    lengths = draw_lengths(jax.random.fold_in(splits[16], 71), 0)
    tissues = place_ends(jax.random.randint(splits[2], (ROWS,), 0, TISSUES), jax.random.fold_in(splits[2], 1), 0, TISSUES - 1).astype(jnp.int32)
    ln1_gain = jnp.clip(1.0 + 0.1 * jax.random.normal(splits[3], (D,), jnp.float32), 0.5, 1.5)
    ln1_bias = centred(splits[4], (D,), 0.2, 1.0, (), jnp.float32)
    qkv_weight = centred(splits[5], (D, 3 * D), D ** -0.5, 0.21875, ((1, 4),))
    qkv_bias = centred(splits[6], (3 * D,), 0.2, 1.0, ((0, 4),), jnp.float32)
    dense_weight = centred(splits[7], (D, D), (max(D // 256, 3)) ** -0.5, 3.5, ((0, 4),))
    dense_bias = centred(splits[8], (D,), 0.5, 2.5, (), jnp.float32)
    ln2_gain = jnp.clip(1.0 + 0.1 * jax.random.normal(splits[9], (D,), jnp.float32), 0.5, 1.5)
    ln2_bias = centred(splits[10], (D,), 0.2, 1.0, (), jnp.float32)
    up_weight = centred(splits[11], (D, FF), D ** -0.5, 0.21875, ((1, 4),))
    up_bias = centred(splits[12], (FF,), 0.3, 1.5, ((0, 4),), jnp.float32)
    down_weight = centred(splits[13], (FF, D), FF ** -0.5, 0.109375, ((0, 4),))
    down_bias = centred(splits[14], (D,), 0.5, 2.5, (), jnp.float32)
    out_probe = centred(splits[15], (ROWS, SLOTS, D), 1.0, 6.0, ((0, 8), (1, 4)))
    return {"tokens": tokens, "lengths": lengths, "tissues": tissues, "ln1_gain": ln1_gain, "ln1_bias": ln1_bias, "qkv_weight": qkv_weight, "qkv_bias": qkv_bias, "dense_weight": dense_weight, "dense_bias": dense_bias, "ln2_gain": ln2_gain, "ln2_bias": ln2_bias, "up_weight": up_weight, "up_bias": up_bias, "down_weight": down_weight, "down_bias": down_bias, "out_probe": out_probe}


epsilon = 1e-05
negative_big = -1e+30

@jax.custom_vjp
def low(v):
    return lax.optimization_barrier(v.astype(jnp.bfloat16)).astype(jnp.float32)

@jax.custom_vjp
def low_back(v):
    return v

def low_keep(v):
    return (low(v), None)

def low_pass(kept, grad):
    return (grad,)

def back_keep(v):
    return (v, None)

def back_low(kept, grad):
    return (low(grad),)
low.defvjp(low_keep, low_pass)
low_back.defvjp(back_keep, back_low)

def layer_norm(values, norm_gain, norm_shift):
    row_mean = lax.optimization_barrier(jnp.mean(values, axis=-1, keepdims=True))
    centered = values - row_mean
    inverse = lax.rsqrt(lax.optimization_barrier(jnp.mean(centered * centered, axis=-1, keepdims=True)) + epsilon)
    return centered * inverse * norm_gain + norm_shift

def tables(slot_count):
    position = jnp.arange(slot_count).astype(jnp.float32)
    frequency = 10000.0 ** (-(2.0 * jnp.arange(ROT // 2).astype(jnp.float32)) / ROT)
    angles = position[:, None] * frequency[None, :]
    angles = jnp.concatenate([angles, angles], axis=1)
    return (jnp.cos(angles), jnp.sin(angles))

def rotate(values, cos_table, sin_table):
    rotary_part = values[..., :ROT]
    low_half = rotary_part[..., :ROT // 2]
    high_half = rotary_part[..., ROT // 2:]
    turned = jnp.concatenate([-high_half, low_half], axis=-1)
    rotated = rotary_part * cos_table[:, None, :] + turned * sin_table[:, None, :]
    return jnp.concatenate([rotated, values[..., ROT:]], axis=-1)

def grouped_input(normed, weight):
    groups = N_NARROW
    columns = weight.shape[1] // groups
    copies = low_back(jnp.broadcast_to(normed[None], (groups,) + normed.shape))
    weight_parts = weight.reshape(weight.shape[0], groups, columns).transpose(1, 0, 2)
    result = jnp.einsum('gsd,gdk->sgk', copies, weight_parts, precision=lax.Precision.HIGHEST)
    return result.reshape(normed.shape[0], groups * columns)

def grouped_output(left, weight):
    groups = N_NARROW
    inner = weight.shape[0] // groups
    left_parts = left.reshape(left.shape[0], groups, inner)
    weight_parts = weight.reshape(groups, inner, weight.shape[1])
    return jnp.einsum('sgk,gkd->gsd', left_parts, weight_parts, precision=lax.Precision.HIGHEST)

def row_forward(row_tokens, row_length, params):
    ln1_gain, ln1_bias, qkv_weight, qkv_bias, dense_weight, dense_bias, ln2_gain, ln2_bias, up_weight, up_bias, down_weight, down_bias = params
    score_scale = 1.0 / math.sqrt(HEAD)
    normed_one = low(layer_norm(row_tokens, ln1_gain, ln1_bias))
    normed_two = low(layer_norm(row_tokens, ln2_gain, ln2_bias))
    joined = low_back(grouped_input(normed_one, qkv_weight) + qkv_bias)
    joined = joined.reshape(SLOTS, HEADS, 3, HEAD)
    cos_table, sin_table = tables(SLOTS)
    queries = low(rotate(joined[:, :, 0], cos_table, sin_table))
    keys_all = low(rotate(joined[:, :, 1], cos_table, sin_table))
    values_all = low(joined[:, :, 2])
    scores = jnp.einsum('qhd,khd->hqk', queries, keys_all, precision=lax.Precision.HIGHEST) * score_scale
    scores = low_back(scores)
    position = jnp.arange(SLOTS)
    allowed = (position[None, :] <= position[:, None]) & (position[None, :] < row_length)
    scores = jnp.where(allowed[None], scores, negative_big)
    probs = jax.nn.softmax(scores, axis=-1)
    context = jnp.einsum('hqk,khd->qhd', low(probs), values_all, precision=lax.Precision.HIGHEST)
    context = low_back(low(context.reshape(SLOTS, HEADS * HEAD)))
    hidden = low_back(grouped_input(normed_two, up_weight) + up_bias)
    active = low(jax.nn.gelu(hidden, approximate=False))
    partial_value = grouped_output(context, dense_weight) + grouped_output(active, down_weight)
    branch = low_back(lax.optimization_barrier(jnp.sum(low(partial_value), axis=0)) + dense_bias + down_bias)
    return row_tokens + branch

def reference(tokens, lengths, tissues, ln1_gain, ln1_bias, qkv_weight, qkv_bias, dense_weight, dense_bias, ln2_gain, ln2_bias, up_weight, up_bias, down_weight, down_bias, out_probe):
    params = tuple((entry.astype(jnp.float32) for entry in (ln1_gain, ln1_bias, qkv_weight, qkv_bias, dense_weight, dense_bias, ln2_gain, ln2_bias, up_weight, up_bias, down_weight, down_bias)))
    tissue_hits = (tissues[:, None] == jnp.arange(TISSUES)[None, :]).astype(jnp.float32)
    counts = lax.optimization_barrier(jnp.sum(tissue_hits * lengths[:, None].astype(jnp.float32), axis=0))
    row_count = lax.optimization_barrier(jnp.sum(tissue_hits * counts[None, :], axis=1))
    row_weight = ROWS * SLOTS / TISSUES / row_count
    valid = (jnp.arange(SLOTS)[None, :] < lengths[:, None]).astype(jnp.float32)
    cotangent = out_probe.astype(jnp.float32) * (valid * row_weight[:, None])[:, :, None]

    def forward(all_tokens, weights):

        def one_row(carried):
            return jax.checkpoint(row_forward)(carried[0], carried[1], weights)
        return lax.map(one_row, (all_tokens, lengths))
    block_out, pull_back = jax.vjp(forward, tokens.astype(jnp.float32), params)
    grad_tokens, grads = pull_back(cotangent)
    return (block_out.astype(jnp.bfloat16), grad_tokens, grads[0], grads[1], grads[2], grads[3], grads[4], grads[5], grads[6], grads[7], grads[8], grads[9], grads[10], grads[11])
```

```python
import functools
import math

import jax
import jax.numpy as jnp
from jax import lax
from jax.experimental import pallas as pl
from jax.experimental.pallas import tpu as pltpu
from jax.sharding import PartitionSpec as P

HEAD = 64
ROT = 16
TISSUES = 8
LANES = 128
EPS = 1e-05
BIG = -1e30
F32 = jnp.float32
BF16 = jnp.bfloat16
ERF_P = 0.39
ERF_C = (
    0.2353254092560988,
    0.09138720671028266,
    0.6495624403330551,
    -0.6354040754153405,
    0.8866667192133076,
    -0.22753770177595345,
)

NN = (((1,), (0,)), ((), ()))
NT = (((1,), (1,)), ((), ()))
TN = (((0,), (0,)), ((), ()))


def mm(a, b, dims=NN):
    return lax.dot_general(a, b, dims, preferred_element_type=F32)


def norm_parts(tokens):
    values = tokens.astype(F32)
    centered = values - jnp.mean(values, axis=-1, keepdims=True)
    inverse = lax.rsqrt(jnp.mean(centered * centered, axis=-1, keepdims=True) + EPS)
    return centered * inverse, inverse


def gelu_pair(x):
    size = jnp.abs(x)
    t = 1.0 / (1.0 + (ERF_P * math.sqrt(0.5)) * size)
    bell = jnp.exp(-0.5 * (x * x))
    poly = jnp.full_like(x, 0.5 * ERF_C[-1])
    for c in ERF_C[-2::-1]:
        poly = poly * t + 0.5 * c
    tail = poly * t * bell
    phi = jnp.where(x < 0, tail, 1.0 - tail)
    return x * phi, phi + x * (bell * (1.0 / math.sqrt(2.0 * math.pi)))


def turn(x, cos_t, low_t, high_t, sign):
    up = pltpu.roll(x, LANES - ROT // 2, 1)
    down = pltpu.roll(x, ROT // 2, 1)
    return x * cos_t + sign * (up * low_t + down * high_t)


def place_two(c, first, second):
    a = jnp.where(c == 0, first, second)
    b = jnp.where(c == 0, second, first)
    return jnp.concatenate([a, b], axis=0)


def out_grad_of(probe, first_slot, length, weight):
    slot = first_slot + lax.broadcasted_iota(jnp.int32, (probe.shape[0], 1), 0)
    scale = jnp.where(slot < length, weight, 0.0)
    return (probe.astype(F32) * scale).astype(BF16)


def qkv_kernel(ints, x0, x1, weight, bias, gain, shift, cos_t, low_t, high_t, out):
    c, half = ints[0], ints[1]
    tokens = place_two(c, x0[0], x1[0])
    rows = tokens.shape[0]
    xhat, _ = norm_parts(tokens)
    normed = (xhat * gain[...] + shift[...]).astype(BF16)
    spots = pl.ds(pl.multiple_of(half * rows, rows), rows)
    cos_b, low_b, high_b = cos_t[spots, :], low_t[spots, :], high_t[spots, :]
    for part in range(3):
        joined = mm(normed, weight[:, part * 256 : part * 256 + 256])
        joined = joined + bias[:, part * 256 : part * 256 + 256]
        for pair in range(2):
            x = joined[:, pair * LANES : pair * LANES + LANES]
            if part < 2:
                x = turn(x, cos_b, low_b, high_b, 1.0)
            x = x.astype(BF16)
            if part == 0:
                x = x * jnp.asarray(1.0 / math.sqrt(HEAD), BF16)
            at = part * 256 + pair * LANES
            out[:, at : at + LANES] = x


def mlp_kernel(first, last, ints, weights, x0, x1, up, up_b, down, dense, gain, shift, *rest):
    if first:
        ug_in = dg_in = sums_in = None
    else:
        ug_in, dg_in, sums_in = rest[:3]
        rest = rest[3:]
    active_o, cgrad_o, u_o, ug_o, dg_o, sums_o = rest
    c, half, length = ints[0], ints[1], ints[2]
    tokens = place_two(c, x0[0], x1[0])
    probe = place_two(c, x0[1], x1[1])
    rows, width = tokens.shape
    xhat, _ = norm_parts(tokens)
    normed = (xhat * gain[...] + shift[...]).astype(BF16)
    grad = out_grad_of(probe, half * rows, length, weights[0])
    cgrad_o[...] = mm(grad, dense[...], NT).astype(BF16)
    inner = up.shape[1]
    step = 256
    total = None
    for at in range(0, inner, step):
        cols = slice(at, at + step)
        hidden = mm(normed, up[:, cols]) + up_b[:, cols]
        active, slope = gelu_pair(hidden)
        active = active.astype(BF16)
        active_o[:, cols] = active
        hgrad = (mm(grad, down[cols, :], NT) * slope).astype(BF16)
        piece = mm(hgrad, up[:, cols], NT)
        total = piece if total is None else total + piece
        ug = mm(normed, hgrad, TN)
        dg = mm(active, grad, TN)
        us = jnp.sum(hgrad.astype(F32), axis=0, keepdims=True)
        if not first:
            ug = ug + ug_in[:, cols]
            dg = dg + dg_in[cols, :]
            us = us + sums_in[2:3, cols]
        ug_o[:, cols] = ug.astype(ug_o.dtype)
        dg_o[cols, :] = dg.astype(dg_o.dtype)
        sums_o[2:3, cols] = us
    u_o[...] = (total * gain[...]).astype(u_o.dtype)
    gs = jnp.sum(total * xhat, axis=0, keepdims=True)
    ss = jnp.sum(total, axis=0, keepdims=True)
    os = jnp.sum(grad.astype(F32), axis=0, keepdims=True)
    if not first:
        gs, ss, os = gs + sums_in[0:1], ss + sums_in[1:2], os + sums_in[3:4]
    sums_o[0:1] = gs
    sums_o[1:2] = ss
    sums_o[3:4] = os


def attend_kernel(ints, near, far, cg_near, cg_far, cos_t, low_t, high_t, ctx_o, jg_o,
                  q_s, k_s, v_s, c_s, kt_s, vt_s, ct_s, dk_s, dv_s):
    y, length = ints[0], ints[1]
    half = near.shape[0]
    slots = 2 * half
    block = 256
    for source, cg, place in ((near, cg_near, y), (far, cg_far, 1 - y)):
        spots = pl.ds(pl.multiple_of(place * half, half), half)
        q_s[spots, :] = source[:, 0:256]
        k_s[spots, :] = source[:, 256:512]
        v_s[spots, :] = source[:, 512:768]
        c_s[spots, :] = cg[...]
    kt_s[...] = k_s[...].T
    vt_s[...] = v_s[...].T
    ct_s[...] = c_s[...].T
    lane = lax.broadcasted_iota(jnp.int32, (block, LANES), 1)
    heads = 3
    for i in range(slots // block - 1, -1, -1):
        rows = slice(i * block, (i + 1) * block)
        seen = (i + 1) * block
        ctx_parts, dq_parts = [], []
        for h in range(heads):
            lanes = slice((h // 2) * LANES, (h // 2) * LANES + LANES)
            lines = slice(h * HEAD, h * HEAD + HEAD)
            q, cg = q_s[rows, lanes], c_s[rows, lanes]
            if h < 2:
                mine = (lane < HEAD) if h % 2 == 0 else (lane >= HEAD)
                q = jnp.where(mine, q, jnp.zeros_like(q))
                cg = jnp.where(mine, cg, jnp.zeros_like(cg))
            scores = mm(k_s[0:seen, lanes], q, NT)
            key = lax.broadcasted_iota(jnp.int32, (seen, block), 0)
            query = i * block + lax.broadcasted_iota(jnp.int32, (seen, block), 1)
            scores = jnp.where((key <= query) & (key < length), scores, BIG)
            peak = jnp.max(scores, axis=0, keepdims=True)
            raised = jnp.exp(scores - peak)
            probs = raised * (1.0 / jnp.sum(raised, axis=0, keepdims=True))
            low = probs.astype(BF16)
            ctx = mm(vt_s[lines, 0:seen], low)
            pgrad = mm(v_s[0:seen, lanes], cg, NT)
            inner = jnp.sum(ct_s[lines, rows].astype(F32) * ctx, axis=0, keepdims=True)
            sgrad = (probs * (pgrad - inner)).astype(BF16)
            dq = mm(kt_s[lines, 0:seen], sgrad)
            dk, dv = mm(sgrad, q), mm(low, cg)
            fresh = i == slots // block - 1 and h != 1
            if fresh:
                dk_s[0:seen, lanes] = dk
                dv_s[0:seen, lanes] = dv
            else:
                dk_s[0:seen, lanes] += dk
                dv_s[0:seen, lanes] += dv
            ctx_parts.append(ctx)
            dq_parts.append(dq)
        empty = jnp.zeros((256 - heads * HEAD, block), F32)
        ctx_o[rows, :] = jnp.concatenate(ctx_parts + [empty], axis=0).T.astype(BF16)
        dq = jnp.concatenate(dq_parts + [empty], axis=0).T * (1.0 / math.sqrt(HEAD))
        for pair in range(2):
            lanes = slice(pair * LANES, pair * LANES + LANES)
            turned = turn(dq[:, lanes], cos_t[rows, :], low_t[rows, :], high_t[rows, :], -1.0)
            jg_o[rows, lanes] = turned.astype(BF16)
            turned = turn(dk_s[rows, lanes], cos_t[rows, :], low_t[rows, :], high_t[rows, :], -1.0)
            jg_o[rows, 256 + pair * LANES : 256 + pair * LANES + LANES] = turned.astype(BF16)
        jg_o[rows, 512:768] = dv_s[rows, :].astype(BF16)


def close_kernel(first, ints, weights, x0, x1, x2, x3, ctx, jg, act_n, act_f, u_n, u_f, weight, dense, down,
                 gain, shift, *rest):
    if first:
        qg_in = sg_in = None
    else:
        qg_in, sg_in = rest[:2]
        rest = rest[2:]
    send_far, send_near, keep_far, keep_near, qg_o, sums_o = rest
    c, y, length = ints[0], ints[1], ints[2]
    block = x0.shape[1]
    width = x0.shape[2]
    gs = ss = bs = qg = dg = None
    for x, act, u, side, slot, out in (
        (x2, act_f, u_f, 1 - y, c, keep_far),
        (x3, act_f, u_f, 1 - y, 1 - c, send_far),
        (x0, act_n, u_n, y, c, keep_near),
        (x1, act_n, u_n, y, 1 - c, send_near),
    ):
        place = 2 * side + slot
        whole = pl.ds(pl.multiple_of(place * block, block), block)
        part = pl.ds(pl.multiple_of(slot * block, block), block)
        context, joined = ctx[whole, :], jg[whole, :]
        out[0] = (mm(context, dense[...]) + mm(act[part, :], down[...])).astype(BF16)
        first_grad = mm(joined, weight[...], NT)
        xhat, _ = norm_parts(x[0])
        normed = (xhat * gain[...] + shift[...]).astype(BF16)
        grad = out_grad_of(x[1], place * block, length, weights[0])
        out[1] = (first_grad * gain[...] + u[part, :].astype(F32)).astype(BF16)
        pieces = (
            jnp.sum(first_grad * xhat, axis=0, keepdims=True),
            jnp.sum(first_grad, axis=0, keepdims=True),
            jnp.sum(joined.astype(F32), axis=0, keepdims=True),
            mm(normed, joined, TN),
            mm(grad, context, TN),
        )
        if gs is None:
            gs, ss, bs, qg, dg = pieces
        else:
            gs, ss, bs, qg, dg = (a + b for a, b in zip((gs, ss, bs, qg, dg), pieces))
    if first:
        qg_o[:, 0:width] = qg
        qg_o[:, width : width + 256] = dg
    else:
        gs, ss, bs = gs + sg_in[0:1], ss + sg_in[1:2], bs + sg_in[2:3]
        qg = qg + qg_in[:, 0:width]
        dg = dg + qg_in[:, width : width + 256]
        columns = []
        for h in range(3):
            for part in range(3):
                at = part * 256 + h * HEAD
                columns.append(qg[:, at : at + HEAD])
        columns.append(dg[:, 0 : 3 * HEAD])
        qg_o[...] = jnp.concatenate(columns, axis=1).astype(BF16)
    sums_o[0:1] = gs
    sums_o[1:2] = ss
    sums_o[2:3] = bs


def final_kernel(ints, weights, tokens, probe, k0, r0, y0, k1, r1, y1, dense_b, down_b, block_o, grad_o):
    place = ints[0]
    block = tokens.shape[1]
    for row, (keep, got, far) in enumerate(((k0, r0, y0), (k1, r1, y1))):
        near = keep[...].astype(F32) + got[...].astype(F32) + far[...].astype(F32)
        values = tokens[row].astype(F32)
        block_o[row] = (values + (near[0] + dense_b[...] + down_b[...])).astype(BF16)
        xhat, inverse = norm_parts(tokens[row])
        u = near[1]
        slot = place * block + lax.broadcasted_iota(jnp.int32, (block, 1), 0)
        scale = jnp.where(slot < ints[1 + row], weights[row], 0.0)
        mean = jnp.mean(u, axis=-1, keepdims=True)
        lean = jnp.mean(u * xhat, axis=-1, keepdims=True)
        grad_o[row] = probe[row].astype(F32) * scale + inverse * (u - mean - xhat * lean)


SMEM = functools.partial(pl.BlockSpec, memory_space=pltpu.SMEM)
VMEM = functools.partial(pl.BlockSpec, memory_space=pltpu.VMEM)


def call(body, outs, scalars, arrays, flops, name, scratch=(), limit=48, alias=None):
    nbytes = sum(a.size * a.dtype.itemsize for a in arrays) + sum(
        math.prod(o.shape) * jnp.dtype(o.dtype).itemsize for o in outs
    )
    return pl.pallas_call(
        body,
        out_shape=outs,
        in_specs=[SMEM()] * len(scalars) + [VMEM()] * len(arrays),
        out_specs=[VMEM()] * len(outs),
        scratch_shapes=list(scratch),
        input_output_aliases=alias or {},
        compiler_params=pltpu.CompilerParams(vmem_limit_bytes=limit * 1024 * 1024),
        cost_estimate=pl.CostEstimate(flops=int(flops), bytes_accessed=int(nbytes), transcendentals=0),
        name=name,
    )(*scalars, *arrays)


def exchange(x, axis, bit):
    size = lax.axis_size(axis)
    return lax.ppermute(x, axis, [(i, i ^ (1 << bit)) for i in range(size)])


def add_low(a, b):
    return (a.astype(F32) + b.astype(F32)).astype(BF16)


def scatter_sum(x, axis, bits):
    place = lax.axis_index(axis)
    for bit in bits:
        half = x.shape[0] // 2
        mine = (place >> bit) & 1
        keep = lax.dynamic_slice_in_dim(x, mine * half, half, 0)
        send = lax.dynamic_slice_in_dim(x, (1 - mine) * half, half, 0)
        x = add_low(keep, exchange(send, axis, bit))
    return x


def gather_back(x, axis, bits):
    place = lax.axis_index(axis)
    for bit in reversed(bits):
        mine = (place >> bit) & 1
        got = exchange(x, axis, bit)
        x = jnp.where(mine == 0, jnp.concatenate([x, got]), jnp.concatenate([got, x]))
    return x


def rotary(slot_count):
    position = jnp.arange(slot_count).astype(F32)
    frequency = 10000.0 ** (-(2.0 * jnp.arange(ROT // 2).astype(F32)) / ROT)
    angles = position[:, None] * frequency[None, :]
    cos, sin = jnp.cos(angles), jnp.sin(angles)
    ones = jnp.ones((slot_count, HEAD - ROT), F32)
    none8 = jnp.zeros_like(sin)
    none = jnp.zeros_like(ones)
    cos_t = jnp.concatenate([cos, cos, ones], axis=1)
    low_t = jnp.concatenate([-sin, none8, none], axis=1)
    high_t = jnp.concatenate([none8, sin, none], axis=1)
    return tuple(jnp.concatenate([t, t], axis=1) for t in (cos_t, low_t, high_t))


def shards(tokens, lengths, tissues, ln1_gain, ln1_bias, qkv_weight, qkv_bias, dense_weight, dense_bias,
           ln2_gain, ln2_bias, up_weight, up_bias, down_weight, down_bias, out_probe):
    rows_local, block, width = tokens.shape
    inner = up_weight.shape[1]
    wide_count, narrow_count = lax.axis_size("wide"), lax.axis_size("narrow")
    place = lax.axis_index("narrow")
    c, y = place % 2, place // 2
    slot_count = block * narrow_count
    bits = list(range(wide_count.bit_length() - 1))

    hits = (tissues[:, None] == jnp.arange(TISSUES)[None, :]).astype(F32)
    counts = jnp.sum(hits * lengths[:, None].astype(F32), axis=0)[None, :]
    for bit in bits:
        counts = counts + exchange(counts, "wide", bit)
    row_count = jnp.sum(hits * counts, axis=1)
    row_weight = rows_local * wide_count * slot_count / TISSUES / row_count

    own = [jnp.stack([tokens[r], out_probe[r]]) for r in range(rows_local)]
    mate = [exchange(x, "narrow", 0) for x in own]
    over = [exchange(x, "narrow", 1) for x in own]
    cross = [exchange(x, "narrow", 0) for x in over]

    tables = rotary(slot_count)
    weight = qkv_weight.reshape(width, 3, 3, HEAD).transpose(0, 2, 1, 3)
    weight = jnp.pad(weight.reshape(width, 3, 3 * HEAD), ((0, 0), (0, 0), (0, HEAD))).reshape(width, 768)
    q_bias = qkv_bias.reshape(3, 3, HEAD).transpose(1, 0, 2).reshape(3, 3 * HEAD)
    q_bias = jnp.pad(q_bias, ((0, 0), (0, HEAD))).reshape(1, 768)
    dense = jnp.pad(dense_weight, ((0, 256 - dense_weight.shape[0]), (0, 0)))
    g1, b1, g2, b2 = (a[None, :] for a in (ln1_gain, ln1_bias, ln2_gain, ln2_bias))
    ub = up_bias[None, :]
    half_rows = 2 * block

    def shape(*dims, dtype=BF16):
        return jax.ShapeDtypeStruct(dims, dtype)

    def ints(*values):
        return jnp.stack([jnp.asarray(v, jnp.int32) for v in values])

    def qkv(r, far):
        x0, x1 = (over[r], cross[r]) if far else (own[r], mate[r])
        return call(
            qkv_kernel,
            [shape(half_rows, 768)],
            [ints(c, 1 - y if far else y)],
            [x0, x1, weight, q_bias, g1, b1, *tables],
            2 * half_rows * width * 768,
            "qkv",
        )[0]

    def mlp(r, far, sums, last):
        x0, x1 = (over[r], cross[r]) if far else (own[r], mate[r])
        first = sums is None
        kind = BF16 if last else F32
        return call(
            functools.partial(mlp_kernel, first, last),
            [
                shape(half_rows, inner),
                shape(half_rows, 256),
                shape(half_rows, width),
                shape(width, inner, dtype=kind),
                shape(inner, width, dtype=kind),
                shape(4, width, dtype=F32),
            ],
            [ints(c, 1 - y if far else y, lengths[r]), row_weight[r : r + 1]],
            [x0, x1, up_weight, ub, down_weight, dense, g2, b2, *(sums or [])],
            2 * half_rows * width * inner * 5,
            "mlp",
        )

    near_q = [qkv(r, False) for r in range(2)]
    a00, cg00, u00, *sums = mlp(0, False, None, False)
    a10, cg10, u10, *sums = mlp(1, False, sums, False)
    far_q0 = qkv(0, True)
    a01, cg01, u01, *sums = mlp(0, True, sums, False)

    def attend(r, near, far, cg_near, cg_far):
        big = pltpu.VMEM((slot_count, 256), BF16)
        tall = pltpu.VMEM((256, slot_count), BF16)
        total = pltpu.VMEM((slot_count, 256), F32)
        return call(
            attend_kernel,
            [shape(slot_count, 256), shape(slot_count, 768)],
            [ints(y, lengths[r])],
            [near, far, cg_near, cg_far, *tables],
            12e9 / 2,
            "attend",
            scratch=[big] * 4 + [tall] * 3 + [total] * 2,
        )

    ctx0, jg0 = attend(0, near_q[0], far_q0, cg00, cg01)
    far_q1 = qkv(1, True)
    a11, cg11, u11, up_part, down_part, mlp_sums = mlp(1, True, sums, True)

    up_chunk = scatter_sum(up_part, "wide", bits)
    down_order = bits[1:] + bits[:1]
    down_chunk = scatter_sum(down_part, "wide", down_order)

    def close(r, ctx, jg, acts, us, sums):
        first = sums is None
        pair = shape(2, block, width)
        return call(
            functools.partial(close_kernel, first),
            [pair] * 4
            + [
                shape(width, width + 256, dtype=F32) if first else shape(width, 768),
                shape(3, width, dtype=F32),
            ],
            [ints(c, y, lengths[r]), row_weight[r : r + 1]],
            [own[r], mate[r], over[r], cross[r], ctx, jg, *acts, *us, weight, dense, down_weight, g1, b1, *(sums or [])],
            7.2e9 / 2,
            "close",
        )

    def reduce_rows(outs):
        send_far, send_near, keep_far, keep_near = outs
        far = add_low(keep_far, exchange(send_far, "narrow", 0))
        return keep_near, exchange(send_near, "narrow", 0), exchange(far, "narrow", 1)

    *outs, qg, close_sums = close(0, ctx0, jg0, (a00, a01), (u00, u01), None)
    row0 = reduce_rows(outs)
    ctx1, jg1 = attend(1, near_q[1], far_q1, cg10, cg11)
    *outs, last_part, close_sums = close(1, ctx1, jg1, (a10, a11), (u10, u11), [qg, close_sums])
    row1 = reduce_rows(outs)
    last_chunk = scatter_sum(last_part, "wide", bits)

    small = jnp.concatenate([close_sums[0:2], mlp_sums[0:2]], axis=0)
    for bit in range(2):
        small = small + exchange(small, "narrow", bit)
    small = jnp.concatenate([small, close_sums[2:3], mlp_sums[2:4], jnp.zeros_like(small[:1])], axis=0)
    for bit in bits:
        small = small + exchange(small, "wide", bit)

    block_out, grad_tokens = call(
        final_kernel,
        [shape(rows_local, block, width), shape(rows_local, block, width, dtype=F32)],
        [ints(place, lengths[0], lengths[1]), row_weight],
        [tokens, out_probe, *row0, *row1, dense_bias[None, :], down_bias[None, :]],
        1e7,
        "final",
    )
    up_grad = gather_back(up_chunk, "wide", bits).astype(F32)
    down_grad = gather_back(down_chunk, "wide", down_order).astype(F32)
    last = gather_back(last_chunk, "wide", bits).astype(F32)
    share = width // narrow_count
    mine = lax.dynamic_slice_in_dim(small[0:4], place * share, share, 1)
    out_bias = lax.dynamic_slice_in_dim(small[6], place * share, share, 0)
    q_bias_grad = small[4].reshape(3, 256)[:, : 3 * HEAD].reshape(3, 3, HEAD).transpose(1, 0, 2).reshape(-1)
    return (
        block_out,
        grad_tokens,
        mine[0],
        mine[1],
        last[:, : 9 * HEAD],
        q_bias_grad,
        last[:, 9 * HEAD :].T,
        out_bias,
        mine[2],
        mine[3],
        up_grad,
        small[5],
        down_grad,
        out_bias,
    )


def solution(mesh):
    placed = (
        P("wide", "narrow", None),
        P("wide"),
        P("wide"),
        P(),
        P(),
        P(None, "narrow"),
        P("narrow"),
        P("narrow", None),
        P(),
        P(),
        P(),
        P(None, "narrow"),
        P("narrow"),
        P("narrow", None),
        P(),
        P("wide", "narrow", None),
    )
    return jax.shard_map(
        shards,
        mesh=mesh,
        in_specs=placed,
        out_specs=(
            P("wide", "narrow", None),
            P("wide", "narrow", None),
            P("narrow"),
            P("narrow"),
            P(None, "narrow"),
            P("narrow"),
            P("narrow", None),
            P("narrow"),
            P("narrow"),
            P("narrow"),
            P(None, "narrow"),
            P("narrow"),
            P("narrow", None),
            P("narrow"),
        ),
        check_vma=False,
    )
```

```python
import functools
import math

import jax
import jax.numpy as jnp
import numpy as np
from jax import lax
from jax.experimental import pallas as pl
from jax.experimental.pallas import tpu as pltpu
from jax.sharding import PartitionSpec as P

HEAD = 64
ROT = 16
TISSUES = 8
LANES = 128
EPS = 1e-05
BIG = -1e30
F32 = jnp.float32
BF16 = jnp.bfloat16
ERF_P = 0.39
ERF_C = (
    0.2353254092560988,
    0.09138720671028266,
    0.6495624403330551,
    -0.6354040754153405,
    0.8866667192133076,
    -0.22753770177595345,
)

NN = (((1,), (0,)), ((), ()))
NT = (((1,), (1,)), ((), ()))
TN = (((0,), (0,)), ((), ()))


def mm(a, b, dims=NN):
    return lax.dot_general(a, b, dims, preferred_element_type=F32)


def norm_parts(tokens):
    values = tokens.astype(F32)
    centered = values - jnp.mean(values, axis=-1, keepdims=True)
    inverse = lax.rsqrt(jnp.mean(centered * centered, axis=-1, keepdims=True) + EPS)
    return centered * inverse, inverse


def gelu_pair(x):
    size = jnp.abs(x)
    t = 1.0 / (1.0 + (ERF_P * math.sqrt(0.5)) * size)
    bell = jnp.exp(-0.5 * (x * x))
    poly = jnp.full_like(x, 0.5 * ERF_C[-1])
    for c in ERF_C[-2::-1]:
        poly = poly * t + 0.5 * c
    tail = poly * t * bell
    phi = jnp.where(x < 0, tail, 1.0 - tail)
    return x * phi, phi + x * (bell * (1.0 / math.sqrt(2.0 * math.pi)))


def turn(x, cos_t, low_t, high_t, sign):
    up = pltpu.roll(x, LANES - ROT // 2, 1)
    down = pltpu.roll(x, ROT // 2, 1)
    return x * cos_t + sign * (up * low_t + down * high_t)


def place_two(c, first, second):
    a = jnp.where(c == 0, first, second)
    b = jnp.where(c == 0, second, first)
    return jnp.concatenate([a, b], axis=0)


def out_grad_of(probe, first_slot, length, weight):
    slot = first_slot + lax.broadcasted_iota(jnp.int32, (probe.shape[0], 1), 0)
    scale = jnp.where(slot < length, weight, 0.0)
    return (probe.astype(F32) * scale).astype(BF16)


def spot():
    place = lax.axis_index("narrow")
    return place % 2, place // 2


def wide_bits(phased):
    if not phased:
        return 0, 0, 0
    place = lax.axis_index("wide")
    return place % 2, (place // 2) % 2, place // 4


def put(bit, half, keep, send, value, *where):
    if isinstance(bit, int):
        (keep if bit == half else send)[where] = value
        return

    @pl.when(bit == half)
    def _():
        keep[where] = value

    @pl.when(bit != half)
    def _():
        send[where] = value


def high_low(values):
    high = values.astype(BF16)
    return jnp.concatenate([high, (values - high.astype(F32)).astype(BF16)], axis=0)


def back_together(pair):
    pair = pair.astype(F32)
    return pair[:8] + pair[8:]


def pack_kernel(row, tokens, probe, *rest):
    out = rest[-1]
    out[0] = tokens[row]
    out[1] = probe[row]


def prepare_kernel(weight, g1, b1, g2, b2, up_b, q_b, dense_b, down_b, weight_o, vectors_o):
    width = weight.shape[1]
    bias = q_b[...].reshape(1, q_b.shape[0])
    pieces = []
    for part in range(3):
        for h in range(3):
            at = (h * 3 + part) * HEAD
            weight_o[part * 256 + h * HEAD : part * 256 + h * HEAD + HEAD, :] = weight[at : at + HEAD, :]
            pieces.append(bias[:, at : at + HEAD])
        weight_o[part * 256 + 3 * HEAD : part * 256 + 256, :] = jnp.zeros((HEAD, width), BF16)
        pieces.append(jnp.zeros((1, HEAD), F32))
    for line, v in enumerate((g1, b1, g2, b2, up_b, None, dense_b, down_b)):
        vectors_o[line : line + 1] = jnp.concatenate(pieces, axis=1) if v is None else v[...].reshape(1, v.shape[0])


def qkv_kernel(far, x0, x1, weight, vectors, cos_t, low_t, high_t, *rest):
    out = rest[-1]
    c, y = spot()
    half = 1 - y if far else y
    gain, shift, bias = vectors[0:1], vectors[1:2], vectors[5:6]
    tokens = place_two(c, x0[0], x1[0])
    rows = tokens.shape[0]
    xhat, _ = norm_parts(tokens)
    normed = (xhat * gain + shift).astype(BF16)
    spots = pl.ds(pl.multiple_of(half * rows, rows), rows)
    cos_b, low_b, high_b = cos_t[spots, :], low_t[spots, :], high_t[spots, :]
    for part in range(3):
        joined = mm(normed, weight[part * 256 : part * 256 + 256, :], NT)
        joined = joined + bias[:, part * 256 : part * 256 + 256]
        for pair in range(2):
            x = joined[:, pair * LANES : pair * LANES + LANES]
            if part < 2:
                x = turn(x, cos_b, low_b, high_b, 1.0)
            x = x.astype(BF16)
            if part == 0:
                x = x * jnp.asarray(1.0 / math.sqrt(HEAD), BF16)
            at = part * 256 + pair * LANES
            out[:, at : at + LANES] = x


def mlp_kernel(row, far, first, last, phased, lengths, weights, x0, x1, up, down, dense, vectors, *rest):
    if first:
        ug_in = dg_in = sums_in = None
    else:
        ug_in, dg_in, sums_in = rest[:3]
    if last:
        active_o, cgrad_o, u_o, u_keep, u_send, d_keep, d_send, sums_o = rest[-8:]
        bit_u, bit_d, _ = wide_bits(phased)
    else:
        active_o, cgrad_o, u_o, ug_o, dg_o, sums_o = rest[-6:]
    c, y = spot()
    half = 1 - y if far else y
    length = lengths[row]
    gain, shift, up_b = vectors[2:3], vectors[3:4], vectors[4:5]
    tokens = place_two(c, x0[0], x1[0])
    probe = place_two(c, x0[1], x1[1])
    rows, width = tokens.shape
    grad = out_grad_of(probe, half * rows, length, weights[row])
    inner = up.shape[1]
    step = 256
    agrads = [mm(grad, down[0:step, :], NT)]
    xhat, _ = norm_parts(tokens)
    normed = (xhat * gain + shift).astype(BF16)
    hiddens = [mm(normed, up[:, 0:step])]
    cgrad_o[:, : dense.shape[0]] = mm(grad, dense[...], NT).astype(BF16)
    cgrad_o[:, dense.shape[0] :] = jnp.zeros((rows, 256 - dense.shape[0]), BF16)
    total = None
    for at in range(0, inner, step):
        cols, after = slice(at, at + step), slice(at + step, at + 2 * step)
        if at + step < inner:
            hiddens.append(mm(normed, up[:, after]))
            agrads.append(mm(grad, down[after, :], NT))
        active, slope = gelu_pair(hiddens.pop(0) + up_b[:, cols])
        active = active.astype(BF16)
        active_o[:, cols] = active
        hgrad = (agrads.pop(0) * slope).astype(BF16)
        piece = mm(hgrad, up[:, cols], NT)
        total = piece if total is None else total + piece
        ug = mm(normed, hgrad, TN)
        dg = mm(active, grad, TN)
        us = jnp.sum(hgrad.astype(F32), axis=0, keepdims=True)
        if not first:
            ug = ug + ug_in[:, cols]
            dg = dg + dg_in[cols, :]
            us = us + sums_in[2:3, cols]
        if last:
            ug, dg = ug.astype(BF16), dg.astype(BF16)
            half = width // 2
            for h in range(2):
                put(bit_u, h, u_keep, u_send, ug[h * half : h * half + half], slice(None), cols)
            for top in range(at, at + step, 128):
                h, to = top // (inner // 2), top % (inner // 2)
                put(bit_d, h, d_keep, d_send, dg[top - at : top - at + 128], slice(to, to + 128))
        else:
            ug_o[:, cols] = ug
            dg_o[cols, :] = dg
        sums_o[2:3, cols] = us
    u_o[...] = (total * gain).astype(u_o.dtype)
    gs = jnp.sum(total * xhat, axis=0, keepdims=True)
    ss = jnp.sum(total, axis=0, keepdims=True)
    os = jnp.sum(grad.astype(F32), axis=0, keepdims=True)
    if not first:
        gs, ss, os = gs + sums_in[0:1], ss + sums_in[1:2], os + sums_in[3:4]
    sums_o[0:1] = gs
    sums_o[1:2] = ss
    sums_o[3:4] = os


def attend_kernel(row, lengths, near, far, cg_near, cg_far, cos_t, low_t, high_t, *rest):
    ctx_o, jg_o, q_s, k_s, v_s, c_s, kt_s, vt_s, ct_s, dk_s, dv_s = rest[-11:]
    _, y = spot()
    length = lengths[row]
    half = near.shape[0]
    slots = 2 * half
    block = 256
    for source, cg, place in ((near, cg_near, y), (far, cg_far, 1 - y)):
        spots = pl.ds(pl.multiple_of(place * half, half), half)
        q_s[spots, :] = source[:, 0:256]
        k_s[spots, :] = source[:, 256:512]
        v_s[spots, :] = source[:, 512:768]
        c_s[spots, :] = cg[...]
    kt_s[...] = k_s[...].T
    vt_s[...] = v_s[...].T
    ct_s[...] = c_s[...].T
    heads, blocks = 3, slots // block
    least = slots * 5 // 8
    lane = lax.broadcasted_iota(jnp.int32, (block, LANES), 1)
    key = lax.broadcasted_iota(jnp.int32, (block, block), 0)
    below = key <= lax.broadcasted_iota(jnp.int32, (block, block), 1)

    def part(j):
        return slice(j * block, j * block + block)

    def places(h):
        pair = (h // 2) * LANES
        return slice(pair, pair + LANES), slice(h * HEAD, h * HEAD + HEAD)

    def products(i, h):
        lanes, _ = places(h)
        q, cg = q_s[part(i), lanes], c_s[part(i), lanes]
        if h < 2:
            mine = (lane < HEAD) if h == 0 else (lane >= HEAD)
            q = jnp.where(mine, q, jnp.zeros_like(q))
            cg = jnp.where(mine, cg, jnp.zeros_like(cg))
        scores = [mm(k_s[part(j), lanes], q, NT) for j in range(i + 1)]
        pgrad = [mm(v_s[part(j), lanes], cg, NT) for j in range(i + 1)]
        return q, cg, scores, pgrad

    def softmax(i, scores):
        for j in range(i + 1):
            allowed = below if j == i else None
            if (j + 1) * block > least:
                inside = key < length - j * block
                allowed = inside if allowed is None else allowed & inside
            if allowed is not None:
                scores[j] = jnp.where(allowed, scores[j], BIG)
        peak = jnp.max(functools.reduce(jnp.maximum, scores), axis=0, keepdims=True)
        raised = [jnp.exp(x - peak) for x in scores]
        scale = 1.0 / jnp.sum(functools.reduce(jnp.add, raised), axis=0, keepdims=True)
        probs = [x * scale for x in raised]
        return probs, [x.astype(BF16) for x in probs]

    def middle(i, h, probs, low, pgrad):
        _, lines = places(h)
        ctx = functools.reduce(jnp.add, [mm(vt_s[lines, part(j)], low[j]) for j in range(i + 1)])
        inner = jnp.sum(ct_s[lines, part(i)].astype(F32) * ctx, axis=0, keepdims=True)
        return ctx, [(p * (g - inner)).astype(BF16) for p, g in zip(probs, pgrad)]

    def gradients(i, h, q, cg, low, sgrad):
        lanes, lines = places(h)
        dq = functools.reduce(jnp.add, [mm(kt_s[lines, part(j)], sgrad[j]) for j in range(i + 1)])
        for j in range(i + 1):
            dk, dv = mm(sgrad[j], q), mm(low[j], cg)
            if i == blocks - 1 and h != 1:
                dk_s[part(j), lanes] = dk
                dv_s[part(j), lanes] = dv
            else:
                dk_s[part(j), lanes] += dk
                dv_s[part(j), lanes] += dv
        return dq

    def finish(i, pieces):
        rows = part(i)
        empty = jnp.zeros((256 - heads * HEAD, block), F32)
        ctx_o[rows, :] = jnp.concatenate([p[0] for p in pieces] + [empty], axis=0).T.astype(BF16)
        dq = jnp.concatenate([p[1] for p in pieces] + [empty], axis=0).T * (1.0 / math.sqrt(HEAD))
        for pair in range(2):
            lanes = slice(pair * LANES, pair * LANES + LANES)
            turned = turn(dq[:, lanes], cos_t[rows, :], low_t[rows, :], high_t[rows, :], -1.0)
            jg_o[rows, lanes] = turned.astype(BF16)
            turned = turn(dk_s[rows, lanes], cos_t[rows, :], low_t[rows, :], high_t[rows, :], -1.0)
            jg_o[rows, 256 + pair * LANES : 256 + pair * LANES + LANES] = turned.astype(BF16)
        jg_o[rows, 512:768] = dv_s[rows, :].astype(BF16)

    tasks = [(i, h) for i in range(blocks - 1, -1, -1) for h in range(heads)]
    pieces, waiting = [], None
    ahead = products(*tasks[0])
    for number in range(len(tasks) + 1):
        if number < len(tasks):
            i, h = tasks[number]
            q, cg, scores, pgrad = ahead
            if number + 1 < len(tasks):
                ahead = products(*tasks[number + 1])
            probs, low = softmax(i, scores)
        if waiting is not None:
            old_i, old_h, ctx, *rest = waiting
            pieces.append((ctx, gradients(old_i, old_h, *rest)))
            if old_h == heads - 1:
                finish(old_i, pieces)
                pieces = []
        if number < len(tasks):
            ctx, sgrad = middle(i, h, probs, low, pgrad)
            waiting = i, h, ctx, q, cg, low, sgrad


def close_kernel(row, first, phased, lengths, weights, x0, x1, x2, x3, ctx, jg, act_n, act_f, u_n, u_f, weight, dense,
                 down, vectors, *rest):
    if first:
        qg_in = sg_in = mg_in = None
        send, keep, qg_o, sums_o = rest[-4:]
    else:
        qg_in, sg_in, mg_in = rest[:3]
        send, keep, a_keep, a_send, b_keep, b_send, sums_o = rest[-7:]
    c, y = spot()
    length = lengths[row]
    gain, shift = vectors[0:1], vectors[1:2]
    block = x0.shape[1]
    gs = ss = bs = qg = dg = None
    for x, act, u, side, slot, out, at in (
        (x2, act_f, u_f, 1 - y, c, keep, 0),
        (x3, act_f, u_f, 1 - y, 1 - c, send, 0),
        (x0, act_n, u_n, y, c, keep, 2),
        (x1, act_n, u_n, y, 1 - c, send, 2),
    ):
        place = 2 * side + slot
        whole = pl.ds(pl.multiple_of(place * block, block), block)
        part = pl.ds(pl.multiple_of(slot * block, block), block)
        context, joined = ctx[whole, :], jg[whole, :]
        out[at] = (mm(context[:, : dense.shape[0]], dense[...]) + mm(act[part, :], down[...])).astype(BF16)
        first_grad = mm(joined, weight[...])
        xhat, _ = norm_parts(x[0])
        normed = (xhat * gain + shift).astype(BF16)
        grad = out_grad_of(x[1], place * block, length, weights[row])
        out[at + 1] = (first_grad * gain + u[part, :].astype(F32)).astype(BF16)
        pieces = (
            jnp.sum(first_grad * xhat, axis=0, keepdims=True),
            jnp.sum(first_grad, axis=0, keepdims=True),
            jnp.sum(joined.astype(F32), axis=0, keepdims=True),
            mm(joined, normed, TN),
            mm(context, grad, TN),
        )
        if gs is None:
            gs, ss, bs, qg, dg = pieces
        else:
            gs, ss, bs, qg, dg = (a + b for a, b in zip((gs, ss, bs, qg, dg), pieces))
    if first:
        qg_o[0:768] = qg
        qg_o[768:1024] = dg
        sums_o[0:1] = gs
        sums_o[1:2] = ss
        sums_o[2:3] = bs
        return
    bit_a, bit_b, _ = wide_bits(phased)
    half = a_keep.shape[0]
    for h in range(3):
        for part in range(3):
            at, to = part * 256 + h * HEAD, (h * 3 + part) * HEAD
            value = (qg[at : at + HEAD] + qg_in[at : at + HEAD]).astype(BF16)
            number, to = to // half, to % half
            if number < 2:
                put(bit_a, number, a_keep, a_send, value, slice(to, to + HEAD))
            else:
                put(bit_b, 0, b_keep, b_send, value, slice(to, to + HEAD))
    value = (dg[0:half] + qg_in[768 : 768 + half]).astype(BF16)
    put(bit_b, 1, b_keep, b_send, value, slice(None))
    small = jnp.concatenate(
        [
            gs + sg_in[0:1],
            ss + sg_in[1:2],
            mg_in[0:2],
            bs + sg_in[2:3],
            mg_in[2:4],
            jnp.zeros_like(gs),
        ],
        axis=0,
    )
    sums_o[...] = small
    a_send[half : half + 16] = high_low(small)


def plus(a, b):
    return (a.astype(F32) + b.astype(F32)).astype(BF16)


def rows_of(number, size):
    return pl.ds(pl.multiple_of(number * size, size), size)


def join_1(u_keep, u_got, d_keep, d_got, *rest):
    u_keep_o, u_send_o, d_keep_o, d_send_o = rest[-4:]
    x, z, _ = wide_bits(True)
    size = u_keep_o.shape[0]
    for keep, got, bit, keep_o, send_o in ((u_keep, u_got, z, u_keep_o, u_send_o), (d_keep, d_got, x, d_keep_o, d_send_o)):
        mine, other = rows_of(bit, size), rows_of(1 - bit, size)
        send_o[...] = plus(keep[other, :], got[other, :])
        keep_o[...] = plus(keep[mine, :], got[mine, :])


def join_2(u_keep, u_got, d_keep, d_got, *rest):
    both = rest[-1]
    both[0] = plus(u_keep[...], u_got[...])
    both[1] = plus(d_keep[...], d_got[...])


def join_far(keep0, got0, keep1, got1, *rest):
    out = rest[-1]
    out[0:2] = plus(keep0[0:2], got0[0:2])
    out[2:4] = plus(keep1[0:2], got1[0:2])


def join_3(both, both_got, a_keep, a_got, b_keep, b_got, small, *rest):
    over_z, over_x, a_o, b_o, small_o = rest[-5:]
    x, z, _ = wide_bits(True)
    size, part = both.shape[1], a_o.shape[0]
    over_z[0:size] = plus(both[0], both_got[0])
    over_x[0:size] = plus(both[1], both_got[1])
    for keep, got, bit, out, out_o in ((a_keep, a_got, z, over_z, a_o), (b_keep, b_got, x, over_x, b_o)):
        mine, other = rows_of(bit, part), rows_of(1 - bit, part)
        out[size : size + part] = plus(keep[other, :], got[other, :])
        out_o[...] = plus(keep[mine, :], got[mine, :])
    total = small[...] + back_together(a_got[2 * part : 2 * part + 16])
    small_o[...] = total
    over_z[size + part : size + part + 16] = high_low(total)


def join_4(over_z, z_got, over_x, x_got, a_keep, b_keep, small, *rest):
    u_o, d_o, last_o, small_o = rest[-4:]
    x, z, _ = wide_bits(True)
    size, part = u_o.shape[0] // 2, a_keep.shape[0]
    for own, got, bit, out in ((over_z, z_got, z, u_o), (over_x, x_got, x, d_o)):
        out[rows_of(bit, size), :] = own[0:size]
        out[rows_of(1 - bit, size), :] = got[0:size]
    last_o[0:part] = plus(a_keep[...], z_got[size : size + part])
    last_o[part : 2 * part] = plus(b_keep[...], x_got[size : size + part])
    total = small[...] + back_together(z_got[size + part : size + part + 16])
    small_o[...] = total
    last_o[2 * part : 2 * part + 16] = high_low(total)


def join_5(last, last_got, small, *rest):
    a_o, b_o, small_o = rest[-3:]
    part = a_o.shape[0]
    a_o[...] = plus(last[0:part], last_got[0:part])
    b_o[...] = plus(last[part : 2 * part], last_got[part : 2 * part])
    small_o[...] = small[...] + back_together(last_got[2 * part : 2 * part + 16])


def join_6(a, a_got, b, b_got, *rest):
    a_o, b_o = rest[-2:]
    x, z, _ = wide_bits(True)
    part = a.shape[0]
    for own, got, bit, out in ((a, a_got, z, a_o), (b, b_got, x, b_o)):
        out[rows_of(bit, part), :] = own[...]
        out[rows_of(1 - bit, part), :] = got[...]


def widen_kernel(u, u_got, d, d_got, *rest):
    u_o, d_o = rest[-2:]
    x, z, _ = wide_bits(True)
    half = u.shape[0]
    for own, got, bit, out in ((u, u_got, x, u_o), (d, d_got, z, d_o)):
        out[rows_of(bit, half), :] = own[...].astype(F32)
        out[rows_of(1 - bit, half), :] = got[...].astype(F32)


def last_kernel(a, a_got, b, b_got, *rest):
    q_o, dense_o = rest[-2:]
    x, z, _ = wide_bits(True)
    half = a.shape[0]
    q_o[rows_of(x, half), :] = a[...].astype(F32)
    q_o[rows_of(1 - x, half), :] = a_got[...].astype(F32)
    mine, other = b[...].astype(F32), b_got[...].astype(F32)
    q_o[2 * half : 3 * half] = jnp.where(z == 0, mine, other)
    dense_o[...] = jnp.where(z == 0, other, mine)


def final_kernel(row, lengths, weights, own, keep, got, far, vectors, *rest):
    block_o, grad_o = rest[-2:]
    block = own.shape[1]
    near = keep[2:4].astype(F32) + got[2:4].astype(F32) + far[2 * row : 2 * row + 2].astype(F32)
    values = own[0].astype(F32)
    block_o[0] = (values + (near[0] + vectors[6:7] + vectors[7:8])).astype(BF16)
    xhat, inverse = norm_parts(own[0])
    u = near[1]
    slot = lax.axis_index("narrow") * block + lax.broadcasted_iota(jnp.int32, (block, 1), 0)
    scale = jnp.where(slot < lengths[row], weights[row], 0.0)
    mean = jnp.mean(u, axis=-1, keepdims=True)
    lean = jnp.mean(u * xhat, axis=-1, keepdims=True)
    grad_o[0] = own[1].astype(F32) * scale + inverse * (u - mean - xhat * lean)


SMEM = functools.partial(pl.BlockSpec, memory_space=pltpu.SMEM)
VMEM = functools.partial(pl.BlockSpec, memory_space=pltpu.VMEM)
ANY = functools.partial(pl.BlockSpec, memory_space=pl.ANY)
COST = 1e8


def call(body, outs, scalars, arrays, name, us, scratch=(), limit=8, after=()):
    return pl.pallas_call(
        body,
        out_shape=outs,
        in_specs=[SMEM()] * len(scalars) + [VMEM()] * len(arrays) + [ANY()] * len(after),
        out_specs=[VMEM()] * len(outs),
        scratch_shapes=list(scratch),
        compiler_params=pltpu.CompilerParams(vmem_limit_bytes=limit * 1024 * 1024),
        cost_estimate=pl.CostEstimate(flops=int(us * COST), bytes_accessed=0, transcendentals=0),
        name=name,
    )(*scalars, *arrays, *after)


def exchange(x, axis, bit):
    size = lax.axis_size(axis)
    return lax.ppermute(x, axis, [(i, i ^ (1 << bit)) for i in range(size)])


def add_low(a, b):
    return (a.astype(F32) + b.astype(F32)).astype(BF16)


def scatter_sum(x, axis, bits):
    place = lax.axis_index(axis)
    for bit in bits:
        half = x.shape[0] // 2
        mine = (place >> bit) & 1
        keep = lax.dynamic_slice_in_dim(x, mine * half, half, 0)
        send = lax.dynamic_slice_in_dim(x, (1 - mine) * half, half, 0)
        x = add_low(keep, exchange(send, axis, bit))
    return x


def gather_back(x, axis, bits):
    place = lax.axis_index(axis)
    for bit in reversed(bits):
        mine = (place >> bit) & 1
        got = exchange(x, axis, bit)
        x = jnp.where(mine == 0, jnp.concatenate([x, got]), jnp.concatenate([got, x]))
    return x


def rotary(slot_count):
    position = np.arange(slot_count, dtype=np.float64)
    frequency = 10000.0 ** (-(2.0 * np.arange(ROT // 2)) / ROT)
    angles = position[:, None] * frequency[None, :]
    cos, sin = np.cos(angles), np.sin(angles)
    none8, none = np.zeros_like(sin), np.zeros((slot_count, HEAD - ROT))
    cos_t = np.concatenate([cos, cos, none + 1.0], axis=1)
    low_t = np.concatenate([-sin, none8, none], axis=1)
    high_t = np.concatenate([none8, sin, none], axis=1)
    return tuple(jnp.asarray(np.concatenate([t, t], axis=1), F32) for t in (cos_t, low_t, high_t))


def shards(tokens, lengths, tissues, ln1_gain, ln1_bias, qkv_weight, qkv_bias, dense_weight, dense_bias,
           ln2_gain, ln2_bias, up_weight, up_bias, down_weight, down_bias, out_probe):
    rows_local, block, width = tokens.shape
    inner = up_weight.shape[1]
    wide_count, narrow_count = lax.axis_size("wide"), lax.axis_size("narrow")
    place = lax.axis_index("narrow")
    slot_count = block * narrow_count
    bits = list(range(wide_count.bit_length() - 1))
    half_rows = 2 * block
    phased = wide_count == 8

    def shape(*dims, dtype=BF16):
        return jax.ShapeDtypeStruct(dims, dtype)

    def pack(r, after=()):
        return call(
            functools.partial(pack_kernel, r), [shape(2, block, width)], [], [tokens, out_probe], "pack", 1, after=after
        )[0]

    def gate(x, after):
        return pl.pallas_call(
            lambda *refs: None,
            out_shape=jax.ShapeDtypeStruct(x.shape, x.dtype),
            in_specs=[ANY()] * (1 + len(after)),
            out_specs=ANY(),
            input_output_aliases={0: 0},
            compiler_params=pltpu.CompilerParams(vmem_limit_bytes=1024 * 1024),
            name="gate",
        )(x, *after)

    own = [pack(0)]
    own.append(pack(1, own))
    over = [exchange(own[0], "narrow", 1)]
    mate = [exchange(x, "narrow", 0) for x in own]
    cross = [None, None]

    tables = rotary(slot_count)
    weight, vectors = call(
        prepare_kernel,
        [shape(768, width), shape(8, width, dtype=F32)],
        [],
        [qkv_weight.T, ln1_gain, ln1_bias, ln2_gain, ln2_bias, up_bias, qkv_bias, dense_bias, down_bias],
        "prepare",
        1,
    )

    def qkv(r, far, after=()):
        x0, x1 = (over[r], cross[r]) if far else (own[r], mate[r])
        return call(
            functools.partial(qkv_kernel, far),
            [shape(half_rows, 768)],
            [],
            [x0, x1, weight, vectors, *tables],
            "qkv",
            3,
            limit=8,
            after=after,
        )[0]

    def mlp(r, far, sums, last, after=()):
        x0, x1 = (over[r], cross[r]) if far else (own[r], mate[r])
        first = sums is None
        return call(
            functools.partial(mlp_kernel, r, far, first, last, phased),
            [
                shape(half_rows, inner),
                shape(half_rows, 256),
                shape(half_rows, width),
                *([shape(width // 2, inner)] * 2 if last else [shape(width, inner, dtype=F32)]),
                *([shape(inner // 2, width)] * 2 if last else [shape(inner, width, dtype=F32)]),
                shape(4, width, dtype=F32),
            ],
            [lengths, row_weight],
            [x0, x1, up_weight, down_weight, dense_weight, vectors, *(sums or [])],
            "mlp",
            7,
            limit=12,
            after=after,
        )

    def attend(r, near, far, cg_near, cg_far, after=()):
        big = pltpu.VMEM((slot_count, 256), BF16)
        tall = pltpu.VMEM((256, slot_count), BF16)
        total = pltpu.VMEM((slot_count, 256), F32)
        return call(
            functools.partial(attend_kernel, r),
            [shape(slot_count, 256), shape(slot_count, 768)],
            [lengths],
            [near, far, cg_near, cg_far, *tables],
            "attend",
            14,
            scratch=[big] * 4 + [tall] * 3 + [total] * 2,
            limit=12,
            after=after,
        )

    def close(r, ctx, jg, acts, us, sums, after=()):
        first = sums is None
        four = shape(4, block, width)
        half = 3 * HEAD
        if first:
            shapes = [four, four, shape(1024, width, dtype=F32), shape(3, width, dtype=F32)]
        else:
            shapes = [four, four, shape(half, width), shape(half + 16, width), shape(half, width), shape(half, width)]
            shapes.append(shape(8, width, dtype=F32))
        return call(
            functools.partial(close_kernel, r, first, phased),
            shapes,
            [lengths, row_weight],
            [own[r], mate[r], over[r], cross[r], ctx, jg, *acts, *us, weight, dense_weight, down_weight, vectors, *(sums or [])],
            "close",
            8.5,
            limit=12,
            after=after,
        )

    hits = (tissues[:, None] == jnp.arange(TISSUES)[None, :]).astype(F32)
    counts = jnp.sum(hits * lengths[:, None].astype(F32), axis=0)[None, :]
    counts = counts + exchange(counts, "wide", bits[0])
    near_q0 = qkv(0, False)
    counts = gate(counts, [near_q0])
    counts = counts + exchange(counts, "wide", bits[1])
    near_q1 = qkv(1, False, [counts])
    for bit in bits[2:]:
        counts = counts + exchange(counts, "wide", bit)
    row_count = jnp.sum(hits * counts, axis=1)
    row_weight = rows_local * wide_count * slot_count / TISSUES / row_count
    a00, cg00, u00, *sums = mlp(0, False, None, False, [near_q1])
    over[0] = gate(over[0], [sums[2]])
    over.append(exchange(gate(own[1], [over[0]]), "narrow", 1))
    cross[0] = exchange(over[0], "narrow", 0)
    a10, cg10, u10, *sums = mlp(1, False, sums, False, [over[0]])
    a01, cg01, u01, *sums = mlp(0, True, sums, False)
    far_q0 = qkv(0, True, [sums[2]])
    ctx0, jg0 = attend(0, near_q0, far_q0, cg00, cg01)
    over[1] = gate(over[1], [ctx0])
    cross[1] = exchange(over[1], "narrow", 0)
    a11, cg11, u11, u_keep, u_send, d_keep, d_send, mlp_sums = mlp(1, True, sums, True)

    def final(r, keep, got, far, before, after=()):
        spec = pl.BlockSpec((1, block, width), lambda i: (r, 0, 0))
        whole = shape(rows_local, block, width), shape(rows_local, block, width, dtype=F32)
        return pl.pallas_call(
            functools.partial(final_kernel, r),
            grid=(1,),
            out_shape=whole,
            in_specs=[SMEM()] * 2 + [VMEM()] * 5 + [ANY()] * (len(before) + len(after)),
            out_specs=[spec, spec],
            input_output_aliases={7: 0, 8: 1} if before else {},
            compiler_params=pltpu.CompilerParams(vmem_limit_bytes=8 * 1024 * 1024),
            cost_estimate=pl.CostEstimate(flops=int(2.5 * COST), bytes_accessed=0, transcendentals=0),
            name="final",
        )(lengths, row_weight, own[r], keep, got, far, vectors, *before, *after)

    def join(body, shapes, arrays, after=()):
        return call(body, shapes, [], arrays, body.__name__, 1, after=after)

    far_q1 = qkv(1, True, [mlp_sums])
    ctx1, jg1 = attend(1, near_q1, far_q1, cg10, cg11)
    quarter = width // 4
    if phased:
        u_keep, u_send, d_keep, d_send = join(
            join_1,
            [shape(quarter, width)] * 4,
            [u_keep, exchange(u_send, "wide", 0), d_keep, exchange(d_send, "wide", 1)],
            [ctx1],
        )
    send0, keep0, qg, close_sums = close(0, ctx0, jg0, (a00, a01), (u00, u01), None, [ctx1, u_keep])
    got0 = exchange(send0, "narrow", 0)
    if phased:
        (both,) = join(
            join_2,
            [shape(2, quarter, width)],
            [u_keep, exchange(u_send, "wide", 1), d_keep, exchange(d_send, "wide", 0)],
            [close_sums],
        )
        both_got = exchange(both, "wide", 2)
    send1, keep1, a_keep, a_send, b_keep, b_send, small = close(
        1, ctx1, jg1, (a10, a11), (u10, u11), [qg, close_sums, mlp_sums], [both] if phased else []
    )
    got1 = exchange(send1, "narrow", 0)
    if phased:
        a_got, b_got = exchange(a_send, "wide", 0), exchange(b_send, "wide", 1)
    if phased:
        part = quarter // 2
        over_z, over_x, a_keep, b_keep, small = join(
            join_3,
            [
                shape(quarter + part + 16, width),
                shape(quarter + part, width),
                shape(part, width),
                shape(part, width),
                shape(8, width, dtype=F32),
            ],
            [both, both_got, a_keep, a_got, b_keep, b_got, small],
        )
        far = join(join_far, [shape(4, block, width)], [keep0, got0, keep1, got1], [over_z])[0]
        far_got = exchange(far, "narrow", 1)
        u_half, d_half, last_part, small = join(
            join_4,
            [shape(2 * quarter, width), shape(2 * quarter, width), shape(quarter + 16, width), shape(8, width, dtype=F32)],
            [over_z, exchange(over_z, "wide", 1), over_x, exchange(over_x, "wide", 0), a_keep, b_keep, small],
        )
        u_got, d_got = exchange(u_half, "wide", 0), exchange(d_half, "wide", 1)
        last_got = exchange(last_part, "wide", 2)
        outs = final(0, keep0, got0, far_got, [], [u_half])
        a_part, b_part, small = join(
            join_5,
            [shape(part, width), shape(part, width), shape(8, width, dtype=F32)],
            [last_part, last_got, small],
            [outs[0]],
        )
        a_got, b_got = exchange(a_part, "wide", 1), exchange(b_part, "wide", 0)
        up_grad, down_grad = join(
            widen_kernel,
            [shape(width, inner, dtype=F32), shape(inner, width, dtype=F32)],
            [u_half, u_got, d_half, d_got],
            [a_part],
        )
        a_half, b_half = join(join_6, [shape(quarter, width)] * 2, [a_part, a_got, b_part, b_got], [up_grad])
        a_got, b_got = exchange(a_half, "wide", 0), exchange(b_half, "wide", 1)
        block_out, grad_tokens = final(1, keep1, got1, far_got, outs, [a_half])
        q_grad, dense_grad = join(
            last_kernel,
            [shape(9 * HEAD, width, dtype=F32), shape(3 * HEAD, width, dtype=F32)],
            [a_half, a_got, b_half, b_got],
            [block_out],
        )
    else:
        far = join(join_far, [shape(4, block, width)], [keep0, got0, keep1, got1])[0]
        far_got = exchange(far, "narrow", 1)
        outs = final(0, keep0, got0, far_got, [])
        block_out, grad_tokens = final(1, keep1, got1, far_got, outs)

        def total(keep, send):
            return gather_back(scatter_sum(jnp.concatenate([keep, send]), "wide", bits), "wide", bits).astype(F32)

        up_grad, down_grad = total(u_keep, u_send), total(d_keep, d_send)
        a, b = total(a_keep, a_send[:quarter]), total(b_keep, b_send)
        q_grad, dense_grad = jnp.concatenate([a, b[:quarter]]), b[quarter:]
        for bit in bits:
            small = small + exchange(small, "wide", bit)

    norms = small[0:4]
    for bit in range(2):
        norms = norms + exchange(norms, "narrow", bit)
    share = width // narrow_count
    mine = lax.dynamic_slice_in_dim(norms, place * share, share, 1)
    out_bias = lax.dynamic_slice_in_dim(small[6], place * share, share, 0)
    q_bias_grad = small[4].reshape(3, 256)[:, : 3 * HEAD].reshape(3, 3, HEAD).transpose(1, 0, 2).reshape(-1)
    return (
        block_out,
        grad_tokens,
        mine[0],
        mine[1],
        q_grad.T,
        q_bias_grad,
        dense_grad,
        out_bias,
        mine[2],
        mine[3],
        up_grad,
        small[5],
        down_grad,
        out_bias,
    )


def solution(mesh):
    placed = (
        P("wide", "narrow", None),
        P("wide"),
        P("wide"),
        P(),
        P(),
        P(None, "narrow"),
        P("narrow"),
        P("narrow", None),
        P(),
        P(),
        P(),
        P(None, "narrow"),
        P("narrow"),
        P("narrow", None),
        P(),
        P("wide", "narrow", None),
    )
    return jax.shard_map(
        shards,
        mesh=mesh,
        in_specs=placed,
        out_specs=(
            P("wide", "narrow", None),
            P("wide", "narrow", None),
            P("narrow"),
            P("narrow"),
            P(None, "narrow"),
            P("narrow"),
            P("narrow", None),
            P("narrow"),
            P("narrow"),
            P("narrow"),
            P(None, "narrow"),
            P("narrow"),
            P("narrow", None),
            P("narrow"),
        ),
        check_vma=False,
    )
```

```python
import functools
import math

import jax
import jax.numpy as jnp
import numpy as np
from jax import lax
from jax.experimental import pallas as pl
from jax.experimental.pallas import tpu as pltpu
from jax.sharding import PartitionSpec as P

HEAD = 64
ROT = 16
TISSUES = 8
LANES = 128
EPS = 1e-05
BIG = -1e30
F32 = jnp.float32
BF16 = jnp.bfloat16
ERF_P = 0.39
ERF_C = (
    0.2353254092560988,
    0.09138720671028266,
    0.6495624403330551,
    -0.6354040754153405,
    0.8866667192133076,
    -0.22753770177595345,
)

NN = (((1,), (0,)), ((), ()))
NT = (((1,), (1,)), ((), ()))
TN = (((0,), (0,)), ((), ()))


def mm(a, b, dims=NN):
    return lax.dot_general(a, b, dims, preferred_element_type=F32)


def norm_parts(tokens):
    values = tokens.astype(F32)
    centered = values - jnp.mean(values, axis=-1, keepdims=True)
    inverse = lax.rsqrt(jnp.mean(centered * centered, axis=-1, keepdims=True) + EPS)
    return centered * inverse, inverse


def gelu_pair(x):
    size = jnp.abs(x)
    t = 1.0 / (1.0 + (ERF_P * math.sqrt(0.5)) * size)
    bell = jnp.exp(-0.5 * (x * x))
    poly = jnp.full_like(x, 0.5 * ERF_C[-1])
    for c in ERF_C[-2::-1]:
        poly = poly * t + 0.5 * c
    tail = poly * t * bell
    phi = jnp.where(x < 0, tail, 1.0 - tail)
    return x * phi, phi + x * (bell * (1.0 / math.sqrt(2.0 * math.pi)))


def turn(x, cos_t, low_t, high_t, sign):
    up = pltpu.roll(x, LANES - ROT // 2, 1)
    down = pltpu.roll(x, ROT // 2, 1)
    return x * cos_t + sign * (up * low_t + down * high_t)


def place_two(c, first, second):
    a = jnp.where(c == 0, first, second)
    b = jnp.where(c == 0, second, first)
    return jnp.concatenate([a, b], axis=0)


def out_grad_of(probe, first_slot, length, weight):
    slot = first_slot + lax.broadcasted_iota(jnp.int32, (probe.shape[0], 1), 0)
    scale = jnp.where(slot < length, weight, 0.0)
    return (probe.astype(F32) * scale).astype(BF16)


def spot():
    place = lax.axis_index("narrow")
    return place % 2, place // 2


def wide_bits(phased):
    if not phased:
        return 0, 0, 0
    place = lax.axis_index("wide")
    return place % 2, (place // 2) % 2, place // 4


def put(bit, half, keep, send, value, *where):
    if isinstance(bit, int):
        (keep if bit == half else send)[where] = value
        return

    @pl.when(bit == half)
    def _():
        keep[where] = value

    @pl.when(bit != half)
    def _():
        send[where] = value


def high_low(values):
    high = values.astype(BF16)
    return jnp.concatenate([high, (values - high.astype(F32)).astype(BF16)], axis=0)


def back_together(pair):
    pair = pair.astype(F32)
    return pair[:8] + pair[8:]


def pack_kernel(row, tokens, probe, *rest):
    out, sems = rest[-2:]
    copies = [pltpu.make_async_copy(x.at[row], out.at[at], sems.at[at]) for at, x in enumerate((tokens, probe))]
    for copy in copies:
        copy.start()
    for copy in copies:
        copy.wait()


def prepare_kernel(weight, g1, b1, g2, b2, up_b, q_b, dense_b, down_b, weight_o, vectors_o):
    width = weight.shape[1]
    bias = q_b[...].reshape(1, q_b.shape[0])
    pieces = []
    for part in range(3):
        for h in range(3):
            at = (h * 3 + part) * HEAD
            weight_o[part * 256 + h * HEAD : part * 256 + h * HEAD + HEAD, :] = weight[at : at + HEAD, :]
            pieces.append(bias[:, at : at + HEAD])
        weight_o[part * 256 + 3 * HEAD : part * 256 + 256, :] = jnp.zeros((HEAD, width), BF16)
        pieces.append(jnp.zeros((1, HEAD), F32))
    for line, v in enumerate((g1, b1, g2, b2, up_b, None, dense_b, down_b)):
        vectors_o[line : line + 1] = jnp.concatenate(pieces, axis=1) if v is None else v[...].reshape(1, v.shape[0])


def pair_of(far, refs):
    return ((refs[0][...], refs[1][...]), refs[2:]) if far else ((refs[0][0], refs[0][1]), refs[1:])


def qkv_kernel(far, x0, *refs):
    x1, (weight, vectors, cos_t, low_t, high_t, *rest) = pair_of(far, refs)
    out = rest[-1]
    c, y = spot()
    half = 1 - y if far else y
    gain, shift, bias = vectors[0:1], vectors[1:2], vectors[5:6]
    tokens = place_two(c, x0[0], x1[0])
    rows = tokens.shape[0]
    xhat, _ = norm_parts(tokens)
    normed = (xhat * gain + shift).astype(BF16)
    spots = pl.ds(pl.multiple_of(half * rows, rows), rows)
    cos_b, low_b, high_b = cos_t[spots, :], low_t[spots, :], high_t[spots, :]
    for part in range(3):
        joined = mm(normed, weight[part * 256 : part * 256 + 256, :], NT)
        joined = joined + bias[:, part * 256 : part * 256 + 256]
        for pair in range(2):
            x = joined[:, pair * LANES : pair * LANES + LANES]
            if part < 2:
                x = turn(x, cos_b, low_b, high_b, 1.0)
            x = x.astype(BF16)
            if part == 0:
                x = x * jnp.asarray(1.0 / math.sqrt(HEAD), BF16)
            at = part * 256 + pair * LANES
            out[:, at : at + LANES] = x


def mlp_kernel(row, far, first, last, phased, lengths, weights, x0, *refs):
    x1, (up, down, dense, vectors, *rest) = pair_of(far, refs)
    if first:
        ug_in = dg_in = sums_in = None
    else:
        ug_in, dg_in, sums_in = rest[:3]
    if last:
        active_o, cgrad_o, u_o, u_keep, u_send, d_keep, d_send, sums_o = rest[-8:]
        bit_u, bit_d, _ = wide_bits(phased)
    else:
        active_o, cgrad_o, u_o, ug_o, dg_o, sums_o = rest[-6:]
    c, y = spot()
    half = 1 - y if far else y
    length = lengths[row]
    gain, shift, up_b = vectors[2:3], vectors[3:4], vectors[4:5]
    tokens = place_two(c, x0[0], x1[0])
    probe = place_two(c, x0[1], x1[1])
    rows, width = tokens.shape
    grad = out_grad_of(probe, half * rows, length, weights[row])
    inner = up.shape[1]
    step = 256
    agrads = [mm(grad, down[0:step, :], NT)]
    xhat, _ = norm_parts(tokens)
    normed = (xhat * gain + shift).astype(BF16)
    hiddens = [mm(normed, up[:, 0:step])]
    cgrad_o[:, : dense.shape[0]] = mm(grad, dense[...], NT).astype(BF16)
    cgrad_o[:, dense.shape[0] :] = jnp.zeros((rows, 256 - dense.shape[0]), BF16)
    total = None
    for at in range(0, inner, step):
        cols, after = slice(at, at + step), slice(at + step, at + 2 * step)
        if at + step < inner:
            hiddens.append(mm(normed, up[:, after]))
            agrads.append(mm(grad, down[after, :], NT))
        active, slope = gelu_pair(hiddens.pop(0) + up_b[:, cols])
        active = active.astype(BF16)
        active_o[:, cols] = active
        hgrad = (agrads.pop(0) * slope).astype(BF16)
        piece = mm(hgrad, up[:, cols], NT)
        total = piece if total is None else total + piece
        ug = mm(normed, hgrad, TN)
        dg = mm(active, grad, TN)
        us = jnp.sum(hgrad.astype(F32), axis=0, keepdims=True)
        if not first:
            ug = ug + ug_in[:, cols]
            dg = dg + dg_in[cols, :]
            us = us + sums_in[2:3, cols]
        if last:
            ug, dg = ug.astype(BF16), dg.astype(BF16)
            half = width // 2
            for h in range(2):
                put(bit_u, h, u_keep, u_send, ug[h * half : h * half + half], slice(None), cols)
            for top in range(at, at + step, 128):
                h, to = top // (inner // 2), top % (inner // 2)
                put(bit_d, h, d_keep, d_send, dg[top - at : top - at + 128], slice(to, to + 128))
        else:
            ug_o[:, cols] = ug
            dg_o[cols, :] = dg
        sums_o[2:3, cols] = us
    u_o[...] = (total * gain).astype(u_o.dtype)
    gs = jnp.sum(total * xhat, axis=0, keepdims=True)
    ss = jnp.sum(total, axis=0, keepdims=True)
    os = jnp.sum(grad.astype(F32), axis=0, keepdims=True)
    if not first:
        gs, ss, os = gs + sums_in[0:1], ss + sums_in[1:2], os + sums_in[3:4]
    sums_o[0:1] = gs
    sums_o[1:2] = ss
    sums_o[3:4] = os


def attend_kernel(row, lengths, near, far, cg_near, cg_far, cos_t, low_t, high_t, *rest):
    ctx_o, jg_o, q_s, k_s, v_s, c_s, kt_s, vt_s, ct_s, dk_s, dv_s = rest[-11:]
    _, y = spot()
    length = lengths[row]
    half = near.shape[0]
    slots = 2 * half
    block = 256
    for source, cg, place in ((near, cg_near, y), (far, cg_far, 1 - y)):
        spots = pl.ds(pl.multiple_of(place * half, half), half)
        q_s[spots, :] = source[:, 0:256]
        k_s[spots, :] = source[:, 256:512]
        v_s[spots, :] = source[:, 512:768]
        c_s[spots, :] = cg[...]
    kt_s[...] = k_s[...].T
    vt_s[...] = v_s[...].T
    ct_s[...] = c_s[...].T
    heads, blocks = 3, slots // block
    least = slots * 5 // 8
    lane = lax.broadcasted_iota(jnp.int32, (block, LANES), 1)
    key = lax.broadcasted_iota(jnp.int32, (block, block), 0)
    below = key <= lax.broadcasted_iota(jnp.int32, (block, block), 1)

    def part(j):
        return slice(j * block, j * block + block)

    def places(h):
        pair = (h // 2) * LANES
        return slice(pair, pair + LANES), slice(h * HEAD, h * HEAD + HEAD)

    def products(i, h):
        lanes, _ = places(h)
        q, cg = q_s[part(i), lanes], c_s[part(i), lanes]
        if h < 2:
            mine = (lane < HEAD) if h == 0 else (lane >= HEAD)
            q = jnp.where(mine, q, jnp.zeros_like(q))
            cg = jnp.where(mine, cg, jnp.zeros_like(cg))
        scores = [mm(k_s[part(j), lanes], q, NT) for j in range(i + 1)]
        pgrad = [mm(v_s[part(j), lanes], cg, NT) for j in range(i + 1)]
        return q, cg, scores, pgrad

    def softmax(i, scores):
        for j in range(i + 1):
            allowed = below if j == i else None
            if (j + 1) * block > least:
                inside = key < length - j * block
                allowed = inside if allowed is None else allowed & inside
            if allowed is not None:
                scores[j] = jnp.where(allowed, scores[j], BIG)
        peak = jnp.max(functools.reduce(jnp.maximum, scores), axis=0, keepdims=True)
        raised = [jnp.exp(x - peak) for x in scores]
        scale = 1.0 / jnp.sum(functools.reduce(jnp.add, raised), axis=0, keepdims=True)
        probs = [x * scale for x in raised]
        return probs, [x.astype(BF16) for x in probs]

    def middle(i, h, probs, low, pgrad):
        _, lines = places(h)
        ctx = functools.reduce(jnp.add, [mm(vt_s[lines, part(j)], low[j]) for j in range(i + 1)])
        inner = jnp.sum(ct_s[lines, part(i)].astype(F32) * ctx, axis=0, keepdims=True)
        return ctx, [(p * (g - inner)).astype(BF16) for p, g in zip(probs, pgrad)]

    def gradients(i, h, q, cg, low, sgrad):
        lanes, lines = places(h)
        dq = functools.reduce(jnp.add, [mm(kt_s[lines, part(j)], sgrad[j]) for j in range(i + 1)])
        for j in range(i + 1):
            dk, dv = mm(sgrad[j], q), mm(low[j], cg)
            if i == blocks - 1 and h != 1:
                dk_s[part(j), lanes] = dk
                dv_s[part(j), lanes] = dv
            else:
                dk_s[part(j), lanes] += dk
                dv_s[part(j), lanes] += dv
        return dq

    def finish(i, pieces):
        rows = part(i)
        empty = jnp.zeros((256 - heads * HEAD, block), F32)
        ctx_o[rows, :] = jnp.concatenate([p[0] for p in pieces] + [empty], axis=0).T.astype(BF16)
        dq = jnp.concatenate([p[1] for p in pieces] + [empty], axis=0).T * (1.0 / math.sqrt(HEAD))
        for pair in range(2):
            lanes = slice(pair * LANES, pair * LANES + LANES)
            turned = turn(dq[:, lanes], cos_t[rows, :], low_t[rows, :], high_t[rows, :], -1.0)
            jg_o[rows, lanes] = turned.astype(BF16)
            turned = turn(dk_s[rows, lanes], cos_t[rows, :], low_t[rows, :], high_t[rows, :], -1.0)
            jg_o[rows, 256 + pair * LANES : 256 + pair * LANES + LANES] = turned.astype(BF16)
        jg_o[rows, 512:768] = dv_s[rows, :].astype(BF16)

    tasks = [(i, h) for i in range(blocks - 1, -1, -1) for h in range(heads)]
    pieces, waiting = [], None
    ahead = products(*tasks[0])
    for number in range(len(tasks) + 1):
        if number < len(tasks):
            i, h = tasks[number]
            q, cg, scores, pgrad = ahead
            if number + 1 < len(tasks):
                ahead = products(*tasks[number + 1])
            probs, low = softmax(i, scores)
        if waiting is not None:
            old_i, old_h, ctx, *rest = waiting
            pieces.append((ctx, gradients(old_i, old_h, *rest)))
            if old_h == heads - 1:
                finish(old_i, pieces)
                pieces = []
        if number < len(tasks):
            ctx, sgrad = middle(i, h, probs, low, pgrad)
            waiting = i, h, ctx, q, cg, low, sgrad


def close_kernel(row, first, phased, lengths, weights, x0, x1, x2, x3, x4, ctx, jg, act_n, act_f, u_n, u_f, weight, dense,
                 down, vectors, *rest):
    if first:
        qg_in = sg_in = mg_in = None
        send, keep, qg_o, sums_o = rest[-4:]
    else:
        qg_in, sg_in, mg_in = rest[:3]
        send, keep, a_keep, a_send, b_keep, b_send, sums_o = rest[-7:]
    c, y = spot()
    length = lengths[row]
    gain, shift = vectors[0:1], vectors[1:2]
    block = x0.shape[1]
    gs = ss = bs = qg = dg = None
    for x, act, u, side, slot, out, at in (
        (x2, act_f, u_f, 1 - y, c, keep, 0),
        ((x3, x4), act_f, u_f, 1 - y, 1 - c, send, 0),
        (x0, act_n, u_n, y, c, keep, 2),
        (x1, act_n, u_n, y, 1 - c, send, 2),
    ):
        place = 2 * side + slot
        whole = pl.ds(pl.multiple_of(place * block, block), block)
        part = pl.ds(pl.multiple_of(slot * block, block), block)
        context, joined = ctx[whole, :], jg[whole, :]
        out[at] = (mm(context[:, : dense.shape[0]], dense[...]) + mm(act[part, :], down[...])).astype(BF16)
        first_grad = mm(joined, weight[...])
        xhat, _ = norm_parts(x[0][...])
        normed = (xhat * gain + shift).astype(BF16)
        grad = out_grad_of(x[1][...], place * block, length, weights[row])
        out[at + 1] = (first_grad * gain + u[part, :].astype(F32)).astype(BF16)
        pieces = (
            jnp.sum(first_grad * xhat, axis=0, keepdims=True),
            jnp.sum(first_grad, axis=0, keepdims=True),
            jnp.sum(joined.astype(F32), axis=0, keepdims=True),
            mm(joined, normed, TN),
            mm(context, grad, TN),
        )
        if gs is None:
            gs, ss, bs, qg, dg = pieces
        else:
            gs, ss, bs, qg, dg = (a + b for a, b in zip((gs, ss, bs, qg, dg), pieces))
    if first:
        qg_o[0:768] = qg
        qg_o[768:1024] = dg
        sums_o[0:1] = gs
        sums_o[1:2] = ss
        sums_o[2:3] = bs
        return
    bit_a = bit_b = wide_bits(phased)[0]
    half = a_keep.shape[0]
    for h in range(3):
        for part in range(3):
            at, to = part * 256 + h * HEAD, (h * 3 + part) * HEAD
            value = (qg[at : at + HEAD] + qg_in[at : at + HEAD]).astype(BF16)
            number, to = to // half, to % half
            if number < 2:
                put(bit_a, number, a_keep, a_send, value, slice(to, to + HEAD))
            else:
                put(bit_b, 0, b_keep, b_send, value, slice(to, to + HEAD))
    value = (dg[0:half] + qg_in[768 : 768 + half]).astype(BF16)
    put(bit_b, 1, b_keep, b_send, value, slice(None))
    small = jnp.concatenate(
        [
            gs + sg_in[0:1],
            ss + sg_in[1:2],
            mg_in[0:2],
            bs + sg_in[2:3],
            mg_in[2:4],
            jnp.zeros_like(gs),
        ],
        axis=0,
    )
    sums_o[...] = small
    a_send[half : half + 16] = high_low(small)


def plus(a, b):
    return (a.astype(F32) + b.astype(F32)).astype(BF16)


def rows_of(number, size):
    return pl.ds(pl.multiple_of(number * size, size), size)


def join_1(u_keep, u_got, d_keep, d_got, *rest):
    u_keep_o, u_send_o, d_keep_o, d_send_o = rest[-4:]
    x, z, _ = wide_bits(True)
    size = u_keep_o.shape[0]
    for keep, got, bit, keep_o, send_o in ((u_keep, u_got, z, u_keep_o, u_send_o), (d_keep, d_got, x, d_keep_o, d_send_o)):
        mine, other = rows_of(bit, size), rows_of(1 - bit, size)
        send_o[...] = plus(keep[other, :], got[other, :])
        keep_o[...] = plus(keep[mine, :], got[mine, :])


def join_2(u_keep, u_got, d_keep, d_got, *rest):
    both = rest[-1]
    both[0] = plus(u_keep[...], u_got[...])
    both[1] = plus(d_keep[...], d_got[...])


def join_far(keep0, got0, keep1, got1, *rest):
    out = rest[-1]
    out[0:2] = plus(keep0[0:2], got0[0:2])
    out[2:4] = plus(keep1[0:2], got1[0:2])


def join_3(both, both_got, *rest):
    u_o, d_o = rest[-2:]
    u_o[...] = plus(both[0], both_got[0])
    d_o[...] = plus(both[1], both_got[1])


def join_4(u, u_got, d, d_got, *rest):
    u_o, d_o = rest[-2:]
    x, z, _ = wide_bits(True)
    size = u.shape[0]
    for own, got, bit, out in ((u, u_got, z, u_o), (d, d_got, x, d_o)):
        out[rows_of(bit, size), :] = own[...]
        out[rows_of(1 - bit, size), :] = got[...]


def last_1(a_keep, a_got, b_keep, b_got, small, *rest):
    a_keep_o, a_send_o, b_keep_o, b_send_o, small_o = rest[-5:]
    x, z, _ = wide_bits(True)
    part = a_keep_o.shape[0]
    for keep, got, bit, keep_o, send_o in ((a_keep, a_got, z, a_keep_o, a_send_o), (b_keep, b_got, z, b_keep_o, b_send_o)):
        mine, other = rows_of(bit, part), rows_of(1 - bit, part)
        send_o[0:part] = plus(keep[other, :], got[other, :])
        keep_o[...] = plus(keep[mine, :], got[mine, :])
    total = small[...] + back_together(a_got[2 * part : 2 * part + 16])
    small_o[...] = total
    a_send_o[part : part + 16] = high_low(total)


def last_2(a_keep, a_got, b_keep, b_got, small, *rest):
    last_o, small_o = rest[-2:]
    part = a_keep.shape[0]
    last_o[0:part] = plus(a_keep[...], a_got[0:part])
    last_o[part : 2 * part] = plus(b_keep[...], b_got[...])
    total = small[...] + back_together(a_got[part : part + 16])
    small_o[...] = total
    last_o[2 * part : 2 * part + 16] = high_low(total)


def last_3(last, last_got, small, *rest):
    a_o, b_o, small_o = rest[-3:]
    part = a_o.shape[0]
    a_o[...] = plus(last[0:part], last_got[0:part])
    b_o[...] = plus(last[part : 2 * part], last_got[part : 2 * part])
    small_o[...] = small[...] + back_together(last_got[2 * part : 2 * part + 16])


def widen_kernel(u, u_got, d, d_got, *rest):
    u_o, d_o, sign = rest[-3:]
    sign[...] = jnp.zeros_like(sign)
    x, z, _ = wide_bits(True)
    half = u.shape[0]
    for own, got, bit, out in ((u, u_got, x, u_o), (d, d_got, z, d_o)):
        out[rows_of(bit, half), :] = own[...].astype(F32)
        out[rows_of(1 - bit, half), :] = got[...].astype(F32)


def last_kernel(a, a_got, b, b_got, *rest):
    q_o, dense_o = rest[-2:]
    x, z, _ = wide_bits(True)
    half = a.shape[0]
    part = half // 2
    q_o[rows_of(x, half), :] = a[...].astype(F32)
    q_o[rows_of(1 - x, half), :] = a_got[...].astype(F32)
    for own, place in ((b, z), (b_got, 1 - z)):
        q_o[rows_of(4 + place, part), :] = own[0:part].astype(F32)
        dense_o[rows_of(place, part), :] = own[part:half].astype(F32)


def final_kernel(row, lengths, weights, own, keep, got, far, vectors, *rest):
    block_o, grad_o, sign = rest[-3:]
    sign[...] = jnp.zeros_like(sign)
    block = own.shape[1]
    near = keep[2:4].astype(F32) + got[2:4].astype(F32) + far[2 * row : 2 * row + 2].astype(F32)
    values = own[0].astype(F32)
    block_o[0] = (values + (near[0] + vectors[6:7] + vectors[7:8])).astype(BF16)
    xhat, inverse = norm_parts(own[0])
    u = near[1]
    slot = lax.axis_index("narrow") * block + lax.broadcasted_iota(jnp.int32, (block, 1), 0)
    scale = jnp.where(slot < lengths[row], weights[row], 0.0)
    mean = jnp.mean(u, axis=-1, keepdims=True)
    lean = jnp.mean(u * xhat, axis=-1, keepdims=True)
    grad_o[0] = own[1].astype(F32) * scale + inverse * (u - mean - xhat * lean)


def vector_kernel(small, mate, far, *rest):
    outs = rest[-7:]
    place = lax.axis_index("narrow")
    total = small[...] + mate[...] + far[...]
    own = small[...]
    share = outs[0].shape[0]
    for number in range(small.shape[1] // share):

        @pl.when(place == number)
        def _():
            at = number * share
            for line in range(4):
                outs[line][...] = total[line : line + 1, at : at + share].reshape(share)
            outs[6][...] = own[6:7, at : at + share].reshape(share)

    pieces = [own[4:5, part * 256 + h * HEAD : part * 256 + h * HEAD + HEAD] for h in range(3) for part in range(3)]
    outs[4][...] = jnp.concatenate(pieces, axis=1).reshape(9 * HEAD)
    outs[5][...] = own[5:6].reshape(own.shape[1])


SMEM = functools.partial(pl.BlockSpec, memory_space=pltpu.SMEM)
VMEM = functools.partial(pl.BlockSpec, memory_space=pltpu.VMEM)
ANY = functools.partial(pl.BlockSpec, memory_space=pl.ANY)
HBM = functools.partial(pl.BlockSpec, memory_space=pltpu.HBM)
COST = 1e8
WAIT = {'join_1': 200, 'join_2': 200, 'join_3': 200, 'join_far': 200}


def call(body, outs, scalars, arrays, name, us, scratch=(), limit=8, after=()):
    return pl.pallas_call(
        body,
        out_shape=outs,
        in_specs=[SMEM()] * len(scalars) + [VMEM()] * len(arrays) + [ANY()] * len(after),
        out_specs=[VMEM()] * len(outs),
        scratch_shapes=list(scratch),
        compiler_params=pltpu.CompilerParams(vmem_limit_bytes=limit * 1024 * 1024),
        cost_estimate=pl.CostEstimate(flops=int(us * COST), bytes_accessed=0, transcendentals=0),
        name=name,
    )(*scalars, *arrays, *after)


def exchange(x, axis, bit):
    size = lax.axis_size(axis)
    return lax.ppermute(x, axis, [(i, i ^ (1 << bit)) for i in range(size)])


def add_low(a, b):
    return (a.astype(F32) + b.astype(F32)).astype(BF16)


def scatter_sum(x, axis, bits):
    place = lax.axis_index(axis)
    for bit in bits:
        half = x.shape[0] // 2
        mine = (place >> bit) & 1
        keep = lax.dynamic_slice_in_dim(x, mine * half, half, 0)
        send = lax.dynamic_slice_in_dim(x, (1 - mine) * half, half, 0)
        x = add_low(keep, exchange(send, axis, bit))
    return x


def gather_back(x, axis, bits):
    place = lax.axis_index(axis)
    for bit in reversed(bits):
        mine = (place >> bit) & 1
        got = exchange(x, axis, bit)
        x = jnp.where(mine == 0, jnp.concatenate([x, got]), jnp.concatenate([got, x]))
    return x


def rotary(slot_count):
    position = np.arange(slot_count, dtype=np.float64)
    frequency = 10000.0 ** (-(2.0 * np.arange(ROT // 2)) / ROT)
    angles = position[:, None] * frequency[None, :]
    cos, sin = np.cos(angles), np.sin(angles)
    none8, none = np.zeros_like(sin), np.zeros((slot_count, HEAD - ROT))
    cos_t = np.concatenate([cos, cos, none + 1.0], axis=1)
    low_t = np.concatenate([-sin, none8, none], axis=1)
    high_t = np.concatenate([none8, sin, none], axis=1)
    return tuple(jnp.asarray(np.concatenate([t, t], axis=1), F32) for t in (cos_t, low_t, high_t))


def shards(tokens, lengths, tissues, ln1_gain, ln1_bias, qkv_weight, qkv_bias, dense_weight, dense_bias,
           ln2_gain, ln2_bias, up_weight, up_bias, down_weight, down_bias, out_probe):
    rows_local, block, width = tokens.shape
    inner = up_weight.shape[1]
    wide_count, narrow_count = lax.axis_size("wide"), lax.axis_size("narrow")
    place = lax.axis_index("narrow")
    slot_count = block * narrow_count
    bits = list(range(wide_count.bit_length() - 1))
    half_rows = 2 * block
    phased = wide_count == 8

    def shape(*dims, dtype=BF16):
        return jax.ShapeDtypeStruct(dims, dtype)

    def pack(r, after=()):
        return pl.pallas_call(
            functools.partial(pack_kernel, r),
            out_shape=shape(2, block, width),
            in_specs=[HBM()] * 2 + [ANY()] * len(after),
            out_specs=VMEM(),
            scratch_shapes=[pltpu.SemaphoreType.DMA((2,))],
            compiler_params=pltpu.CompilerParams(vmem_limit_bytes=8 * 1024 * 1024),
            name="pack",
        )(tokens, out_probe, *after)

    def gate(x, after):
        return pl.pallas_call(
            lambda *refs: None,
            out_shape=jax.ShapeDtypeStruct(x.shape, x.dtype),
            in_specs=[ANY()] * (1 + len(after)),
            out_specs=ANY(),
            input_output_aliases={0: 0},
            compiler_params=pltpu.CompilerParams(vmem_limit_bytes=1024 * 1024),
            name="gate",
        )(x, *after)

    own = [pack(0)]
    own.append(pack(1, own))
    over = [exchange(own[0], "narrow", 1)]
    mate = [exchange(x, "narrow", 0) for x in own]
    cross = [None, None]

    tables = rotary(slot_count)
    weight, vectors = call(
        prepare_kernel,
        [shape(768, width), shape(8, width, dtype=F32)],
        [],
        [qkv_weight.T, ln1_gain, ln1_bias, ln2_gain, ln2_bias, up_bias, qkv_bias, dense_bias, down_bias],
        "prepare",
        1,
    )

    def qkv(r, far, after=()):
        units = [over[r], *cross[r]] if far else [own[r], mate[r]]
        return call(
            functools.partial(qkv_kernel, far),
            [shape(half_rows, 768)],
            [],
            [*units, weight, vectors, *tables],
            "qkv",
            3,
            limit=8,
            after=after,
        )[0]

    def mlp(r, far, sums, last, after=()):
        units = [over[r], *cross[r]] if far else [own[r], mate[r]]
        first = sums is None
        return call(
            functools.partial(mlp_kernel, r, far, first, last, phased),
            [
                shape(half_rows, inner),
                shape(half_rows, 256),
                shape(half_rows, width),
                *([shape(width // 2, inner)] * 2 if last else [shape(width, inner, dtype=F32)]),
                *([shape(inner // 2, width)] * 2 if last else [shape(inner, width, dtype=F32)]),
                shape(4, width, dtype=F32),
            ],
            [lengths, row_weight],
            [*units, up_weight, down_weight, dense_weight, vectors, *(sums or [])],
            "mlp",
            7,
            limit=12,
            after=after,
        )

    def attend(r, near, far, cg_near, cg_far, after=()):
        big = pltpu.VMEM((slot_count, 256), BF16)
        tall = pltpu.VMEM((256, slot_count), BF16)
        total = pltpu.VMEM((slot_count, 256), F32)
        return call(
            functools.partial(attend_kernel, r),
            [shape(slot_count, 256), shape(slot_count, 768)],
            [lengths],
            [near, far, cg_near, cg_far, *tables],
            "attend",
            14,
            scratch=[big] * 4 + [tall] * 3 + [total] * 2,
            limit=12,
            after=after,
        )

    def close(r, ctx, jg, acts, us, sums, after=()):
        first = sums is None
        four = shape(4, block, width)
        half = 3 * HEAD
        if first:
            shapes = [four, four, shape(1024, width, dtype=F32), shape(3, width, dtype=F32)]
        else:
            shapes = [four, four, shape(half, width), shape(half + 16, width), shape(half, width), shape(half, width)]
            shapes.append(shape(8, width, dtype=F32))
        return call(
            functools.partial(close_kernel, r, first, phased),
            shapes,
            [lengths, row_weight],
            [own[r], mate[r], over[r], *cross[r], ctx, jg, *acts, *us, weight, dense_weight, down_weight, vectors, *(sums or [])],
            "close",
            0,
            limit=12,
            after=after,
        )

    hits = (tissues[:, None] == jnp.arange(TISSUES)[None, :]).astype(F32)
    counts = jnp.sum(hits * lengths[:, None].astype(F32), axis=0)[None, :]
    counts = counts + exchange(counts, "wide", bits[0])
    near_q0 = qkv(0, False)
    counts = gate(counts, [near_q0])
    counts = counts + exchange(counts, "wide", bits[1])
    near_q1 = qkv(1, False, [counts])
    for bit in bits[2:]:
        counts = counts + exchange(counts, "wide", bit)
    row_count = jnp.sum(hits * counts, axis=1)
    row_weight = rows_local * wide_count * slot_count / TISSUES / row_count
    over.append(exchange(gate(own[1], [near_q1]), "narrow", 1))
    a00, cg00, u00, *sums = mlp(0, False, None, False, [near_q1])
    a10, cg10, u10, *sums = mlp(1, False, sums, False)
    over[0] = gate(over[0], [sums[2]])
    cross[0] = [exchange(over[0][k], "narrow", 0) for k in range(2)]
    a01, cg01, u01, *sums = mlp(0, True, sums, False)
    far_q0 = qkv(0, True, [sums[2]])
    over[1] = gate(over[1], [far_q0])
    cross[1] = [exchange(over[1][k], "narrow", 0) for k in range(2)]
    a11, cg11, u11, u_keep, u_send, d_keep, d_send, mlp_sums = mlp(1, True, sums, True)

    def final(r, keep, got, far, before, after=()):
        spec = pl.BlockSpec((1, block, width), lambda i: (r, 0, 0))
        whole = shape(rows_local, block, width), shape(rows_local, block, width, dtype=F32)
        return pl.pallas_call(
            functools.partial(final_kernel, r),
            grid=(1,),
            out_shape=[*whole, shape(8, LANES, dtype=F32)],
            in_specs=[SMEM()] * 2 + [VMEM()] * 5 + [ANY()] * (len(before) + len(after)),
            out_specs=[spec, spec, pl.BlockSpec((8, LANES), lambda i: (0, 0))],
            input_output_aliases={7: 0, 8: 1} if before else {},
            compiler_params=pltpu.CompilerParams(vmem_limit_bytes=8 * 1024 * 1024),
            cost_estimate=pl.CostEstimate(flops=int(2.5 * COST), bytes_accessed=0, transcendentals=0),
            name="final",
        )(lengths, row_weight, own[r], keep, got, far, vectors, *before, *after)

    def join(body, shapes, arrays, after=(), us=0):
        return call(body, shapes, [], arrays, body.__name__, WAIT.get(body.__name__, us), after=after)

    far_q1 = qkv(1, True, [mlp_sums])
    ctx0, jg0 = attend(0, near_q0, far_q0, cg00, cg01, [far_q1])
    quarter = width // 4
    part = quarter // 2
    if phased:
        u_keep, u_send, d_keep, d_send = join(
            join_1,
            [shape(quarter, width)] * 4,
            [u_keep, exchange(u_send, "wide", 0), d_keep, exchange(d_send, "wide", 1)],
            [ctx0],
        )
    ctx1, jg1 = attend(1, near_q1, far_q1, cg10, cg11, [ctx0, u_keep] if phased else [ctx0])
    if phased:
        (both,) = join(
            join_2,
            [shape(2, quarter, width)],
            [u_keep, exchange(u_send, "wide", 1), d_keep, exchange(d_send, "wide", 0)],
            [ctx1],
        )
        both_got = exchange(both, "wide", 2)
    send0, keep0, qg, close_sums = close(
        0, ctx0, jg0, (a00, a01), (u00, u01), None, [ctx1, both] if phased else [ctx1]
    )
    got0 = exchange(send0, "narrow", 0)
    send1, keep1, a_keep, a_send, b_keep, b_send, small = close(
        1, ctx1, jg1, (a10, a11), (u10, u11), [qg, close_sums, mlp_sums]
    )
    got1 = exchange(send1, "narrow", 0)
    if phased:
        tiny = shape(8, width, dtype=F32)
        a_keep, a_send, b_keep, b_send, small = join(
            last_1,
            [shape(part, width), shape(part + 16, width), shape(part, width), shape(part, width), tiny],
            [a_keep, exchange(a_send, "wide", 0), b_keep, exchange(b_send, "wide", 0), small],
        )
        u_part, d_part = join(join_3, [shape(quarter, width)] * 2, [both, both_got], [a_keep])
        far = join(join_far, [shape(4, block, width)], [keep0, got0, keep1, got1], [u_part])[0]
        far_got = exchange(far, "narrow", 1)
        last, small = join(
            last_2,
            [shape(quarter + 16, width), tiny],
            [a_keep, exchange(a_send, "wide", 1), b_keep, exchange(b_send, "wide", 1), small],
            [far],
        )
        last_got = exchange(last, "wide", 2)
        u_half, d_half = join(
            join_4,
            [shape(2 * quarter, width)] * 2,
            [u_part, exchange(u_part, "wide", 1), d_part, exchange(d_part, "wide", 0)],
            [last],
            us=10,
        )
        a_part, b_part, small = join(
            last_3, [shape(part, width), shape(part, width), tiny], [last, last_got, small], [u_half]
        )
        a_half, b_half = join(
            join_4,
            [shape(quarter, width)] * 2,
            [a_part, exchange(a_part, "wide", 1), b_part, exchange(b_part, "wide", 0)],
            us=20,
        )
        *outs, _ = final(0, keep0, got0, far_got, [], [a_half])
        block_out, grad_tokens, sign = final(1, keep1, got1, far_got, outs)
        up_grad, down_grad, sign = join(
            widen_kernel,
            [shape(width, inner, dtype=F32), shape(inner, width, dtype=F32), shape(8, LANES, dtype=F32)],
            [u_half, exchange(u_half, "wide", 0), d_half, exchange(d_half, "wide", 1)],
            [sign],
        )
        q_grad, dense_grad = join(
            last_kernel,
            [shape(9 * HEAD, width, dtype=F32), shape(3 * HEAD, width, dtype=F32)],
            [a_half, exchange(a_half, "wide", 0), b_half, exchange(b_half, "wide", 1)],
            [sign],
        )
    else:
        far = join(join_far, [shape(4, block, width)], [keep0, got0, keep1, got1])[0]
        far_got = exchange(far, "narrow", 1)
        *outs, _ = final(0, keep0, got0, far_got, [])
        block_out, grad_tokens, sign = final(1, keep1, got1, far_got, outs)

        def total(keep, send):
            return gather_back(scatter_sum(jnp.concatenate([keep, send]), "wide", bits), "wide", bits).astype(F32)

        up_grad, down_grad = total(u_keep, u_send), total(d_keep, d_send)
        a, b = total(a_keep, a_send[:quarter]), total(b_keep, b_send)
        q_grad, dense_grad = jnp.concatenate([a, b[:quarter]]), b[quarter:]
        for bit in bits:
            small = small + exchange(small, "wide", bit)

    share = width // narrow_count
    if phased:
        small = gate(small, [a_half])
    mate_small = exchange(small, "narrow", 0)
    far_small = exchange(small + mate_small, "narrow", 1)
    line = shape(share, dtype=F32)
    gain_1, shift_1, gain_2, shift_2, q_bias_grad, up_bias_grad, out_bias = join(
        vector_kernel,
        [line, line, line, line, shape(9 * HEAD, dtype=F32), shape(inner, dtype=F32), line],
        [small, mate_small, far_small],
        [sign],
    )
    return (
        block_out,
        grad_tokens,
        gain_1,
        shift_1,
        q_grad.T,
        q_bias_grad,
        dense_grad,
        out_bias,
        gain_2,
        shift_2,
        up_grad,
        up_bias_grad,
        down_grad,
        out_bias,
    )


def solution(mesh):
    placed = (
        P("wide", "narrow", None),
        P("wide"),
        P("wide"),
        P(),
        P(),
        P(None, "narrow"),
        P("narrow"),
        P("narrow", None),
        P(),
        P(),
        P(),
        P(None, "narrow"),
        P("narrow"),
        P("narrow", None),
        P(),
        P("wide", "narrow", None),
    )
    return jax.shard_map(
        shards,
        mesh=mesh,
        in_specs=placed,
        out_specs=(
            P("wide", "narrow", None),
            P("wide", "narrow", None),
            P("narrow"),
            P("narrow"),
            P(None, "narrow"),
            P("narrow"),
            P("narrow", None),
            P("narrow"),
            P("narrow"),
            P("narrow"),
            P(None, "narrow"),
            P("narrow"),
            P("narrow", None),
            P("narrow"),
        ),
        check_vma=False,
    )
```

```python
import functools
import math

import jax
import jax.numpy as jnp
import numpy as np
from jax import lax
from jax.experimental import pallas as pl
from jax.experimental.pallas import tpu as pltpu
from jax.sharding import PartitionSpec as P

HEAD = 64
ROT = 16
TISSUES = 8
LANES = 128
EPS = 1e-05
BIG = -1e30
F32 = jnp.float32
BF16 = jnp.bfloat16
ERF_P = 0.39
ERF_C = (
    0.2353254092560988,
    0.09138720671028266,
    0.6495624403330551,
    -0.6354040754153405,
    0.8866667192133076,
    -0.22753770177595345,
)

NN = (((1,), (0,)), ((), ()))
NT = (((1,), (1,)), ((), ()))
TN = (((0,), (0,)), ((), ()))


def mm(a, b, dims=NN):
    return lax.dot_general(a, b, dims, preferred_element_type=F32)


def norm_parts(tokens):
    values = tokens.astype(F32)
    centered = values - jnp.mean(values, axis=-1, keepdims=True)
    inverse = lax.rsqrt(jnp.mean(centered * centered, axis=-1, keepdims=True) + EPS)
    return centered * inverse, inverse


def gelu_pair(x):
    size = jnp.abs(x)
    t = 1.0 / (1.0 + (ERF_P * math.sqrt(0.5)) * size)
    bell = jnp.exp(-0.5 * (x * x))
    poly = jnp.full_like(x, 0.5 * ERF_C[-1])
    for c in ERF_C[-2::-1]:
        poly = poly * t + 0.5 * c
    tail = poly * t * bell
    phi = jnp.where(x < 0, tail, 1.0 - tail)
    return x * phi, phi + x * (bell * (1.0 / math.sqrt(2.0 * math.pi)))


def turn(x, cos_t, low_t, high_t, sign):
    up = pltpu.roll(x, LANES - ROT // 2, 1)
    down = pltpu.roll(x, ROT // 2, 1)
    return x * cos_t + sign * (up * low_t + down * high_t)


def place_two(c, first, second):
    a = jnp.where(c == 0, first, second)
    b = jnp.where(c == 0, second, first)
    return jnp.concatenate([a, b], axis=0)


def out_grad_of(probe, first_slot, length, weight):
    slot = first_slot + lax.broadcasted_iota(jnp.int32, (probe.shape[0], 1), 0)
    scale = jnp.where(slot < length, weight, 0.0)
    return (probe.astype(F32) * scale).astype(BF16)


def spot():
    place = lax.axis_index("narrow")
    return place % 2, place // 2


def wide_bits(phased):
    if not phased:
        return 0, 0, 0
    place = lax.axis_index("wide")
    return place % 2, (place // 2) % 2, place // 4


def put(bit, half, keep, send, value, *where):
    if isinstance(bit, int):
        (keep if bit == half else send)[where] = value
        return

    @pl.when(bit == half)
    def _():
        keep[where] = value

    @pl.when(bit != half)
    def _():
        send[where] = value


def high_low(values):
    high = values.astype(BF16)
    return jnp.concatenate([high, (values - high.astype(F32)).astype(BF16)], axis=0)


def back_together(pair):
    pair = pair.astype(F32)
    return pair[:8] + pair[8:]


def pack_kernel(tokens, probe, *rest):
    out = rest[-1]
    out[0] = tokens[...]
    out[1] = probe[...]


def prepare_kernel(weight, g1, b1, g2, b2, up_b, q_b, dense_b, down_b, weight_o, vectors_o):
    width = weight.shape[1]
    bias = q_b[...].reshape(1, q_b.shape[0])
    pieces = []
    for part in range(3):
        for h in range(3):
            at = (h * 3 + part) * HEAD
            weight_o[part * 256 + h * HEAD : part * 256 + h * HEAD + HEAD, :] = weight[at : at + HEAD, :]
            pieces.append(bias[:, at : at + HEAD])
        weight_o[part * 256 + 3 * HEAD : part * 256 + 256, :] = jnp.zeros((HEAD, width), BF16)
        pieces.append(jnp.zeros((1, HEAD), F32))
    for line, v in enumerate((g1, b1, g2, b2, up_b, None, dense_b, down_b)):
        vectors_o[line : line + 1] = jnp.concatenate(pieces, axis=1) if v is None else v[...].reshape(1, v.shape[0])


def pair_of(far, refs):
    return ((refs[0][...], refs[1][...]), refs[2:]) if far else ((refs[0][0], refs[0][1]), refs[1:])


def qkv_kernel(far, x0, *refs):
    x1, (weight, vectors, cos_t, low_t, high_t, *rest) = pair_of(far, refs)
    out = rest[-1]
    c, y = spot()
    half = 1 - y if far else y
    gain, shift, bias = vectors[0:1], vectors[1:2], vectors[5:6]
    tokens = place_two(c, x0[0], x1[0])
    rows = tokens.shape[0]
    xhat, _ = norm_parts(tokens)
    normed = (xhat * gain + shift).astype(BF16)
    spots = pl.ds(pl.multiple_of(half * rows, rows), rows)
    cos_b, low_b, high_b = cos_t[spots, :], low_t[spots, :], high_t[spots, :]
    for part in range(3):
        joined = mm(normed, weight[part * 256 : part * 256 + 256, :], NT)
        joined = joined + bias[:, part * 256 : part * 256 + 256]
        for pair in range(2):
            x = joined[:, pair * LANES : pair * LANES + LANES]
            if part < 2:
                x = turn(x, cos_b, low_b, high_b, 1.0)
            x = x.astype(BF16)
            if part == 0:
                x = x * jnp.asarray(1.0 / math.sqrt(HEAD), BF16)
            at = part * 256 + pair * LANES
            out[:, at : at + LANES] = x


def mlp_kernel(row, far, first, last, phased, lengths, weights, x0, *refs):
    x1, (up, down, dense, vectors, *rest) = pair_of(far, refs)
    if first:
        ug_in = dg_in = sums_in = None
    else:
        ug_in, dg_in, sums_in = rest[:3]
    if last:
        active_o, cgrad_o, u_o, u_keep, u_send, d_keep, d_send, sums_o = rest[-8:]
        bit_u, bit_d, _ = wide_bits(phased)
    else:
        active_o, cgrad_o, u_o, ug_o, dg_o, sums_o = rest[-6:]
    c, y = spot()
    half = 1 - y if far else y
    length = lengths[row]
    gain, shift, up_b = vectors[2:3], vectors[3:4], vectors[4:5]
    tokens = place_two(c, x0[0], x1[0])
    probe = place_two(c, x0[1], x1[1])
    rows, width = tokens.shape
    grad = out_grad_of(probe, half * rows, length, weights[row])
    inner = up.shape[1]
    step = 256
    agrads = [mm(grad, down[0:step, :], NT)]
    xhat, _ = norm_parts(tokens)
    normed = (xhat * gain + shift).astype(BF16)
    hiddens = [mm(normed, up[:, 0:step])]
    cgrad_o[:, : dense.shape[0]] = mm(grad, dense[...], NT).astype(BF16)
    cgrad_o[:, dense.shape[0] :] = jnp.zeros((rows, 256 - dense.shape[0]), BF16)
    total = None
    for at in range(0, inner, step):
        cols, after = slice(at, at + step), slice(at + step, at + 2 * step)
        if at + step < inner:
            hiddens.append(mm(normed, up[:, after]))
            agrads.append(mm(grad, down[after, :], NT))
        active, slope = gelu_pair(hiddens.pop(0) + up_b[:, cols])
        active = active.astype(BF16)
        active_o[:, cols] = active
        hgrad = (agrads.pop(0) * slope).astype(BF16)
        piece = mm(hgrad, up[:, cols], NT)
        total = piece if total is None else total + piece
        ug = mm(normed, hgrad, TN)
        dg = mm(active, grad, TN)
        us = jnp.sum(hgrad.astype(F32), axis=0, keepdims=True)
        if not first:
            ug = ug + ug_in[:, cols]
            dg = dg + dg_in[cols, :]
            us = us + sums_in[2:3, cols]
        if last:
            ug, dg = ug.astype(BF16), dg.astype(BF16)
            half = width // 2
            for h in range(2):
                put(bit_u, h, u_keep, u_send, ug[h * half : h * half + half], slice(None), cols)
            for top in range(at, at + step, 128):
                h, to = top // (inner // 2), top % (inner // 2)
                put(bit_d, h, d_keep, d_send, dg[top - at : top - at + 128], slice(to, to + 128))
        else:
            ug_o[:, cols] = ug
            dg_o[cols, :] = dg
        sums_o[2:3, cols] = us
    u_o[...] = (total * gain).astype(u_o.dtype)
    gs = jnp.sum(total * xhat, axis=0, keepdims=True)
    ss = jnp.sum(total, axis=0, keepdims=True)
    os = jnp.sum(grad.astype(F32), axis=0, keepdims=True)
    if not first:
        gs, ss, os = gs + sums_in[0:1], ss + sums_in[1:2], os + sums_in[3:4]
    sums_o[0:1] = gs
    sums_o[1:2] = ss
    sums_o[3:4] = os


def attend_kernel(row, lengths, near, far, cg_near, cg_far, cos_t, low_t, high_t, *rest):
    ctx_o, jg_o, q_s, k_s, v_s, c_s, kt_s, vt_s, ct_s, dk_s, dv_s = rest[-11:]
    _, y = spot()
    length = lengths[row]
    half = near.shape[0]
    slots = 2 * half
    block = 256
    for source, cg, place in ((near, cg_near, y), (far, cg_far, 1 - y)):
        spots = pl.ds(pl.multiple_of(place * half, half), half)
        q_s[spots, :] = source[:, 0:256]
        k_s[spots, :] = source[:, 256:512]
        v_s[spots, :] = source[:, 512:768]
        c_s[spots, :] = cg[...]
    kt_s[...] = k_s[...].T
    vt_s[...] = v_s[...].T
    ct_s[...] = c_s[...].T
    heads, blocks = 3, slots // block
    least = slots * 5 // 8
    lane = lax.broadcasted_iota(jnp.int32, (block, LANES), 1)
    key = lax.broadcasted_iota(jnp.int32, (block, block), 0)
    below = key <= lax.broadcasted_iota(jnp.int32, (block, block), 1)

    def part(j):
        return slice(j * block, j * block + block)

    def places(h):
        pair = (h // 2) * LANES
        return slice(pair, pair + LANES), slice(h * HEAD, h * HEAD + HEAD)

    def products(i, h):
        lanes, _ = places(h)
        q, cg = q_s[part(i), lanes], c_s[part(i), lanes]
        if h < 2:
            mine = (lane < HEAD) if h == 0 else (lane >= HEAD)
            q = jnp.where(mine, q, jnp.zeros_like(q))
            cg = jnp.where(mine, cg, jnp.zeros_like(cg))
        scores = [mm(k_s[part(j), lanes], q, NT) for j in range(i + 1)]
        pgrad = [mm(v_s[part(j), lanes], cg, NT) for j in range(i + 1)]
        return q, cg, scores, pgrad

    def softmax(i, scores):
        for j in range(i + 1):
            allowed = below if j == i else None
            if (j + 1) * block > least:
                inside = key < length - j * block
                allowed = inside if allowed is None else allowed & inside
            if allowed is not None:
                scores[j] = jnp.where(allowed, scores[j], BIG)
        peak = jnp.max(functools.reduce(jnp.maximum, scores), axis=0, keepdims=True)
        raised = [jnp.exp(x - peak) for x in scores]
        scale = 1.0 / jnp.sum(functools.reduce(jnp.add, raised), axis=0, keepdims=True)
        probs = [x * scale for x in raised]
        return probs, [x.astype(BF16) for x in probs]

    def middle(i, h, probs, low, pgrad):
        _, lines = places(h)
        ctx = functools.reduce(jnp.add, [mm(vt_s[lines, part(j)], low[j]) for j in range(i + 1)])
        inner = jnp.sum(ct_s[lines, part(i)].astype(F32) * ctx, axis=0, keepdims=True)
        return ctx, [(p * (g - inner)).astype(BF16) for p, g in zip(probs, pgrad)]

    def gradients(i, h, q, cg, low, sgrad):
        lanes, lines = places(h)
        dq = functools.reduce(jnp.add, [mm(kt_s[lines, part(j)], sgrad[j]) for j in range(i + 1)])
        for j in range(i + 1):
            dk, dv = mm(sgrad[j], q), mm(low[j], cg)
            if i == blocks - 1 and h != 1:
                dk_s[part(j), lanes] = dk
                dv_s[part(j), lanes] = dv
            else:
                dk_s[part(j), lanes] += dk
                dv_s[part(j), lanes] += dv
        return dq

    def finish(i, pieces):
        rows = part(i)
        empty = jnp.zeros((256 - heads * HEAD, block), F32)
        ctx_o[rows, :] = jnp.concatenate([p[0] for p in pieces] + [empty], axis=0).T.astype(BF16)
        dq = jnp.concatenate([p[1] for p in pieces] + [empty], axis=0).T * (1.0 / math.sqrt(HEAD))
        for pair in range(2):
            lanes = slice(pair * LANES, pair * LANES + LANES)
            turned = turn(dq[:, lanes], cos_t[rows, :], low_t[rows, :], high_t[rows, :], -1.0)
            jg_o[rows, lanes] = turned.astype(BF16)
            turned = turn(dk_s[rows, lanes], cos_t[rows, :], low_t[rows, :], high_t[rows, :], -1.0)
            jg_o[rows, 256 + pair * LANES : 256 + pair * LANES + LANES] = turned.astype(BF16)
        jg_o[rows, 512:768] = dv_s[rows, :].astype(BF16)

    tasks = [(i, h) for i in range(blocks - 1, -1, -1) for h in range(heads)]
    pieces, waiting = [], None
    ahead = products(*tasks[0])
    for number in range(len(tasks) + 1):
        if number < len(tasks):
            i, h = tasks[number]
            q, cg, scores, pgrad = ahead
            if number + 1 < len(tasks):
                ahead = products(*tasks[number + 1])
            probs, low = softmax(i, scores)
        if waiting is not None:
            old_i, old_h, ctx, *rest = waiting
            pieces.append((ctx, gradients(old_i, old_h, *rest)))
            if old_h == heads - 1:
                finish(old_i, pieces)
                pieces = []
        if number < len(tasks):
            ctx, sgrad = middle(i, h, probs, low, pgrad)
            waiting = i, h, ctx, q, cg, low, sgrad


def close_kernel(row, first, phased, lengths, weights, x0, x1, x2, x3, x4, ctx, jg, act_n, act_f, u_n, u_f, weight, dense,
                 down, vectors, *rest):
    if first:
        qg_in = sg_in = mg_in = None
        send, keep, qg_o, sums_o = rest[-4:]
    else:
        qg_in, sg_in, mg_in = rest[:3]
        send, keep, a_keep, a_send, b_keep, b_send, sums_o = rest[-7:]
    c, y = spot()
    length = lengths[row]
    gain, shift = vectors[0:1], vectors[1:2]
    block = x0.shape[1]
    gs = ss = bs = qg = dg = None
    for x, act, u, side, slot, out, at in (
        (x2, act_f, u_f, 1 - y, c, keep, 0),
        ((x3, x4), act_f, u_f, 1 - y, 1 - c, send, 0),
        (x0, act_n, u_n, y, c, keep, 2),
        (x1, act_n, u_n, y, 1 - c, send, 2),
    ):
        place = 2 * side + slot
        whole = pl.ds(pl.multiple_of(place * block, block), block)
        part = pl.ds(pl.multiple_of(slot * block, block), block)
        context, joined = ctx[whole, :], jg[whole, :]
        out[at] = (mm(context[:, : dense.shape[0]], dense[...]) + mm(act[part, :], down[...])).astype(BF16)
        first_grad = mm(joined, weight[...])
        xhat, _ = norm_parts(x[0][...])
        normed = (xhat * gain + shift).astype(BF16)
        grad = out_grad_of(x[1][...], place * block, length, weights[row])
        out[at + 1] = (first_grad * gain + u[part, :].astype(F32)).astype(BF16)
        pieces = (
            jnp.sum(first_grad * xhat, axis=0, keepdims=True),
            jnp.sum(first_grad, axis=0, keepdims=True),
            jnp.sum(joined.astype(F32), axis=0, keepdims=True),
            mm(joined, normed, TN),
            mm(context, grad, TN),
        )
        if gs is None:
            gs, ss, bs, qg, dg = pieces
        else:
            gs, ss, bs, qg, dg = (a + b for a, b in zip((gs, ss, bs, qg, dg), pieces))
    if first:
        qg_o[0:768] = qg
        qg_o[768:1024] = dg
        sums_o[0:1] = gs
        sums_o[1:2] = ss
        sums_o[2:3] = bs
        return
    bit_a = bit_b = wide_bits(phased)[0]
    half = a_keep.shape[0]
    for h in range(3):
        for part in range(3):
            at, to = part * 256 + h * HEAD, (h * 3 + part) * HEAD
            value = (qg[at : at + HEAD] + qg_in[at : at + HEAD]).astype(BF16)
            number, to = to // half, to % half
            if number < 2:
                put(bit_a, number, a_keep, a_send, value, slice(to, to + HEAD))
            else:
                put(bit_b, 0, b_keep, b_send, value, slice(to, to + HEAD))
    value = (dg[0:half] + qg_in[768 : 768 + half]).astype(BF16)
    put(bit_b, 1, b_keep, b_send, value, slice(None))
    small = jnp.concatenate(
        [
            gs + sg_in[0:1],
            ss + sg_in[1:2],
            mg_in[0:2],
            bs + sg_in[2:3],
            mg_in[2:4],
            jnp.zeros_like(gs),
        ],
        axis=0,
    )
    sums_o[...] = small
    a_send[half : half + 16] = high_low(small)


def plus(a, b):
    return (a.astype(F32) + b.astype(F32)).astype(BF16)


def rows_of(number, size):
    return pl.ds(pl.multiple_of(number * size, size), size)


def join_1(u_keep, u_got, d_keep, d_got, *rest):
    u_keep_o, u_send_o, d_keep_o, d_send_o = rest[-4:]
    x, z, _ = wide_bits(True)
    size = u_keep_o.shape[0]
    for keep, got, bit, keep_o, send_o in ((u_keep, u_got, z, u_keep_o, u_send_o), (d_keep, d_got, x, d_keep_o, d_send_o)):
        mine, other = rows_of(bit, size), rows_of(1 - bit, size)
        send_o[...] = plus(keep[other, :], got[other, :])
        keep_o[...] = plus(keep[mine, :], got[mine, :])


def join_2(u_keep, u_got, d_keep, d_got, *rest):
    both = rest[-1]
    both[0] = plus(u_keep[...], u_got[...])
    both[1] = plus(d_keep[...], d_got[...])


def join_far(keep0, got0, keep1, got1, *rest):
    out = rest[-1]
    out[0:2] = plus(keep0[0:2], got0[0:2])
    out[2:4] = plus(keep1[0:2], got1[0:2])


def join_3(both, both_got, *rest):
    u_o, d_o = rest[-2:]
    u_o[...] = plus(both[0], both_got[0])
    d_o[...] = plus(both[1], both_got[1])


def join_4(u, u_got, d, d_got, *rest):
    u_o, d_o = rest[-2:]
    x, z, _ = wide_bits(True)
    size = u.shape[0]
    for own, got, bit, out in ((u, u_got, z, u_o), (d, d_got, x, d_o)):
        out[rows_of(bit, size), :] = own[...]
        out[rows_of(1 - bit, size), :] = got[...]


def last_1(a_keep, a_got, b_keep, b_got, small, *rest):
    a_keep_o, a_send_o, b_keep_o, b_send_o, small_o = rest[-5:]
    x, z, _ = wide_bits(True)
    part = a_keep_o.shape[0]
    for keep, got, bit, keep_o, send_o in ((a_keep, a_got, z, a_keep_o, a_send_o), (b_keep, b_got, z, b_keep_o, b_send_o)):
        mine, other = rows_of(bit, part), rows_of(1 - bit, part)
        send_o[0:part] = plus(keep[other, :], got[other, :])
        keep_o[...] = plus(keep[mine, :], got[mine, :])
    total = small[...] + back_together(a_got[2 * part : 2 * part + 16])
    small_o[...] = total
    a_send_o[part : part + 16] = high_low(total)


def last_2(a_keep, a_got, b_keep, b_got, small, *rest):
    last_o, small_o = rest[-2:]
    part = a_keep.shape[0]
    last_o[0:part] = plus(a_keep[...], a_got[0:part])
    last_o[part : 2 * part] = plus(b_keep[...], b_got[...])
    total = small[...] + back_together(a_got[part : part + 16])
    small_o[...] = total
    last_o[2 * part : 2 * part + 16] = high_low(total)


def last_3(last, last_got, small, *rest):
    a_o, b_o, small_o = rest[-3:]
    part = a_o.shape[0]
    a_o[...] = plus(last[0:part], last_got[0:part])
    b_o[...] = plus(last[part : 2 * part], last_got[part : 2 * part])
    small_o[...] = small[...] + back_together(last_got[2 * part : 2 * part + 16])


def widen_kernel(u, u_got, d, d_got, *rest):
    u_o, d_o, sign = rest[-3:]
    sign[...] = jnp.zeros_like(sign)
    x, z, _ = wide_bits(True)
    half = u.shape[0]
    for own, got, bit, out in ((u, u_got, x, u_o), (d, d_got, z, d_o)):
        out[rows_of(bit, half), :] = own[...].astype(F32)
        out[rows_of(1 - bit, half), :] = got[...].astype(F32)


def last_kernel(a, a_got, b, b_got, *rest):
    q_o, dense_o = rest[-2:]
    x, z, _ = wide_bits(True)
    half = a.shape[0]
    part = half // 2
    q_o[rows_of(x, half), :] = a[...].astype(F32)
    q_o[rows_of(1 - x, half), :] = a_got[...].astype(F32)
    for own, place in ((b, z), (b_got, 1 - z)):
        q_o[rows_of(4 + place, part), :] = own[0:part].astype(F32)
        dense_o[rows_of(place, part), :] = own[part:half].astype(F32)


def final_kernel(lengths, weights, own0, keep0, got0, own1, keep1, got1, far, vectors, *rest):
    block_o, grad_o, sign = rest[-3:]
    sign[...] = jnp.zeros_like(sign)
    block = own0.shape[1]
    slot = lax.axis_index("narrow") * block + lax.broadcasted_iota(jnp.int32, (block, 1), 0)
    for row, (own, keep, got) in enumerate(((own0, keep0, got0), (own1, keep1, got1))):

        @pl.when(pl.program_id(0) == row)
        def _():
            near = keep[2:4].astype(F32) + got[2:4].astype(F32) + far[2 * row : 2 * row + 2].astype(F32)
            values = own[0].astype(F32)
            block_o[0] = (values + (near[0] + vectors[6:7] + vectors[7:8])).astype(BF16)
            xhat, inverse = norm_parts(own[0])
            u = near[1]
            scale = jnp.where(slot < lengths[row], weights[row], 0.0)
            mean = jnp.mean(u, axis=-1, keepdims=True)
            lean = jnp.mean(u * xhat, axis=-1, keepdims=True)
            grad_o[0] = own[1].astype(F32) * scale + inverse * (u - mean - xhat * lean)


def vector_kernel(small, mate, far, *rest):
    outs = rest[-8:]
    place = lax.axis_index("narrow")
    total = small[...] + mate[...] + far[...]
    own = small[...]
    share = outs[0].shape[0]
    for number in range(small.shape[1] // share):

        @pl.when(place == number)
        def _():
            at = number * share
            for line in range(4):
                outs[line][...] = total[line : line + 1, at : at + share].reshape(share)
            for out in outs[6:8]:
                out[...] = own[6:7, at : at + share].reshape(share)

    pieces = [own[4:5, part * 256 + h * HEAD : part * 256 + h * HEAD + HEAD] for h in range(3) for part in range(3)]
    outs[4][...] = jnp.concatenate(pieces, axis=1).reshape(9 * HEAD)
    outs[5][...] = own[5:6].reshape(own.shape[1])


SMEM = functools.partial(pl.BlockSpec, memory_space=pltpu.SMEM)
VMEM = functools.partial(pl.BlockSpec, memory_space=pltpu.VMEM)
ANY = functools.partial(pl.BlockSpec, memory_space=pl.ANY)
HBM = functools.partial(pl.BlockSpec, memory_space=pltpu.HBM)
COST = 1e8
WAIT = {'join_1': 200, 'join_2': 200, 'join_3': 200, 'join_far': 200}


def call(body, outs, scalars, arrays, name, us, scratch=(), limit=8, after=()):
    return pl.pallas_call(
        body,
        out_shape=outs,
        in_specs=[SMEM()] * len(scalars) + [VMEM()] * len(arrays) + [ANY()] * len(after),
        out_specs=[VMEM()] * len(outs),
        scratch_shapes=list(scratch),
        compiler_params=pltpu.CompilerParams(vmem_limit_bytes=limit * 1024 * 1024),
        cost_estimate=pl.CostEstimate(flops=int(us * COST), bytes_accessed=0, transcendentals=0),
        name=name,
    )(*scalars, *arrays, *after)


def exchange(x, axis, bit):
    size = lax.axis_size(axis)
    return lax.ppermute(x, axis, [(i, i ^ (1 << bit)) for i in range(size)])


def add_low(a, b):
    return (a.astype(F32) + b.astype(F32)).astype(BF16)


def scatter_sum(x, axis, bits):
    place = lax.axis_index(axis)
    for bit in bits:
        half = x.shape[0] // 2
        mine = (place >> bit) & 1
        keep = lax.dynamic_slice_in_dim(x, mine * half, half, 0)
        send = lax.dynamic_slice_in_dim(x, (1 - mine) * half, half, 0)
        x = add_low(keep, exchange(send, axis, bit))
    return x


def gather_back(x, axis, bits):
    place = lax.axis_index(axis)
    for bit in reversed(bits):
        mine = (place >> bit) & 1
        got = exchange(x, axis, bit)
        x = jnp.where(mine == 0, jnp.concatenate([x, got]), jnp.concatenate([got, x]))
    return x


def rotary(slot_count):
    position = np.arange(slot_count, dtype=np.float64)
    frequency = 10000.0 ** (-(2.0 * np.arange(ROT // 2)) / ROT)
    angles = position[:, None] * frequency[None, :]
    cos, sin = np.cos(angles), np.sin(angles)
    none8, none = np.zeros_like(sin), np.zeros((slot_count, HEAD - ROT))
    cos_t = np.concatenate([cos, cos, none + 1.0], axis=1)
    low_t = np.concatenate([-sin, none8, none], axis=1)
    high_t = np.concatenate([none8, sin, none], axis=1)
    return tuple(jnp.asarray(np.concatenate([t, t], axis=1), F32) for t in (cos_t, low_t, high_t))


def shards(tokens, lengths, tissues, ln1_gain, ln1_bias, qkv_weight, qkv_bias, dense_weight, dense_bias,
           ln2_gain, ln2_bias, up_weight, up_bias, down_weight, down_bias, out_probe):
    rows_local, block, width = tokens.shape
    inner = up_weight.shape[1]
    wide_count, narrow_count = lax.axis_size("wide"), lax.axis_size("narrow")
    place = lax.axis_index("narrow")
    slot_count = block * narrow_count
    bits = list(range(wide_count.bit_length() - 1))
    half_rows = 2 * block
    phased = wide_count == 8

    def shape(*dims, dtype=BF16):
        return jax.ShapeDtypeStruct(dims, dtype)

    def pack(r, after=()):
        return call(pack_kernel, [shape(2, block, width)], [], [tokens[r], out_probe[r]], "pack", 0, after=after)[0]

    def gate(x, after):
        return pl.pallas_call(
            lambda *refs: None,
            out_shape=jax.ShapeDtypeStruct(x.shape, x.dtype),
            in_specs=[ANY()] * (1 + len(after)),
            out_specs=ANY(),
            input_output_aliases={0: 0},
            compiler_params=pltpu.CompilerParams(vmem_limit_bytes=1024 * 1024),
            name="gate",
        )(x, *after)

    own = [pack(0)]
    own.append(pack(1, own))
    over = [exchange(own[0], "narrow", 1)]
    mate = [exchange(x, "narrow", 0) for x in own]
    cross = [None, None]

    tables = rotary(slot_count)
    weight, vectors = call(
        prepare_kernel,
        [shape(768, width), shape(8, width, dtype=F32)],
        [],
        [qkv_weight.T, ln1_gain, ln1_bias, ln2_gain, ln2_bias, up_bias, qkv_bias, dense_bias, down_bias],
        "prepare",
        1,
    )

    def qkv(r, far, after=()):
        units = [over[r], *cross[r]] if far else [own[r], mate[r]]
        return call(
            functools.partial(qkv_kernel, far),
            [shape(half_rows, 768)],
            [],
            [*units, weight, vectors, *tables],
            "qkv",
            3,
            limit=8,
            after=after,
        )[0]

    def mlp(r, far, sums, last, after=()):
        units = [over[r], *cross[r]] if far else [own[r], mate[r]]
        first = sums is None
        return call(
            functools.partial(mlp_kernel, r, far, first, last, phased),
            [
                shape(half_rows, inner),
                shape(half_rows, 256),
                shape(half_rows, width),
                *([shape(width // 2, inner)] * 2 if last else [shape(width, inner, dtype=F32)]),
                *([shape(inner // 2, width)] * 2 if last else [shape(inner, width, dtype=F32)]),
                shape(4, width, dtype=F32),
            ],
            [lengths, row_weight],
            [*units, up_weight, down_weight, dense_weight, vectors, *(sums or [])],
            "mlp",
            7,
            limit=12,
            after=after,
        )

    def attend(r, near, far, cg_near, cg_far, after=()):
        big = pltpu.VMEM((slot_count, 256), BF16)
        tall = pltpu.VMEM((256, slot_count), BF16)
        total = pltpu.VMEM((slot_count, 256), F32)
        return call(
            functools.partial(attend_kernel, r),
            [shape(slot_count, 256), shape(slot_count, 768)],
            [lengths],
            [near, far, cg_near, cg_far, *tables],
            "attend",
            14,
            scratch=[big] * 4 + [tall] * 3 + [total] * 2,
            limit=12,
            after=after,
        )

    def close(r, ctx, jg, acts, us, sums, after=()):
        first = sums is None
        four = shape(4, block, width)
        half = 3 * HEAD
        if first:
            shapes = [four, four, shape(1024, width, dtype=F32), shape(3, width, dtype=F32)]
        else:
            shapes = [four, four, shape(half, width), shape(half + 16, width), shape(half, width), shape(half, width)]
            shapes.append(shape(8, width, dtype=F32))
        return call(
            functools.partial(close_kernel, r, first, phased),
            shapes,
            [lengths, row_weight],
            [own[r], mate[r], over[r], *cross[r], ctx, jg, *acts, *us, weight, dense_weight, down_weight, vectors, *(sums or [])],
            "close",
            0,
            limit=12,
            after=after,
        )

    hits = (tissues[:, None] == jnp.arange(TISSUES)[None, :]).astype(F32)
    counts = jnp.sum(hits * lengths[:, None].astype(F32), axis=0)[None, :]
    counts = counts + exchange(counts, "wide", bits[0])
    near_q0 = qkv(0, False)
    counts = gate(counts, [near_q0])
    counts = counts + exchange(counts, "wide", bits[1])
    near_q1 = qkv(1, False, [counts])
    for bit in bits[2:]:
        counts = counts + exchange(counts, "wide", bit)
    row_count = jnp.sum(hits * counts, axis=1)
    row_weight = rows_local * wide_count * slot_count / TISSUES / row_count
    over.append(exchange(gate(own[1], [near_q1]), "narrow", 1))
    a00, cg00, u00, *sums = mlp(0, False, None, False, [near_q1])
    a10, cg10, u10, *sums = mlp(1, False, sums, False)
    over[0] = gate(over[0], [sums[2]])
    cross[0] = [exchange(over[0][k], "narrow", 0) for k in range(2)]
    a01, cg01, u01, *sums = mlp(0, True, sums, False)
    far_q0 = qkv(0, True, [sums[2]])
    over[1] = gate(over[1], [far_q0])
    cross[1] = [exchange(over[1][k], "narrow", 0) for k in range(2)]
    a11, cg11, u11, u_keep, u_send, d_keep, d_send, mlp_sums = mlp(1, True, sums, True)

    def final(far, after=()):
        spec = pl.BlockSpec((1, block, width), lambda i: (i, 0, 0))
        return pl.pallas_call(
            final_kernel,
            grid=(rows_local,),
            out_shape=[
                shape(rows_local, block, width),
                shape(rows_local, block, width, dtype=F32),
                shape(8, LANES, dtype=F32),
            ],
            in_specs=[SMEM()] * 2 + [VMEM()] * 8 + [ANY()] * len(after),
            out_specs=[spec, spec, pl.BlockSpec((8, LANES), lambda i: (0, 0))],
            compiler_params=pltpu.CompilerParams(vmem_limit_bytes=12 * 1024 * 1024),
            cost_estimate=pl.CostEstimate(flops=int(2.5 * COST), bytes_accessed=0, transcendentals=0),
            name="final",
        )(lengths, row_weight, own[0], keep0, got0, own[1], keep1, got1, far, vectors, *after)

    def join(body, shapes, arrays, after=(), us=0):
        return call(body, shapes, [], arrays, body.__name__, WAIT.get(body.__name__, us), after=after)

    far_q1 = qkv(1, True, [mlp_sums])
    ctx0, jg0 = attend(0, near_q0, far_q0, cg00, cg01, [far_q1])
    quarter = width // 4
    part = quarter // 2
    if phased:
        u_keep, u_send, d_keep, d_send = join(
            join_1,
            [shape(quarter, width)] * 4,
            [u_keep, exchange(u_send, "wide", 0), d_keep, exchange(d_send, "wide", 1)],
            [ctx0],
        )
    ctx1, jg1 = attend(1, near_q1, far_q1, cg10, cg11, [ctx0, u_keep] if phased else [ctx0])
    if phased:
        (both,) = join(
            join_2,
            [shape(2, quarter, width)],
            [u_keep, exchange(u_send, "wide", 1), d_keep, exchange(d_send, "wide", 0)],
            [ctx1],
        )
        both_got = exchange(both, "wide", 2)
    send0, keep0, qg, close_sums = close(
        0, ctx0, jg0, (a00, a01), (u00, u01), None, [ctx1, both] if phased else [ctx1]
    )
    got0 = exchange(send0, "narrow", 0)
    send1, keep1, a_keep, a_send, b_keep, b_send, small = close(
        1, ctx1, jg1, (a10, a11), (u10, u11), [qg, close_sums, mlp_sums]
    )
    got1 = exchange(send1, "narrow", 0)
    if phased:
        tiny = shape(8, width, dtype=F32)
        a_keep, a_send, b_keep, b_send, small = join(
            last_1,
            [shape(part, width), shape(part + 16, width), shape(part, width), shape(part, width), tiny],
            [a_keep, exchange(a_send, "wide", 0), b_keep, exchange(b_send, "wide", 0), small],
        )
        u_part, d_part = join(join_3, [shape(quarter, width)] * 2, [both, both_got], [a_keep])
        far = join(join_far, [shape(4, block, width)], [keep0, got0, keep1, got1], [u_part])[0]
        far_got = exchange(far, "narrow", 1)
        last, small = join(
            last_2,
            [shape(quarter + 16, width), tiny],
            [a_keep, exchange(a_send, "wide", 1), b_keep, exchange(b_send, "wide", 1), small],
            [far],
        )
        last_got = exchange(last, "wide", 2)
        u_half, d_half = join(
            join_4,
            [shape(2 * quarter, width)] * 2,
            [u_part, exchange(u_part, "wide", 1), d_part, exchange(d_part, "wide", 0)],
            [last],
            us=10,
        )
        a_part, b_part, small = join(
            last_3, [shape(part, width), shape(part, width), tiny], [last, last_got, small], [u_half]
        )
        a_half, b_half = join(
            join_4,
            [shape(quarter, width)] * 2,
            [a_part, exchange(a_part, "wide", 1), b_part, exchange(b_part, "wide", 0)],
            us=20,
        )
        block_out, grad_tokens, sign = final(far_got, [a_half])
        up_grad, down_grad, sign = join(
            widen_kernel,
            [shape(width, inner, dtype=F32), shape(inner, width, dtype=F32), shape(8, LANES, dtype=F32)],
            [u_half, exchange(u_half, "wide", 0), d_half, exchange(d_half, "wide", 1)],
            [sign],
        )
        q_grad, dense_grad = join(
            last_kernel,
            [shape(9 * HEAD, width, dtype=F32), shape(3 * HEAD, width, dtype=F32)],
            [a_half, exchange(a_half, "wide", 0), b_half, exchange(b_half, "wide", 1)],
            [sign],
        )
    else:
        far = join(join_far, [shape(4, block, width)], [keep0, got0, keep1, got1])[0]
        far_got = exchange(far, "narrow", 1)
        block_out, grad_tokens, sign = final(far_got)

        def total(keep, send):
            return gather_back(scatter_sum(jnp.concatenate([keep, send]), "wide", bits), "wide", bits).astype(F32)

        up_grad, down_grad = total(u_keep, u_send), total(d_keep, d_send)
        a, b = total(a_keep, a_send[:quarter]), total(b_keep, b_send)
        q_grad, dense_grad = jnp.concatenate([a, b[:quarter]]), b[quarter:]
        for bit in bits:
            small = small + exchange(small, "wide", bit)

    share = width // narrow_count
    if phased:
        small = gate(small, [a_half])
    far_small = exchange(small, "narrow", 1)
    mate_small = exchange(small + far_small, "narrow", 0)
    line = shape(share, dtype=F32)
    gain_1, shift_1, gain_2, shift_2, q_bias_grad, up_bias_grad, dense_bias_grad, down_bias_grad = join(
        vector_kernel,
        [line, line, line, line, shape(9 * HEAD, dtype=F32), shape(inner, dtype=F32), line, line],
        [small, mate_small, far_small],
        [sign],
    )
    return (
        block_out,
        grad_tokens,
        gain_1,
        shift_1,
        q_grad.T,
        q_bias_grad,
        dense_grad,
        dense_bias_grad,
        gain_2,
        shift_2,
        up_grad,
        up_bias_grad,
        down_grad,
        down_bias_grad,
    )


def solution(mesh):
    placed = (
        P("wide", "narrow", None),
        P("wide"),
        P("wide"),
        P(),
        P(),
        P(None, "narrow"),
        P("narrow"),
        P("narrow", None),
        P(),
        P(),
        P(),
        P(None, "narrow"),
        P("narrow"),
        P("narrow", None),
        P(),
        P("wide", "narrow", None),
    )
    return jax.shard_map(
        shards,
        mesh=mesh,
        in_specs=placed,
        out_specs=(
            P("wide", "narrow", None),
            P("wide", "narrow", None),
            P("narrow"),
            P("narrow"),
            P(None, "narrow"),
            P("narrow"),
            P("narrow", None),
            P("narrow"),
            P("narrow"),
            P("narrow"),
            P(None, "narrow"),
            P("narrow"),
            P("narrow", None),
            P("narrow"),
        ),
        check_vma=False,
    )
```

```python
import functools
import math

import jax
import jax.numpy as jnp
import numpy as np
from jax import lax
from jax.experimental import pallas as pl
from jax.experimental.pallas import tpu as pltpu
from jax.sharding import PartitionSpec as P

HEAD = 64
ROT = 16
TISSUES = 8
LANES = 128
EPS = 1e-05
BIG = -1e30
F32 = jnp.float32
BF16 = jnp.bfloat16
ERF_P = 0.39
ERF_C = (
    0.2353254092560988,
    0.09138720671028266,
    0.6495624403330551,
    -0.6354040754153405,
    0.8866667192133076,
    -0.22753770177595345,
)

NN = (((1,), (0,)), ((), ()))
NT = (((1,), (1,)), ((), ()))
TN = (((0,), (0,)), ((), ()))


def mm(a, b, dims=NN):
    return lax.dot_general(a, b, dims, preferred_element_type=F32)


def norm_parts(tokens):
    values = tokens.astype(F32)
    centered = values - jnp.mean(values, axis=-1, keepdims=True)
    inverse = lax.rsqrt(jnp.mean(centered * centered, axis=-1, keepdims=True) + EPS)
    return centered * inverse, inverse


def gelu_pair(x):
    size = jnp.abs(x)
    t = 1.0 / (1.0 + (ERF_P * math.sqrt(0.5)) * size)
    bell = jnp.exp(-0.5 * (x * x))
    poly = jnp.full_like(x, 0.5 * ERF_C[-1])
    for c in ERF_C[-2::-1]:
        poly = poly * t + 0.5 * c
    tail = poly * t * bell
    phi = jnp.where(x < 0, tail, 1.0 - tail)
    return x * phi, phi + x * (bell * (1.0 / math.sqrt(2.0 * math.pi)))


def turn(x, cos_t, low_t, high_t, sign):
    up = pltpu.roll(x, LANES - ROT // 2, 1)
    down = pltpu.roll(x, ROT // 2, 1)
    return x * cos_t + sign * (up * low_t + down * high_t)


def place_two(c, first, second):
    a = jnp.where(c == 0, first, second)
    b = jnp.where(c == 0, second, first)
    return jnp.concatenate([a, b], axis=0)


def out_grad_of(probe, first_slot, length, weight):
    slot = first_slot + lax.broadcasted_iota(jnp.int32, (probe.shape[0], 1), 0)
    scale = jnp.where(slot < length, weight, 0.0)
    return (probe.astype(F32) * scale).astype(BF16)


def spot():
    place = lax.axis_index("narrow")
    return place % 2, place // 2


def wide_bits(phased):
    if not phased:
        return 0, 0, 0
    place = lax.axis_index("wide")
    return place % 2, (place // 2) % 2, place // 4


def put(bit, half, keep, send, value, *where):
    if isinstance(bit, int):
        (keep if bit == half else send)[where] = value
        return

    @pl.when(bit == half)
    def _():
        keep[where] = value

    @pl.when(bit != half)
    def _():
        send[where] = value


def high_low(values):
    high = values.astype(BF16)
    return jnp.concatenate([high, (values - high.astype(F32)).astype(BF16)], axis=0)


def back_together(pair):
    pair = pair.astype(F32)
    return pair[:8] + pair[8:]


def pack_kernel(tokens, probe, *rest):
    out = rest[-1]
    out[0] = tokens[...]
    out[1] = probe[...]


def prepare_kernel(weight, g1, b1, g2, b2, up_b, q_b, dense_b, down_b, weight_o, vectors_o):
    width = weight.shape[1]
    bias = q_b[...].reshape(1, q_b.shape[0])
    pieces = []
    for part in range(3):
        for h in range(3):
            at = (h * 3 + part) * HEAD
            weight_o[part * 256 + h * HEAD : part * 256 + h * HEAD + HEAD, :] = weight[at : at + HEAD, :]
            pieces.append(bias[:, at : at + HEAD])
        weight_o[part * 256 + 3 * HEAD : part * 256 + 256, :] = jnp.zeros((HEAD, width), BF16)
        pieces.append(jnp.zeros((1, HEAD), F32))
    for line, v in enumerate((g1, b1, g2, b2, up_b, None, dense_b, down_b)):
        vectors_o[line : line + 1] = jnp.concatenate(pieces, axis=1) if v is None else v[...].reshape(1, v.shape[0])


def pair_of(far, refs):
    return ((refs[0][...], refs[1][...]), refs[2:]) if far else ((refs[0][0], refs[0][1]), refs[1:])


def qkv_kernel(far, x0, *refs):
    x1, (weight, vectors, cos_t, low_t, high_t, *rest) = pair_of(far, refs)
    out = rest[-1]
    c, y = spot()
    half = 1 - y if far else y
    gain, shift, bias = vectors[0:1], vectors[1:2], vectors[5:6]
    tokens = place_two(c, x0[0], x1[0])
    rows = tokens.shape[0]
    xhat, _ = norm_parts(tokens)
    normed = (xhat * gain + shift).astype(BF16)
    spots = pl.ds(pl.multiple_of(half * rows, rows), rows)
    cos_b, low_b, high_b = cos_t[spots, :], low_t[spots, :], high_t[spots, :]
    for part in range(3):
        joined = mm(normed, weight[part * 256 : part * 256 + 256, :], NT)
        joined = joined + bias[:, part * 256 : part * 256 + 256]
        for pair in range(2):
            x = joined[:, pair * LANES : pair * LANES + LANES]
            if part < 2:
                x = turn(x, cos_b, low_b, high_b, 1.0)
            x = x.astype(BF16)
            if part == 0:
                x = x * jnp.asarray(1.0 / math.sqrt(HEAD), BF16)
            at = part * 256 + pair * LANES
            out[:, at : at + LANES] = x


def context_grad(grad, dense, out):
    out[:, : dense.shape[0]] = mm(grad, dense[...], NT).astype(BF16)
    out[:, dense.shape[0] :] = jnp.zeros((grad.shape[0], 256 - dense.shape[0]), BF16)


def mlp_kernel(row, far, first, last, phased, lengths, weights, x0, *refs):
    x1, (up, down, dense, vectors, *rest) = pair_of(far, refs)
    if first:
        ug_in = dg_in = sums_in = None
    else:
        ug_in, dg_in, sums_in = rest[:3]
    if last:
        active_o, hgrad_o, u_keep, u_send, d_keep, d_send, sums_o = rest[-7:]
        bit_u, bit_d, _ = wide_bits(phased)
    else:
        active_o, cgrad_o, u_o, ug_o, dg_o, sums_o = rest[-6:]
    c, y = spot()
    half = 1 - y if far else y
    length = lengths[row]
    gain, shift, up_b = vectors[2:3], vectors[3:4], vectors[4:5]
    tokens = place_two(c, x0[0], x1[0])
    probe = place_two(c, x0[1], x1[1])
    rows, width = tokens.shape
    grad = out_grad_of(probe, half * rows, length, weights[row])
    inner = up.shape[1]
    step = 256
    agrads = [mm(grad, down[0:step, :], NT)]
    xhat, _ = norm_parts(tokens)
    normed = (xhat * gain + shift).astype(BF16)
    hiddens = [mm(normed, up[:, 0:step])]
    if not last:
        context_grad(grad, dense, cgrad_o)
    total = None
    for at in range(0, inner, step):
        cols, after = slice(at, at + step), slice(at + step, at + 2 * step)
        if at + step < inner:
            hiddens.append(mm(normed, up[:, after]))
            agrads.append(mm(grad, down[after, :], NT))
        active, slope = gelu_pair(hiddens.pop(0) + up_b[:, cols])
        active = active.astype(BF16)
        active_o[:, cols] = active
        hgrad = (agrads.pop(0) * slope).astype(BF16)
        if last:
            hgrad_o[:, cols] = hgrad
        else:
            piece = mm(hgrad, up[:, cols], NT)
            total = piece if total is None else total + piece
        ug = mm(normed, hgrad, TN)
        dg = mm(active, grad, TN)
        us = jnp.sum(hgrad.astype(F32), axis=0, keepdims=True)
        if not first:
            ug = ug + ug_in[:, cols]
            dg = dg + dg_in[cols, :]
            us = us + sums_in[2:3, cols]
        if last:
            ug, dg = ug.astype(BF16), dg.astype(BF16)
            half = width // 2
            for h in range(2):
                put(bit_u, h, u_keep, u_send, ug[h * half : h * half + half], slice(None), cols)
            for top in range(at, at + step, 128):
                h, to = top // (inner // 2), top % (inner // 2)
                put(bit_d, h, d_keep, d_send, dg[top - at : top - at + 128], slice(to, to + 128))
        else:
            ug_o[:, cols] = ug
            dg_o[cols, :] = dg
        sums_o[2:3, cols] = us
    if last:
        for line in (0, 1, 3):
            sums_o[line : line + 1] = sums_in[line : line + 1]
        return
    u_o[...] = (total * gain).astype(u_o.dtype)
    gs = jnp.sum(total * xhat, axis=0, keepdims=True)
    ss = jnp.sum(total, axis=0, keepdims=True)
    os = jnp.sum(grad.astype(F32), axis=0, keepdims=True)
    if not first:
        gs, ss, os = gs + sums_in[0:1], ss + sums_in[1:2], os + sums_in[3:4]
    sums_o[0:1] = gs
    sums_o[1:2] = ss
    sums_o[3:4] = os


def input_kernel(row, lengths, weights, x0, *refs):
    x1, (up, dense, vectors, hgrad, sums, *rest) = pair_of(True, refs)
    cgrad_o, u_o, sums_o = rest[-3:]
    c, y = spot()
    tokens = place_two(c, x0[0], x1[0])
    probe = place_two(c, x0[1], x1[1])
    total = mm(hgrad[...], up[...], NT)
    grad = out_grad_of(probe, (1 - y) * tokens.shape[0], lengths[row], weights[row])
    context_grad(grad, dense, cgrad_o)
    xhat, _ = norm_parts(tokens)
    u_o[...] = (total * vectors[2:3]).astype(u_o.dtype)
    sums_o[0:1] = sums[0:1] + jnp.sum(total * xhat, axis=0, keepdims=True)
    sums_o[1:2] = sums[1:2] + jnp.sum(total, axis=0, keepdims=True)
    sums_o[2:3] = sums[2:3]
    sums_o[3:4] = sums[3:4] + jnp.sum(grad.astype(F32), axis=0, keepdims=True)


def attend_kernel(row, lengths, near, far, cg_near, cg_far, cos_t, low_t, high_t, *rest):
    ctx_o, jg_o, q_s, k_s, v_s, c_s, kt_s, vt_s, ct_s, dk_s, dv_s = rest[-11:]
    _, y = spot()
    length = lengths[row]
    half = near.shape[0]
    slots = 2 * half
    block = 256
    for source, cg, place in ((near, cg_near, y), (far, cg_far, 1 - y)):
        spots = pl.ds(pl.multiple_of(place * half, half), half)
        q_s[spots, :] = source[:, 0:256]
        k_s[spots, :] = source[:, 256:512]
        v_s[spots, :] = source[:, 512:768]
        c_s[spots, :] = cg[...]
    kt_s[...] = k_s[...].T
    vt_s[...] = v_s[...].T
    ct_s[...] = c_s[...].T
    heads, blocks = 3, slots // block
    least = slots * 5 // 8
    lane = lax.broadcasted_iota(jnp.int32, (block, LANES), 1)
    key = lax.broadcasted_iota(jnp.int32, (block, block), 0)
    below = key <= lax.broadcasted_iota(jnp.int32, (block, block), 1)

    def part(j):
        return slice(j * block, j * block + block)

    def places(h):
        pair = (h // 2) * LANES
        return slice(pair, pair + LANES), slice(h * HEAD, h * HEAD + HEAD)

    def products(i, h):
        lanes, _ = places(h)
        q, cg = q_s[part(i), lanes], c_s[part(i), lanes]
        if h < 2:
            mine = (lane < HEAD) if h == 0 else (lane >= HEAD)
            q = jnp.where(mine, q, jnp.zeros_like(q))
            cg = jnp.where(mine, cg, jnp.zeros_like(cg))
        scores = [mm(k_s[part(j), lanes], q, NT) for j in range(i + 1)]
        pgrad = [mm(v_s[part(j), lanes], cg, NT) for j in range(i + 1)]
        return q, cg, scores, pgrad

    def softmax(i, scores):
        for j in range(i + 1):
            allowed = below if j == i else None
            if (j + 1) * block > least:
                inside = key < length - j * block
                allowed = inside if allowed is None else allowed & inside
            if allowed is not None:
                scores[j] = jnp.where(allowed, scores[j], BIG)
        peak = jnp.max(functools.reduce(jnp.maximum, scores), axis=0, keepdims=True)
        raised = [jnp.exp(x - peak) for x in scores]
        scale = 1.0 / jnp.sum(functools.reduce(jnp.add, raised), axis=0, keepdims=True)
        probs = [x * scale for x in raised]
        return probs, [x.astype(BF16) for x in probs]

    def middle(i, h, probs, low, pgrad):
        _, lines = places(h)
        ctx = functools.reduce(jnp.add, [mm(vt_s[lines, part(j)], low[j]) for j in range(i + 1)])
        inner = jnp.sum(ct_s[lines, part(i)].astype(F32) * ctx, axis=0, keepdims=True)
        return ctx, [(p * (g - inner)).astype(BF16) for p, g in zip(probs, pgrad)]

    def gradients(i, h, q, cg, low, sgrad):
        lanes, lines = places(h)
        dq = functools.reduce(jnp.add, [mm(kt_s[lines, part(j)], sgrad[j]) for j in range(i + 1)])
        for j in range(i + 1):
            dk, dv = mm(sgrad[j], q), mm(low[j], cg)
            if i == blocks - 1 and h != 1:
                dk_s[part(j), lanes] = dk
                dv_s[part(j), lanes] = dv
            else:
                dk_s[part(j), lanes] += dk
                dv_s[part(j), lanes] += dv
        return dq

    def finish(i, pieces):
        rows = part(i)
        empty = jnp.zeros((256 - heads * HEAD, block), F32)
        ctx_o[rows, :] = jnp.concatenate([p[0] for p in pieces] + [empty], axis=0).T.astype(BF16)
        dq = jnp.concatenate([p[1] for p in pieces] + [empty], axis=0).T * (1.0 / math.sqrt(HEAD))
        for pair in range(2):
            lanes = slice(pair * LANES, pair * LANES + LANES)
            turned = turn(dq[:, lanes], cos_t[rows, :], low_t[rows, :], high_t[rows, :], -1.0)
            jg_o[rows, lanes] = turned.astype(BF16)
            turned = turn(dk_s[rows, lanes], cos_t[rows, :], low_t[rows, :], high_t[rows, :], -1.0)
            jg_o[rows, 256 + pair * LANES : 256 + pair * LANES + LANES] = turned.astype(BF16)
        jg_o[rows, 512:768] = dv_s[rows, :].astype(BF16)

    tasks = [(i, h) for i in range(blocks - 1, -1, -1) for h in range(heads)]
    pieces, waiting = [], None
    ahead = products(*tasks[0])
    for number in range(len(tasks) + 1):
        if number < len(tasks):
            i, h = tasks[number]
            q, cg, scores, pgrad = ahead
            if number + 1 < len(tasks):
                ahead = products(*tasks[number + 1])
            probs, low = softmax(i, scores)
        if waiting is not None:
            old_i, old_h, ctx, *rest = waiting
            pieces.append((ctx, gradients(old_i, old_h, *rest)))
            if old_h == heads - 1:
                finish(old_i, pieces)
                pieces = []
        if number < len(tasks):
            ctx, sgrad = middle(i, h, probs, low, pgrad)
            waiting = i, h, ctx, q, cg, low, sgrad


def close_kernel(row, first, phased, lengths, weights, x0, x1, x2, x3, x4, ctx, jg, act_n, act_f, u_n, u_f, weight, dense,
                 down, vectors, *rest):
    if first:
        qg_in = sg_in = mg_in = None
        send, keep, qg_o, sums_o = rest[-4:]
    else:
        qg_in, sg_in, mg_in = rest[:3]
        send, keep, a_keep, a_send, b_keep, b_send, sums_o = rest[-7:]
    c, y = spot()
    length = lengths[row]
    gain, shift = vectors[0:1], vectors[1:2]
    block = x0.shape[1]
    gs = ss = bs = qg = dg = None
    for x, act, u, side, slot, out, at in (
        (x2, act_f, u_f, 1 - y, c, keep, 0),
        ((x3, x4), act_f, u_f, 1 - y, 1 - c, send, 0),
        (x0, act_n, u_n, y, c, keep, 2),
        (x1, act_n, u_n, y, 1 - c, send, 2),
    ):
        place = 2 * side + slot
        whole = pl.ds(pl.multiple_of(place * block, block), block)
        part = pl.ds(pl.multiple_of(slot * block, block), block)
        context, joined = ctx[whole, :], jg[whole, :]
        out[at] = (mm(context[:, : dense.shape[0]], dense[...]) + mm(act[part, :], down[...])).astype(BF16)
        first_grad = mm(joined, weight[...])
        xhat, _ = norm_parts(x[0][...])
        normed = (xhat * gain + shift).astype(BF16)
        grad = out_grad_of(x[1][...], place * block, length, weights[row])
        out[at + 1] = (first_grad * gain + u[part, :].astype(F32)).astype(BF16)
        pieces = (
            jnp.sum(first_grad * xhat, axis=0, keepdims=True),
            jnp.sum(first_grad, axis=0, keepdims=True),
            jnp.sum(joined.astype(F32), axis=0, keepdims=True),
            mm(joined, normed, TN),
            mm(context, grad, TN),
        )
        if gs is None:
            gs, ss, bs, qg, dg = pieces
        else:
            gs, ss, bs, qg, dg = (a + b for a, b in zip((gs, ss, bs, qg, dg), pieces))
    if first:
        qg_o[0:768] = qg
        qg_o[768:1024] = dg
        sums_o[0:1] = gs
        sums_o[1:2] = ss
        sums_o[2:3] = bs
        return
    bit_a = bit_b = wide_bits(phased)[0]
    half = a_keep.shape[0]
    for h in range(3):
        for part in range(3):
            at, to = part * 256 + h * HEAD, (h * 3 + part) * HEAD
            value = (qg[at : at + HEAD] + qg_in[at : at + HEAD]).astype(BF16)
            number, to = to // half, to % half
            if number < 2:
                put(bit_a, number, a_keep, a_send, value, slice(to, to + HEAD))
            else:
                put(bit_b, 0, b_keep, b_send, value, slice(to, to + HEAD))
    value = (dg[0:half] + qg_in[768 : 768 + half]).astype(BF16)
    put(bit_b, 1, b_keep, b_send, value, slice(None))
    small = jnp.concatenate(
        [
            gs + sg_in[0:1],
            ss + sg_in[1:2],
            mg_in[0:2],
            bs + sg_in[2:3],
            mg_in[2:4],
            jnp.zeros_like(gs),
        ],
        axis=0,
    )
    sums_o[...] = small
    a_send[half : half + 16] = high_low(small)


def plus(a, b):
    return (a.astype(F32) + b.astype(F32)).astype(BF16)


def rows_of(number, size):
    return pl.ds(pl.multiple_of(number * size, size), size)


def join_1(u_keep, u_got, d_keep, d_got, *rest):
    u_keep_o, u_send_o, d_keep_o, d_send_o = rest[-4:]
    x, z, _ = wide_bits(True)
    size = u_keep_o.shape[0]
    for keep, got, bit, keep_o, send_o in ((u_keep, u_got, z, u_keep_o, u_send_o), (d_keep, d_got, x, d_keep_o, d_send_o)):
        mine, other = rows_of(bit, size), rows_of(1 - bit, size)
        send_o[...] = plus(keep[other, :], got[other, :])
        keep_o[...] = plus(keep[mine, :], got[mine, :])


def join_2(u_keep, u_got, d_keep, d_got, *rest):
    both = rest[-1]
    both[0] = plus(u_keep[...], u_got[...])
    both[1] = plus(d_keep[...], d_got[...])


def join_far(keep0, got0, keep1, got1, *rest):
    out = rest[-1]
    out[0:2] = plus(keep0[0:2], got0[0:2])
    out[2:4] = plus(keep1[0:2], got1[0:2])


def join_3(both, both_got, *rest):
    u_o, d_o = rest[-2:]
    u_o[...] = plus(both[0], both_got[0])
    d_o[...] = plus(both[1], both_got[1])


def join_4(u, u_got, d, d_got, *rest):
    u_o, d_o = rest[-2:]
    x, z, _ = wide_bits(True)
    size = u.shape[0]
    for own, got, bit, out in ((u, u_got, z, u_o), (d, d_got, x, d_o)):
        out[rows_of(bit, size), :] = own[...]
        out[rows_of(1 - bit, size), :] = got[...]


def last_1(a_keep, a_got, b_keep, b_got, small, *rest):
    a_keep_o, a_send_o, b_keep_o, b_send_o, small_o = rest[-5:]
    x, z, _ = wide_bits(True)
    part = a_keep_o.shape[0]
    for keep, got, bit, keep_o, send_o in ((a_keep, a_got, z, a_keep_o, a_send_o), (b_keep, b_got, z, b_keep_o, b_send_o)):
        mine, other = rows_of(bit, part), rows_of(1 - bit, part)
        send_o[0:part] = plus(keep[other, :], got[other, :])
        keep_o[...] = plus(keep[mine, :], got[mine, :])
    total = small[...] + back_together(a_got[2 * part : 2 * part + 16])
    small_o[...] = total
    a_send_o[part : part + 16] = high_low(total)


def last_2(a_keep, a_got, b_keep, b_got, small, *rest):
    last_o, small_o = rest[-2:]
    part = a_keep.shape[0]
    last_o[0:part] = plus(a_keep[...], a_got[0:part])
    last_o[part : 2 * part] = plus(b_keep[...], b_got[...])
    total = small[...] + back_together(a_got[part : part + 16])
    small_o[...] = total
    last_o[2 * part : 2 * part + 16] = high_low(total)


def last_3(last, last_got, small, *rest):
    a_o, b_o, small_o = rest[-3:]
    part = a_o.shape[0]
    a_o[...] = plus(last[0:part], last_got[0:part])
    b_o[...] = plus(last[part : 2 * part], last_got[part : 2 * part])
    small_o[...] = small[...] + back_together(last_got[2 * part : 2 * part + 16])


def widen_kernel(u, u_got, d, d_got, *rest):
    u_o, d_o, sign = rest[-3:]
    sign[...] = jnp.zeros_like(sign)
    x, z, _ = wide_bits(True)
    half = u.shape[0]
    for own, got, bit, out in ((u, u_got, x, u_o), (d, d_got, z, d_o)):
        out[rows_of(bit, half), :] = own[...].astype(F32)
        out[rows_of(1 - bit, half), :] = got[...].astype(F32)


def last_kernel(a, a_got, b, b_got, *rest):
    q_o, dense_o = rest[-2:]
    x, z, _ = wide_bits(True)
    half = a.shape[0]
    part = half // 2
    q_o[rows_of(x, half), :] = a[...].astype(F32)
    q_o[rows_of(1 - x, half), :] = a_got[...].astype(F32)
    for own, place in ((b, z), (b_got, 1 - z)):
        q_o[rows_of(4 + place, part), :] = own[0:part].astype(F32)
        dense_o[rows_of(place, part), :] = own[part:half].astype(F32)


def final_kernel(lengths, weights, own0, keep0, got0, own1, keep1, got1, far, vectors, *rest):
    block_o, grad_o, sign = rest[-3:]
    sign[...] = jnp.zeros_like(sign)
    block = own0.shape[1]
    slot = lax.axis_index("narrow") * block + lax.broadcasted_iota(jnp.int32, (block, 1), 0)
    for row, (own, keep, got) in enumerate(((own0, keep0, got0), (own1, keep1, got1))):

        @pl.when(pl.program_id(0) == row)
        def _():
            near = keep[2:4].astype(F32) + got[2:4].astype(F32) + far[2 * row : 2 * row + 2].astype(F32)
            values = own[0].astype(F32)
            block_o[0] = (values + (near[0] + vectors[6:7] + vectors[7:8])).astype(BF16)
            xhat, inverse = norm_parts(own[0])
            u = near[1]
            scale = jnp.where(slot < lengths[row], weights[row], 0.0)
            mean = jnp.mean(u, axis=-1, keepdims=True)
            lean = jnp.mean(u * xhat, axis=-1, keepdims=True)
            grad_o[0] = own[1].astype(F32) * scale + inverse * (u - mean - xhat * lean)


def vector_kernel(small, mate, far, *rest):
    outs = rest[-8:]
    place = lax.axis_index("narrow")
    total = small[...] + mate[...] + far[...]
    own = small[...]
    share = outs[0].shape[0]
    for number in range(small.shape[1] // share):

        @pl.when(place == number)
        def _():
            at = number * share
            for line in range(4):
                outs[line][...] = total[line : line + 1, at : at + share].reshape(share)
            for out in outs[6:8]:
                out[...] = own[6:7, at : at + share].reshape(share)

    pieces = [own[4:5, part * 256 + h * HEAD : part * 256 + h * HEAD + HEAD] for h in range(3) for part in range(3)]
    outs[4][...] = jnp.concatenate(pieces, axis=1).reshape(9 * HEAD)
    outs[5][...] = own[5:6].reshape(own.shape[1])


SMEM = functools.partial(pl.BlockSpec, memory_space=pltpu.SMEM)
VMEM = functools.partial(pl.BlockSpec, memory_space=pltpu.VMEM)
ANY = functools.partial(pl.BlockSpec, memory_space=pl.ANY)
HBM = functools.partial(pl.BlockSpec, memory_space=pltpu.HBM)
COST = 1e8
WAIT = {'join_1': 200, 'join_2': 200, 'join_3': 200, 'join_far': 200}


def call(body, outs, scalars, arrays, name, us, scratch=(), limit=8, after=()):
    return pl.pallas_call(
        body,
        out_shape=outs,
        in_specs=[SMEM()] * len(scalars) + [VMEM()] * len(arrays) + [ANY()] * len(after),
        out_specs=[VMEM()] * len(outs),
        scratch_shapes=list(scratch),
        compiler_params=pltpu.CompilerParams(vmem_limit_bytes=limit * 1024 * 1024),
        cost_estimate=pl.CostEstimate(flops=int(us * COST), bytes_accessed=0, transcendentals=0),
        name=name,
    )(*scalars, *arrays, *after)


def exchange(x, axis, bit):
    size = lax.axis_size(axis)
    return lax.ppermute(x, axis, [(i, i ^ (1 << bit)) for i in range(size)])


def add_low(a, b):
    return (a.astype(F32) + b.astype(F32)).astype(BF16)


def scatter_sum(x, axis, bits):
    place = lax.axis_index(axis)
    for bit in bits:
        half = x.shape[0] // 2
        mine = (place >> bit) & 1
        keep = lax.dynamic_slice_in_dim(x, mine * half, half, 0)
        send = lax.dynamic_slice_in_dim(x, (1 - mine) * half, half, 0)
        x = add_low(keep, exchange(send, axis, bit))
    return x


def gather_back(x, axis, bits):
    place = lax.axis_index(axis)
    for bit in reversed(bits):
        mine = (place >> bit) & 1
        got = exchange(x, axis, bit)
        x = jnp.where(mine == 0, jnp.concatenate([x, got]), jnp.concatenate([got, x]))
    return x


def rotary(slot_count):
    position = np.arange(slot_count, dtype=np.float64)
    frequency = 10000.0 ** (-(2.0 * np.arange(ROT // 2)) / ROT)
    angles = position[:, None] * frequency[None, :]
    cos, sin = np.cos(angles), np.sin(angles)
    none8, none = np.zeros_like(sin), np.zeros((slot_count, HEAD - ROT))
    cos_t = np.concatenate([cos, cos, none + 1.0], axis=1)
    low_t = np.concatenate([-sin, none8, none], axis=1)
    high_t = np.concatenate([none8, sin, none], axis=1)
    return tuple(jnp.asarray(np.concatenate([t, t], axis=1), F32) for t in (cos_t, low_t, high_t))


def shards(tokens, lengths, tissues, ln1_gain, ln1_bias, qkv_weight, qkv_bias, dense_weight, dense_bias,
           ln2_gain, ln2_bias, up_weight, up_bias, down_weight, down_bias, out_probe):
    rows_local, block, width = tokens.shape
    inner = up_weight.shape[1]
    wide_count, narrow_count = lax.axis_size("wide"), lax.axis_size("narrow")
    place = lax.axis_index("narrow")
    slot_count = block * narrow_count
    bits = list(range(wide_count.bit_length() - 1))
    half_rows = 2 * block
    phased = wide_count == 8

    def shape(*dims, dtype=BF16):
        return jax.ShapeDtypeStruct(dims, dtype)

    def pack(r, after=()):
        return call(pack_kernel, [shape(2, block, width)], [], [tokens[r], out_probe[r]], "pack", 0, after=after)[0]

    def gate(x, after):
        return pl.pallas_call(
            lambda *refs: None,
            out_shape=jax.ShapeDtypeStruct(x.shape, x.dtype),
            in_specs=[ANY()] * (1 + len(after)),
            out_specs=ANY(),
            input_output_aliases={0: 0},
            compiler_params=pltpu.CompilerParams(vmem_limit_bytes=1024 * 1024),
            name="gate",
        )(x, *after)

    own = [pack(0)]
    own.append(pack(1, own))
    over = [exchange(own[0], "narrow", 1)]
    mate = [exchange(x, "narrow", 0) for x in own]
    cross = [None, None]

    tables = rotary(slot_count)
    weight, vectors = call(
        prepare_kernel,
        [shape(768, width), shape(8, width, dtype=F32)],
        [],
        [qkv_weight.T, ln1_gain, ln1_bias, ln2_gain, ln2_bias, up_bias, qkv_bias, dense_bias, down_bias],
        "prepare",
        1,
    )

    def qkv(r, far, after=()):
        units = [over[r], *cross[r]] if far else [own[r], mate[r]]
        return call(
            functools.partial(qkv_kernel, far),
            [shape(half_rows, 768)],
            [],
            [*units, weight, vectors, *tables],
            "qkv",
            3,
            limit=8,
            after=after,
        )[0]

    def mlp(r, far, sums, last, after=()):
        units = [over[r], *cross[r]] if far else [own[r], mate[r]]
        first = sums is None
        return call(
            functools.partial(mlp_kernel, r, far, first, last, phased),
            [
                shape(half_rows, inner),
                *([shape(half_rows, inner)] if last else [shape(half_rows, 256), shape(half_rows, width)]),
                *([shape(width // 2, inner)] * 2 if last else [shape(width, inner, dtype=F32)]),
                *([shape(inner // 2, width)] * 2 if last else [shape(inner, width, dtype=F32)]),
                shape(4, width, dtype=F32),
            ],
            [lengths, row_weight],
            [*units, up_weight, down_weight, dense_weight, vectors, *(sums or [])],
            "mlp",
            7,
            limit=12,
            after=after,
        )

    def attend(r, near, far, cg_near, cg_far, after=()):
        big = pltpu.VMEM((slot_count, 256), BF16)
        tall = pltpu.VMEM((256, slot_count), BF16)
        total = pltpu.VMEM((slot_count, 256), F32)
        return call(
            functools.partial(attend_kernel, r),
            [shape(slot_count, 256), shape(slot_count, 768)],
            [lengths],
            [near, far, cg_near, cg_far, *tables],
            "attend",
            14,
            scratch=[big] * 4 + [tall] * 3 + [total] * 2,
            limit=12,
            after=after,
        )

    def close(r, ctx, jg, acts, us, sums, after=()):
        first = sums is None
        four = shape(4, block, width)
        half = 3 * HEAD
        if first:
            shapes = [four, four, shape(1024, width, dtype=F32), shape(3, width, dtype=F32)]
        else:
            shapes = [four, four, shape(half, width), shape(half + 16, width), shape(half, width), shape(half, width)]
            shapes.append(shape(8, width, dtype=F32))
        return call(
            functools.partial(close_kernel, r, first, phased),
            shapes,
            [lengths, row_weight],
            [own[r], mate[r], over[r], *cross[r], ctx, jg, *acts, *us, weight, dense_weight, down_weight, vectors, *(sums or [])],
            "close",
            0,
            limit=12,
            after=after,
        )

    hits = (tissues[:, None] == jnp.arange(TISSUES)[None, :]).astype(F32)
    counts = jnp.sum(hits * lengths[:, None].astype(F32), axis=0)[None, :]
    counts = counts + exchange(counts, "wide", bits[0])
    near_q0 = qkv(0, False)
    counts = gate(counts, [near_q0])
    counts = counts + exchange(counts, "wide", bits[1])
    near_q1 = qkv(1, False, [counts])
    for bit in bits[2:]:
        counts = counts + exchange(counts, "wide", bit)
    row_count = jnp.sum(hits * counts, axis=1)
    row_weight = rows_local * wide_count * slot_count / TISSUES / row_count
    over.append(exchange(gate(own[1], [near_q1]), "narrow", 1))
    a00, cg00, u00, *sums = mlp(0, False, None, False, [near_q1])
    a10, cg10, u10, *sums = mlp(1, False, sums, False)
    over[0] = gate(over[0], [sums[2]])
    cross[0] = [exchange(over[0][k], "narrow", 0) for k in range(2)]
    a01, cg01, u01, *sums = mlp(0, True, sums, False)
    far_q0 = qkv(0, True, [sums[2]])
    over[1] = gate(over[1], [far_q0])
    cross[1] = [exchange(over[1][k], "narrow", 0) for k in range(2)]
    a11, hgrad, u_keep, u_send, d_keep, d_send, mlp_sums = mlp(1, True, sums, True)

    def final(far, after=()):
        spec = pl.BlockSpec((1, block, width), lambda i: (i, 0, 0))
        return pl.pallas_call(
            final_kernel,
            grid=(rows_local,),
            out_shape=[
                shape(rows_local, block, width),
                shape(rows_local, block, width, dtype=F32),
                shape(8, LANES, dtype=F32),
            ],
            in_specs=[SMEM()] * 2 + [VMEM()] * 8 + [ANY()] * len(after),
            out_specs=[spec, spec, pl.BlockSpec((8, LANES), lambda i: (0, 0))],
            compiler_params=pltpu.CompilerParams(vmem_limit_bytes=12 * 1024 * 1024),
            cost_estimate=pl.CostEstimate(flops=int(2.5 * COST), bytes_accessed=0, transcendentals=0),
            name="final",
        )(lengths, row_weight, own[0], keep0, got0, own[1], keep1, got1, far, vectors, *after)

    def join(body, shapes, arrays, after=(), us=0):
        return call(body, shapes, [], arrays, body.__name__, WAIT.get(body.__name__, us), after=after)

    far_q1 = qkv(1, True, [mlp_sums])
    cg11, u11, mlp_sums = call(
        functools.partial(input_kernel, 1),
        [shape(half_rows, 256), shape(half_rows, width), shape(4, width, dtype=F32)],
        [lengths, row_weight],
        [over[1], *cross[1], up_weight, dense_weight, vectors, hgrad, mlp_sums],
        "inputs",
        2,
        limit=12,
        after=[far_q1],
    )
    ctx0, jg0 = attend(0, near_q0, far_q0, cg00, cg01, [mlp_sums])
    quarter = width // 4
    part = quarter // 2
    if phased:
        u_keep, u_send, d_keep, d_send = join(
            join_1,
            [shape(quarter, width)] * 4,
            [u_keep, exchange(u_send, "wide", 0), d_keep, exchange(d_send, "wide", 1)],
            [ctx0],
        )
    ctx1, jg1 = attend(1, near_q1, far_q1, cg10, cg11, [ctx0, u_keep] if phased else [ctx0])
    if phased:
        (both,) = join(
            join_2,
            [shape(2, quarter, width)],
            [u_keep, exchange(u_send, "wide", 1), d_keep, exchange(d_send, "wide", 0)],
            [ctx1],
        )
        both_got = exchange(both, "wide", 2)
    send0, keep0, qg, close_sums = close(
        0, ctx0, jg0, (a00, a01), (u00, u01), None, [ctx1, both] if phased else [ctx1]
    )
    got0 = exchange(send0, "narrow", 0)
    send1, keep1, a_keep, a_send, b_keep, b_send, small = close(
        1, ctx1, jg1, (a10, a11), (u10, u11), [qg, close_sums, mlp_sums]
    )
    got1 = exchange(send1, "narrow", 0)
    if phased:
        tiny = shape(8, width, dtype=F32)
        a_keep, a_send, b_keep, b_send, small = join(
            last_1,
            [shape(part, width), shape(part + 16, width), shape(part, width), shape(part, width), tiny],
            [a_keep, exchange(a_send, "wide", 0), b_keep, exchange(b_send, "wide", 0), small],
        )
        u_part, d_part = join(join_3, [shape(quarter, width)] * 2, [both, both_got], [a_keep])
        far = join(join_far, [shape(4, block, width)], [keep0, got0, keep1, got1], [u_part])[0]
        far_got = exchange(far, "narrow", 1)
        last, small = join(
            last_2,
            [shape(quarter + 16, width), tiny],
            [a_keep, exchange(a_send, "wide", 1), b_keep, exchange(b_send, "wide", 1), small],
            [far],
        )
        last_got = exchange(last, "wide", 2)
        u_half, d_half = join(
            join_4,
            [shape(2 * quarter, width)] * 2,
            [u_part, exchange(u_part, "wide", 1), d_part, exchange(d_part, "wide", 0)],
            [last],
            us=10,
        )
        a_part, b_part, small = join(
            last_3, [shape(part, width), shape(part, width), tiny], [last, last_got, small], [u_half]
        )
        a_half, b_half = join(
            join_4,
            [shape(quarter, width)] * 2,
            [a_part, exchange(a_part, "wide", 1), b_part, exchange(b_part, "wide", 0)],
            us=20,
        )
        block_out, grad_tokens, sign = final(far_got, [a_half])
        up_grad, down_grad, sign = join(
            widen_kernel,
            [shape(width, inner, dtype=F32), shape(inner, width, dtype=F32), shape(8, LANES, dtype=F32)],
            [u_half, exchange(u_half, "wide", 0), d_half, exchange(d_half, "wide", 1)],
            [sign],
        )
        q_grad, dense_grad = join(
            last_kernel,
            [shape(9 * HEAD, width, dtype=F32), shape(3 * HEAD, width, dtype=F32)],
            [a_half, exchange(a_half, "wide", 0), b_half, exchange(b_half, "wide", 1)],
            [sign],
        )
    else:
        far = join(join_far, [shape(4, block, width)], [keep0, got0, keep1, got1])[0]
        far_got = exchange(far, "narrow", 1)
        block_out, grad_tokens, sign = final(far_got)

        def total(keep, send):
            return gather_back(scatter_sum(jnp.concatenate([keep, send]), "wide", bits), "wide", bits).astype(F32)

        up_grad, down_grad = total(u_keep, u_send), total(d_keep, d_send)
        a, b = total(a_keep, a_send[:quarter]), total(b_keep, b_send)
        q_grad, dense_grad = jnp.concatenate([a, b[:quarter]]), b[quarter:]
        for bit in bits:
            small = small + exchange(small, "wide", bit)

    share = width // narrow_count
    if phased:
        small = gate(small, [a_half])
    far_small = exchange(small, "narrow", 1)
    mate_small = exchange(small + far_small, "narrow", 0)
    line = shape(share, dtype=F32)
    gain_1, shift_1, gain_2, shift_2, q_bias_grad, up_bias_grad, dense_bias_grad, down_bias_grad = join(
        vector_kernel,
        [line, line, line, line, shape(9 * HEAD, dtype=F32), shape(inner, dtype=F32), line, line],
        [small, mate_small, far_small],
        [sign],
    )
    return (
        block_out,
        grad_tokens,
        gain_1,
        shift_1,
        q_grad.T,
        q_bias_grad,
        dense_grad,
        dense_bias_grad,
        gain_2,
        shift_2,
        up_grad,
        up_bias_grad,
        down_grad,
        down_bias_grad,
    )


def solution(mesh):
    placed = (
        P("wide", "narrow", None),
        P("wide"),
        P("wide"),
        P(),
        P(),
        P(None, "narrow"),
        P("narrow"),
        P("narrow", None),
        P(),
        P(),
        P(),
        P(None, "narrow"),
        P("narrow"),
        P("narrow", None),
        P(),
        P("wide", "narrow", None),
    )
    return jax.shard_map(
        shards,
        mesh=mesh,
        in_specs=placed,
        out_specs=(
            P("wide", "narrow", None),
            P("wide", "narrow", None),
            P("narrow"),
            P("narrow"),
            P(None, "narrow"),
            P("narrow"),
            P("narrow", None),
            P("narrow"),
            P("narrow"),
            P("narrow"),
            P(None, "narrow"),
            P("narrow"),
            P("narrow", None),
            P("narrow"),
        ),
        check_vma=False,
    )
```

```python
import functools
import math

import jax
import jax.numpy as jnp
import numpy as np
from jax import lax
from jax.experimental import pallas as pl
from jax.experimental.pallas import tpu as pltpu
from jax.sharding import PartitionSpec as P

HEAD = 64
ROT = 16
TISSUES = 8
LANES = 128
EPS = 1e-05
BIG = -1e30
F32 = jnp.float32
BF16 = jnp.bfloat16
ERF_P = 0.39
ERF_C = (
    0.2353254092560988,
    0.09138720671028266,
    0.6495624403330551,
    -0.6354040754153405,
    0.8866667192133076,
    -0.22753770177595345,
)

NN = (((1,), (0,)), ((), ()))
NT = (((1,), (1,)), ((), ()))
TN = (((0,), (0,)), ((), ()))


def mm(a, b, dims=NN):
    return lax.dot_general(a, b, dims, preferred_element_type=F32)


def norm_parts(tokens):
    values = tokens.astype(F32)
    centered = values - jnp.mean(values, axis=-1, keepdims=True)
    inverse = lax.rsqrt(jnp.mean(centered * centered, axis=-1, keepdims=True) + EPS)
    return centered * inverse, inverse


def gelu_pair(x):
    size = jnp.abs(x)
    t = 1.0 / (1.0 + (ERF_P * math.sqrt(0.5)) * size)
    bell = jnp.exp(-0.5 * (x * x))
    poly = jnp.full_like(x, 0.5 * ERF_C[-1])
    for c in ERF_C[-2::-1]:
        poly = poly * t + 0.5 * c
    tail = poly * t * bell
    phi = jnp.where(x < 0, tail, 1.0 - tail)
    return x * phi, phi + x * (bell * (1.0 / math.sqrt(2.0 * math.pi)))


def turn(x, cos_t, low_t, high_t, sign):
    up = pltpu.roll(x, LANES - ROT // 2, 1)
    down = pltpu.roll(x, ROT // 2, 1)
    return x * cos_t + sign * (up * low_t + down * high_t)


def place_two(c, first, second):
    a = jnp.where(c == 0, first, second)
    b = jnp.where(c == 0, second, first)
    return jnp.concatenate([a, b], axis=0)


def out_grad_of(probe, first_slot, length, weight):
    slot = first_slot + lax.broadcasted_iota(jnp.int32, (probe.shape[0], 1), 0)
    scale = jnp.where(slot < length, weight, 0.0)
    return (probe.astype(F32) * scale).astype(BF16)


def spot():
    place = lax.axis_index("narrow")
    return place % 2, place // 2


def wide_bits(phased):
    if not phased:
        return 0, 0, 0
    place = lax.axis_index("wide")
    return place % 2, (place // 2) % 2, place // 4


def put(bit, half, keep, send, value, *where):
    if isinstance(bit, int):
        (keep if bit == half else send)[where] = value
        return

    @pl.when(bit == half)
    def _():
        keep[where] = value

    @pl.when(bit != half)
    def _():
        send[where] = value


def high_low(values):
    high = values.astype(BF16)
    return jnp.concatenate([high, (values - high.astype(F32)).astype(BF16)], axis=0)


def back_together(pair):
    pair = pair.astype(F32)
    return pair[:8] + pair[8:]


def pack_kernel(tokens, probe, *rest):
    out = rest[-1]
    out[0] = tokens[...]
    out[1] = probe[...]


def prepare_kernel(weight, g1, b1, g2, b2, up_b, q_b, dense_b, down_b, weight_o, vectors_o):
    width = weight.shape[1]
    bias = q_b[...].reshape(1, q_b.shape[0])
    pieces = []
    for part in range(3):
        for h in range(3):
            at = (h * 3 + part) * HEAD
            weight_o[part * 256 + h * HEAD : part * 256 + h * HEAD + HEAD, :] = weight[at : at + HEAD, :]
            pieces.append(bias[:, at : at + HEAD])
        weight_o[part * 256 + 3 * HEAD : part * 256 + 256, :] = jnp.zeros((HEAD, width), BF16)
        pieces.append(jnp.zeros((1, HEAD), F32))
    for line, v in enumerate((g1, b1, g2, b2, up_b, None, dense_b, down_b)):
        vectors_o[line : line + 1] = jnp.concatenate(pieces, axis=1) if v is None else v[...].reshape(1, v.shape[0])


def pair_of(far, refs):
    return ((refs[0][...], refs[1][...]), refs[2:]) if far else ((refs[0][0], refs[0][1]), refs[1:])


def qkv_kernel(far, x0, *refs):
    x1, (weight, vectors, cos_t, low_t, high_t, *rest) = pair_of(far, refs)
    out = rest[-1]
    c, y = spot()
    half = 1 - y if far else y
    gain, shift, bias = vectors[0:1], vectors[1:2], vectors[5:6]
    tokens = place_two(c, x0[0], x1[0])
    rows = tokens.shape[0]
    xhat, _ = norm_parts(tokens)
    normed = (xhat * gain + shift).astype(BF16)
    spots = pl.ds(pl.multiple_of(half * rows, rows), rows)
    cos_b, low_b, high_b = cos_t[spots, :], low_t[spots, :], high_t[spots, :]
    for part in range(3):
        joined = mm(normed, weight[part * 256 : part * 256 + 256, :], NT)
        joined = joined + bias[:, part * 256 : part * 256 + 256]
        for pair in range(2):
            x = joined[:, pair * LANES : pair * LANES + LANES]
            if part < 2:
                x = turn(x, cos_b, low_b, high_b, 1.0)
            x = x.astype(BF16)
            if part == 0:
                x = x * jnp.asarray(1.0 / math.sqrt(HEAD), BF16)
            at = part * 256 + pair * LANES
            out[:, at : at + LANES] = x


def context_grad(grad, dense, out):
    out[:, : dense.shape[0]] = mm(grad, dense[...], NT).astype(BF16)
    out[:, dense.shape[0] :] = jnp.zeros((grad.shape[0], 256 - dense.shape[0]), BF16)


def mlp_kernel(row, far, first, last, phased, lengths, weights, x0, *refs):
    x1, (up, down, dense, vectors, *rest) = pair_of(far, refs)
    if first:
        ug_in = dg_in = sums_in = None
    else:
        ug_in, dg_in, sums_in = rest[:3]
    if last:
        active_o, hgrad_o, u_keep, u_send, d_keep, d_send, sums_o = rest[-7:]
        bit_u, bit_d, _ = wide_bits(phased)
    else:
        active_o, cgrad_o, u_o, ug_o, dg_o, sums_o = rest[-6:]
    c, y = spot()
    half = 1 - y if far else y
    length = lengths[row]
    gain, shift, up_b = vectors[2:3], vectors[3:4], vectors[4:5]
    tokens = place_two(c, x0[0], x1[0])
    probe = place_two(c, x0[1], x1[1])
    rows, width = tokens.shape
    grad = out_grad_of(probe, half * rows, length, weights[row])
    inner = up.shape[1]
    step = 256
    agrads = [mm(grad, down[0:step, :], NT)]
    xhat, _ = norm_parts(tokens)
    normed = (xhat * gain + shift).astype(BF16)
    hiddens = [mm(normed, up[:, 0:step])]
    if not last:
        context_grad(grad, dense, cgrad_o)
    total = None
    for at in range(0, inner, step):
        cols, after = slice(at, at + step), slice(at + step, at + 2 * step)
        if at + step < inner:
            hiddens.append(mm(normed, up[:, after]))
            agrads.append(mm(grad, down[after, :], NT))
        active, slope = gelu_pair(hiddens.pop(0) + up_b[:, cols])
        active = active.astype(BF16)
        active_o[:, cols] = active
        hgrad = (agrads.pop(0) * slope).astype(BF16)
        if last:
            hgrad_o[:, cols] = hgrad
        else:
            piece = mm(hgrad, up[:, cols], NT)
            total = piece if total is None else total + piece
        ug = mm(normed, hgrad, TN)
        dg = mm(active, grad, TN)
        us = jnp.sum(hgrad.astype(F32), axis=0, keepdims=True)
        if not first:
            ug = ug + ug_in[:, cols]
            dg = dg + dg_in[cols, :]
            us = us + sums_in[2:3, cols]
        if last:
            ug, dg = ug.astype(BF16), dg.astype(BF16)
            half = width // 2
            for h in range(2):
                put(bit_u, h, u_keep, u_send, ug[h * half : h * half + half], slice(None), cols)
            for top in range(at, at + step, 128):
                h, to = top // (inner // 2), top % (inner // 2)
                put(bit_d, h, d_keep, d_send, dg[top - at : top - at + 128], slice(to, to + 128))
        else:
            ug_o[:, cols] = ug
            dg_o[cols, :] = dg
        sums_o[2:3, cols] = us
    if last:
        for line in (0, 1, 3):
            sums_o[line : line + 1] = sums_in[line : line + 1]
        return
    u_o[...] = (total * gain).astype(u_o.dtype)
    gs = jnp.sum(total * xhat, axis=0, keepdims=True)
    ss = jnp.sum(total, axis=0, keepdims=True)
    os = jnp.sum(grad.astype(F32), axis=0, keepdims=True)
    if not first:
        gs, ss, os = gs + sums_in[0:1], ss + sums_in[1:2], os + sums_in[3:4]
    sums_o[0:1] = gs
    sums_o[1:2] = ss
    sums_o[3:4] = os


def input_kernel(row, lengths, weights, x0, *refs):
    x1, (up, dense, vectors, hgrad, sums, *rest) = pair_of(True, refs)
    cgrad_o, u_o, sums_o = rest[-3:]
    c, y = spot()
    tokens = place_two(c, x0[0], x1[0])
    probe = place_two(c, x0[1], x1[1])
    total = mm(hgrad[...], up[...], NT)
    grad = out_grad_of(probe, (1 - y) * tokens.shape[0], lengths[row], weights[row])
    context_grad(grad, dense, cgrad_o)
    xhat, _ = norm_parts(tokens)
    u_o[...] = (total * vectors[2:3]).astype(u_o.dtype)
    sums_o[0:1] = sums[0:1] + jnp.sum(total * xhat, axis=0, keepdims=True)
    sums_o[1:2] = sums[1:2] + jnp.sum(total, axis=0, keepdims=True)
    sums_o[2:3] = sums[2:3]
    sums_o[3:4] = sums[3:4] + jnp.sum(grad.astype(F32), axis=0, keepdims=True)


def attend_kernel(row, lengths, near, far, cg_near, cg_far, cos_t, low_t, high_t, *rest):
    ctx_o, jg_o, q_s, k_s, v_s, c_s, kt_s, vt_s, ct_s, dk_s, dv_s = rest[-11:]
    _, y = spot()
    length = lengths[row]
    half = near.shape[0]
    slots = 2 * half
    block = 256
    for source, cg, place in ((near, cg_near, y), (far, cg_far, 1 - y)):
        spots = pl.ds(pl.multiple_of(place * half, half), half)
        q_s[spots, :] = source[:, 0:256]
        k_s[spots, :] = source[:, 256:512]
        v_s[spots, :] = source[:, 512:768]
        c_s[spots, :] = cg[...]
    kt_s[...] = k_s[...].T
    vt_s[...] = v_s[...].T
    ct_s[...] = c_s[...].T
    heads, blocks = 3, slots // block
    least = slots * 5 // 8
    lane = lax.broadcasted_iota(jnp.int32, (block, LANES), 1)
    key = lax.broadcasted_iota(jnp.int32, (block, block), 0)
    below = key <= lax.broadcasted_iota(jnp.int32, (block, block), 1)

    def part(j):
        return slice(j * block, j * block + block)

    def places(h):
        pair = (h // 2) * LANES
        return slice(pair, pair + LANES), slice(h * HEAD, h * HEAD + HEAD)

    def products(i, h):
        lanes, _ = places(h)
        q, cg = q_s[part(i), lanes], c_s[part(i), lanes]
        if h < 2:
            mine = (lane < HEAD) if h == 0 else (lane >= HEAD)
            q = jnp.where(mine, q, jnp.zeros_like(q))
            cg = jnp.where(mine, cg, jnp.zeros_like(cg))
        scores = [mm(k_s[part(j), lanes], q, NT) for j in range(i + 1)]
        pgrad = [mm(v_s[part(j), lanes], cg, NT) for j in range(i + 1)]
        return q, cg, scores, pgrad

    def softmax(i, scores):
        for j in range(i + 1):
            allowed = below if j == i else None
            if (j + 1) * block > least:
                inside = key < length - j * block
                allowed = inside if allowed is None else allowed & inside
            if allowed is not None:
                scores[j] = jnp.where(allowed, scores[j], BIG)
        peak = jnp.max(functools.reduce(jnp.maximum, scores), axis=0, keepdims=True)
        raised = [jnp.exp(x - peak) for x in scores]
        scale = 1.0 / jnp.sum(functools.reduce(jnp.add, raised), axis=0, keepdims=True)
        probs = [x * scale for x in raised]
        return probs, [x.astype(BF16) for x in probs]

    def middle(i, h, probs, low, pgrad):
        _, lines = places(h)
        ctx = functools.reduce(jnp.add, [mm(vt_s[lines, part(j)], low[j]) for j in range(i + 1)])
        inner = jnp.sum(ct_s[lines, part(i)].astype(F32) * ctx, axis=0, keepdims=True)
        return ctx, [(p * (g - inner)).astype(BF16) for p, g in zip(probs, pgrad)]

    def gradients(i, h, q, cg, low, sgrad):
        lanes, lines = places(h)
        dq = functools.reduce(jnp.add, [mm(kt_s[lines, part(j)], sgrad[j]) for j in range(i + 1)])
        for j in range(i + 1):
            dk, dv = mm(sgrad[j], q), mm(low[j], cg)
            if i == blocks - 1 and h != 1:
                dk_s[part(j), lanes] = dk
                dv_s[part(j), lanes] = dv
            else:
                dk_s[part(j), lanes] += dk
                dv_s[part(j), lanes] += dv
        return dq

    def finish(i, pieces):
        rows = part(i)
        empty = jnp.zeros((256 - heads * HEAD, block), F32)
        ctx_o[rows, :] = jnp.concatenate([p[0] for p in pieces] + [empty], axis=0).T.astype(BF16)
        dq = jnp.concatenate([p[1] for p in pieces] + [empty], axis=0).T * (1.0 / math.sqrt(HEAD))
        for pair in range(2):
            lanes = slice(pair * LANES, pair * LANES + LANES)
            turned = turn(dq[:, lanes], cos_t[rows, :], low_t[rows, :], high_t[rows, :], -1.0)
            jg_o[rows, lanes] = turned.astype(BF16)
            turned = turn(dk_s[rows, lanes], cos_t[rows, :], low_t[rows, :], high_t[rows, :], -1.0)
            jg_o[rows, 256 + pair * LANES : 256 + pair * LANES + LANES] = turned.astype(BF16)
        jg_o[rows, 512:768] = dv_s[rows, :].astype(BF16)

    tasks = [(i, h) for i in range(blocks - 1, -1, -1) for h in range(heads)]
    pieces, waiting = [], None
    ahead = products(*tasks[0])
    for number in range(len(tasks) + 1):
        if number < len(tasks):
            i, h = tasks[number]
            q, cg, scores, pgrad = ahead
            if number + 1 < len(tasks):
                ahead = products(*tasks[number + 1])
            probs, low = softmax(i, scores)
        if waiting is not None:
            old_i, old_h, ctx, *rest = waiting
            pieces.append((ctx, gradients(old_i, old_h, *rest)))
            if old_h == heads - 1:
                finish(old_i, pieces)
                pieces = []
        if number < len(tasks):
            ctx, sgrad = middle(i, h, probs, low, pgrad)
            waiting = i, h, ctx, q, cg, low, sgrad


def close_kernel(row, first, phased, lengths, weights, x0, x1, x2, x3, x4, ctx, jg, act_n, act_f, u_n, u_f, weight, dense,
                 down, vectors, *rest):
    if first:
        qg_in = sg_in = mg_in = None
        send, keep, qg_o, sums_o = rest[-4:]
    else:
        qg_in, sg_in, mg_in = rest[:3]
        send, keep, a_keep, a_send, b_keep, b_send, sums_o = rest[-7:]
    c, y = spot()
    length = lengths[row]
    gain, shift = vectors[0:1], vectors[1:2]
    block = x0.shape[1]
    gs = ss = bs = qg = dg = None
    for x, act, u, side, slot, out, at in (
        (x2, act_f, u_f, 1 - y, c, keep, 0),
        ((x3, x4), act_f, u_f, 1 - y, 1 - c, send, 0),
        (x0, act_n, u_n, y, c, keep, 2),
        (x1, act_n, u_n, y, 1 - c, send, 2),
    ):
        place = 2 * side + slot
        whole = pl.ds(pl.multiple_of(place * block, block), block)
        part = pl.ds(pl.multiple_of(slot * block, block), block)
        context, joined = ctx[whole, :], jg[whole, :]
        out[at] = (mm(context[:, : dense.shape[0]], dense[...]) + mm(act[part, :], down[...])).astype(BF16)
        first_grad = mm(joined, weight[...])
        xhat, _ = norm_parts(x[0][...])
        normed = (xhat * gain + shift).astype(BF16)
        grad = out_grad_of(x[1][...], place * block, length, weights[row])
        out[at + 1] = (first_grad * gain + u[part, :].astype(F32)).astype(BF16)
        pieces = (
            jnp.sum(first_grad * xhat, axis=0, keepdims=True),
            jnp.sum(first_grad, axis=0, keepdims=True),
            jnp.sum(joined.astype(F32), axis=0, keepdims=True),
            mm(joined, normed, TN),
            mm(context, grad, TN),
        )
        if gs is None:
            gs, ss, bs, qg, dg = pieces
        else:
            gs, ss, bs, qg, dg = (a + b for a, b in zip((gs, ss, bs, qg, dg), pieces))
    if first:
        qg_o[0:768] = qg
        qg_o[768:1024] = dg
        sums_o[0:1] = gs
        sums_o[1:2] = ss
        sums_o[2:3] = bs
        return
    bit_a = bit_b = wide_bits(phased)[0]
    half = a_keep.shape[0]
    for h in range(3):
        for part in range(3):
            at, to = part * 256 + h * HEAD, (h * 3 + part) * HEAD
            value = (qg[at : at + HEAD] + qg_in[at : at + HEAD]).astype(BF16)
            number, to = to // half, to % half
            if number < 2:
                put(bit_a, number, a_keep, a_send, value, slice(to, to + HEAD))
            else:
                put(bit_b, 0, b_keep, b_send, value, slice(to, to + HEAD))
    value = (dg[0:half] + qg_in[768 : 768 + half]).astype(BF16)
    put(bit_b, 1, b_keep, b_send, value, slice(None))
    small = jnp.concatenate(
        [
            gs + sg_in[0:1],
            ss + sg_in[1:2],
            mg_in[0:2],
            bs + sg_in[2:3],
            mg_in[2:4],
            jnp.zeros_like(gs),
        ],
        axis=0,
    )
    sums_o[...] = small
    a_send[half : half + 16] = high_low(small)


def plus(a, b):
    return (a.astype(F32) + b.astype(F32)).astype(BF16)


def rows_of(number, size):
    return pl.ds(pl.multiple_of(number * size, size), size)


def join_1(u_keep, u_got, d_keep, d_got, *rest):
    u_keep_o, u_send_o, d_keep_o, d_send_o = rest[-4:]
    x, z, _ = wide_bits(True)
    size = u_keep_o.shape[0]
    for keep, got, bit, keep_o, send_o in ((u_keep, u_got, z, u_keep_o, u_send_o), (d_keep, d_got, x, d_keep_o, d_send_o)):
        mine, other = rows_of(bit, size), rows_of(1 - bit, size)
        send_o[...] = plus(keep[other, :], got[other, :])
        keep_o[...] = plus(keep[mine, :], got[mine, :])


def join_2(u_keep, u_got, d_keep, d_got, *rest):
    both = rest[-1]
    both[0] = plus(u_keep[...], u_got[...])
    both[1] = plus(d_keep[...], d_got[...])


def join_far(keep0, got0, keep1, got1, *rest):
    out = rest[-1]
    out[0:2] = plus(keep0[0:2], got0[0:2])
    out[2:4] = plus(keep1[0:2], got1[0:2])


def join_3(both, both_got, *rest):
    u_o, d_o = rest[-2:]
    u_o[...] = plus(both[0], both_got[0])
    d_o[...] = plus(both[1], both_got[1])


def join_4(u, u_got, d, d_got, *rest):
    u_o, d_o = rest[-2:]
    x, z, _ = wide_bits(True)
    size = u.shape[0]
    for own, got, bit, out in ((u, u_got, z, u_o), (d, d_got, x, d_o)):
        out[rows_of(bit, size), :] = own[...]
        out[rows_of(1 - bit, size), :] = got[...]


def last_1(a_keep, a_got, b_keep, b_got, small, *rest):
    a_keep_o, b_keep_o, send_o, small_o = rest[-4:]
    _, z, _ = wide_bits(True)
    part = a_keep_o.shape[0]
    mine, other = rows_of(z, part), rows_of(1 - z, part)
    for keep, got, keep_o, to in ((a_keep, a_got, a_keep_o, 0), (b_keep, b_got, b_keep_o, part + 16)):
        send_o[to : to + part] = plus(keep[other, :], got[other, :])
        keep_o[...] = plus(keep[mine, :], got[mine, :])
    total = small[...] + back_together(a_got[2 * part : 2 * part + 16])
    small_o[...] = total
    send_o[part : part + 16] = high_low(total)


def last_2(a_keep, b_keep, got, small, *rest):
    last_o, small_o = rest[-2:]
    part = a_keep.shape[0]
    last_o[0:part] = plus(a_keep[...], got[0:part])
    last_o[part : 2 * part] = plus(b_keep[...], got[part + 16 :])
    total = small[...] + back_together(got[part : part + 16])
    small_o[...] = total
    last_o[2 * part : 2 * part + 16] = high_low(total)


def last_3(last, last_got, small, *rest):
    a_o, b_o, small_o = rest[-3:]
    part = a_o.shape[0]
    a_o[...] = plus(last[0:part], last_got[0:part])
    b_o[...] = plus(last[part : 2 * part], last_got[part : 2 * part])
    small_o[...] = small[...] + back_together(last_got[2 * part : 2 * part + 16])


def widen_kernel(u, u_got, d, d_got, *rest):
    u_o, d_o, sign = rest[-3:]
    sign[...] = jnp.zeros_like(sign)
    x, z, _ = wide_bits(True)
    half = u.shape[0]
    for own, got, bit, out in ((u, u_got, x, u_o), (d, d_got, z, d_o)):
        out[rows_of(bit, half), :] = own[...].astype(F32)
        out[rows_of(1 - bit, half), :] = got[...].astype(F32)


def last_kernel(a, a_got, b, b_got, *rest):
    q_o, dense_o = rest[-2:]
    x, z, _ = wide_bits(True)
    half = a.shape[0]
    part = half // 2
    q_o[rows_of(x, half), :] = a[...].astype(F32)
    q_o[rows_of(1 - x, half), :] = a_got[...].astype(F32)
    for own, place in ((b, z), (b_got, 1 - z)):
        q_o[rows_of(4 + place, part), :] = own[0:part].astype(F32)
        dense_o[rows_of(place, part), :] = own[part:half].astype(F32)


def final_kernel(lengths, weights, own0, keep0, got0, own1, keep1, got1, far, vectors, *rest):
    block_o, grad_o, sign = rest[-3:]
    sign[...] = jnp.zeros_like(sign)
    block = own0.shape[1]
    slot = lax.axis_index("narrow") * block + lax.broadcasted_iota(jnp.int32, (block, 1), 0)
    for row, (own, keep, got) in enumerate(((own0, keep0, got0), (own1, keep1, got1))):

        @pl.when(pl.program_id(0) == row)
        def _():
            near = keep[2:4].astype(F32) + got[2:4].astype(F32) + far[2 * row : 2 * row + 2].astype(F32)
            values = own[0].astype(F32)
            block_o[0] = (values + (near[0] + vectors[6:7] + vectors[7:8])).astype(BF16)
            xhat, inverse = norm_parts(own[0])
            u = near[1]
            scale = jnp.where(slot < lengths[row], weights[row], 0.0)
            mean = jnp.mean(u, axis=-1, keepdims=True)
            lean = jnp.mean(u * xhat, axis=-1, keepdims=True)
            grad_o[0] = own[1].astype(F32) * scale + inverse * (u - mean - xhat * lean)


def vector_kernel(small, mate, far, *rest):
    outs = rest[-8:]
    place = lax.axis_index("narrow")
    total = small[...] + mate[...] + far[...]
    own = small[...]
    share = outs[0].shape[0]
    for number in range(small.shape[1] // share):

        @pl.when(place == number)
        def _():
            at = number * share
            for line in range(4):
                outs[line][...] = total[line : line + 1, at : at + share].reshape(share)
            for out in outs[6:8]:
                out[...] = own[6:7, at : at + share].reshape(share)

    pieces = [own[4:5, part * 256 + h * HEAD : part * 256 + h * HEAD + HEAD] for h in range(3) for part in range(3)]
    outs[4][...] = jnp.concatenate(pieces, axis=1).reshape(9 * HEAD)
    outs[5][...] = own[5:6].reshape(own.shape[1])


SMEM = functools.partial(pl.BlockSpec, memory_space=pltpu.SMEM)
VMEM = functools.partial(pl.BlockSpec, memory_space=pltpu.VMEM)
ANY = functools.partial(pl.BlockSpec, memory_space=pl.ANY)
HBM = functools.partial(pl.BlockSpec, memory_space=pltpu.HBM)
COST = 1e8
WAIT = {'join_1': 200, 'join_2': 200, 'join_3': 200, 'join_far': 200}


def call(body, outs, scalars, arrays, name, us, scratch=(), limit=8, after=()):
    return pl.pallas_call(
        body,
        out_shape=outs,
        in_specs=[SMEM()] * len(scalars) + [VMEM()] * len(arrays) + [ANY()] * len(after),
        out_specs=[VMEM()] * len(outs),
        scratch_shapes=list(scratch),
        compiler_params=pltpu.CompilerParams(vmem_limit_bytes=limit * 1024 * 1024),
        cost_estimate=pl.CostEstimate(flops=int(us * COST), bytes_accessed=0, transcendentals=0),
        name=name,
    )(*scalars, *arrays, *after)


def exchange(x, axis, bit):
    size = lax.axis_size(axis)
    return lax.ppermute(x, axis, [(i, i ^ (1 << bit)) for i in range(size)])


def add_low(a, b):
    return (a.astype(F32) + b.astype(F32)).astype(BF16)


def scatter_sum(x, axis, bits):
    place = lax.axis_index(axis)
    for bit in bits:
        half = x.shape[0] // 2
        mine = (place >> bit) & 1
        keep = lax.dynamic_slice_in_dim(x, mine * half, half, 0)
        send = lax.dynamic_slice_in_dim(x, (1 - mine) * half, half, 0)
        x = add_low(keep, exchange(send, axis, bit))
    return x


def gather_back(x, axis, bits):
    place = lax.axis_index(axis)
    for bit in reversed(bits):
        mine = (place >> bit) & 1
        got = exchange(x, axis, bit)
        x = jnp.where(mine == 0, jnp.concatenate([x, got]), jnp.concatenate([got, x]))
    return x


def rotary(slot_count):
    position = np.arange(slot_count, dtype=np.float64)
    frequency = 10000.0 ** (-(2.0 * np.arange(ROT // 2)) / ROT)
    angles = position[:, None] * frequency[None, :]
    cos, sin = np.cos(angles), np.sin(angles)
    none8, none = np.zeros_like(sin), np.zeros((slot_count, HEAD - ROT))
    cos_t = np.concatenate([cos, cos, none + 1.0], axis=1)
    low_t = np.concatenate([-sin, none8, none], axis=1)
    high_t = np.concatenate([none8, sin, none], axis=1)
    return tuple(jnp.asarray(np.concatenate([t, t], axis=1), F32) for t in (cos_t, low_t, high_t))


def shards(tokens, lengths, tissues, ln1_gain, ln1_bias, qkv_weight, qkv_bias, dense_weight, dense_bias,
           ln2_gain, ln2_bias, up_weight, up_bias, down_weight, down_bias, out_probe):
    rows_local, block, width = tokens.shape
    inner = up_weight.shape[1]
    wide_count, narrow_count = lax.axis_size("wide"), lax.axis_size("narrow")
    place = lax.axis_index("narrow")
    slot_count = block * narrow_count
    bits = list(range(wide_count.bit_length() - 1))
    half_rows = 2 * block
    phased = wide_count == 8

    def shape(*dims, dtype=BF16):
        return jax.ShapeDtypeStruct(dims, dtype)

    def pack(r, after=()):
        return call(pack_kernel, [shape(2, block, width)], [], [tokens[r], out_probe[r]], "pack", 0, after=after)[0]

    def gate(x, after):
        return pl.pallas_call(
            lambda *refs: None,
            out_shape=jax.ShapeDtypeStruct(x.shape, x.dtype),
            in_specs=[ANY()] * (1 + len(after)),
            out_specs=ANY(),
            input_output_aliases={0: 0},
            compiler_params=pltpu.CompilerParams(vmem_limit_bytes=1024 * 1024),
            name="gate",
        )(x, *after)

    own = [pack(0)]
    own.append(pack(1, own))
    over = [exchange(own[0], "narrow", 1)]
    mate = [exchange(x, "narrow", 0) for x in own]
    cross = [None, None]

    tables = rotary(slot_count)
    weight, vectors = call(
        prepare_kernel,
        [shape(768, width), shape(8, width, dtype=F32)],
        [],
        [qkv_weight.T, ln1_gain, ln1_bias, ln2_gain, ln2_bias, up_bias, qkv_bias, dense_bias, down_bias],
        "prepare",
        1,
    )

    def qkv(r, far, after=()):
        units = [over[r], *cross[r]] if far else [own[r], mate[r]]
        return call(
            functools.partial(qkv_kernel, far),
            [shape(half_rows, 768)],
            [],
            [*units, weight, vectors, *tables],
            "qkv",
            3,
            limit=8,
            after=after,
        )[0]

    def mlp(r, far, sums, last, after=()):
        units = [over[r], *cross[r]] if far else [own[r], mate[r]]
        first = sums is None
        return call(
            functools.partial(mlp_kernel, r, far, first, last, phased),
            [
                shape(half_rows, inner),
                *([shape(half_rows, inner)] if last else [shape(half_rows, 256), shape(half_rows, width)]),
                *([shape(width // 2, inner)] * 2 if last else [shape(width, inner, dtype=F32)]),
                *([shape(inner // 2, width)] * 2 if last else [shape(inner, width, dtype=F32)]),
                shape(4, width, dtype=F32),
            ],
            [lengths, row_weight],
            [*units, up_weight, down_weight, dense_weight, vectors, *(sums or [])],
            "mlp",
            7,
            limit=12,
            after=after,
        )

    def attend(r, near, far, cg_near, cg_far, after=()):
        big = pltpu.VMEM((slot_count, 256), BF16)
        tall = pltpu.VMEM((256, slot_count), BF16)
        total = pltpu.VMEM((slot_count, 256), F32)
        return call(
            functools.partial(attend_kernel, r),
            [shape(slot_count, 256), shape(slot_count, 768)],
            [lengths],
            [near, far, cg_near, cg_far, *tables],
            "attend",
            14,
            scratch=[big] * 4 + [tall] * 3 + [total] * 2,
            limit=12,
            after=after,
        )

    def close(r, ctx, jg, acts, us, sums, after=()):
        first = sums is None
        four = shape(4, block, width)
        half = 3 * HEAD
        if first:
            shapes = [four, four, shape(1024, width, dtype=F32), shape(3, width, dtype=F32)]
        else:
            shapes = [four, four, shape(half, width), shape(half + 16, width), shape(half, width), shape(half, width)]
            shapes.append(shape(8, width, dtype=F32))
        return call(
            functools.partial(close_kernel, r, first, phased),
            shapes,
            [lengths, row_weight],
            [own[r], mate[r], over[r], *cross[r], ctx, jg, *acts, *us, weight, dense_weight, down_weight, vectors, *(sums or [])],
            "close",
            0,
            limit=12,
            after=after,
        )

    hits = (tissues[:, None] == jnp.arange(TISSUES)[None, :]).astype(F32)
    counts = jnp.sum(hits * lengths[:, None].astype(F32), axis=0)[None, :]
    counts = counts + exchange(counts, "wide", bits[0])
    near_q0 = qkv(0, False)
    counts = gate(counts, [near_q0])
    counts = counts + exchange(counts, "wide", bits[1])
    near_q1 = qkv(1, False, [counts])
    for bit in bits[2:]:
        counts = counts + exchange(counts, "wide", bit)
    row_count = jnp.sum(hits * counts, axis=1)
    row_weight = rows_local * wide_count * slot_count / TISSUES / row_count
    over.append(exchange(gate(own[1], [near_q1]), "narrow", 1))
    a00, cg00, u00, *sums = mlp(0, False, None, False, [near_q1])
    a10, cg10, u10, *sums = mlp(1, False, sums, False)
    over[0] = gate(over[0], [sums[2]])
    cross[0] = [exchange(over[0][k], "narrow", 0) for k in range(2)]
    a01, cg01, u01, *sums = mlp(0, True, sums, False)
    far_q0 = qkv(0, True, [sums[2]])
    over[1] = gate(over[1], [far_q0])
    cross[1] = [exchange(over[1][k], "narrow", 0) for k in range(2)]
    a11, hgrad, u_keep, u_send, d_keep, d_send, mlp_sums = mlp(1, True, sums, True)

    def final(far, after=()):
        spec = pl.BlockSpec((1, block, width), lambda i: (i, 0, 0))
        return pl.pallas_call(
            final_kernel,
            grid=(rows_local,),
            out_shape=[
                shape(rows_local, block, width),
                shape(rows_local, block, width, dtype=F32),
                shape(8, LANES, dtype=F32),
            ],
            in_specs=[SMEM()] * 2 + [VMEM()] * 8 + [ANY()] * len(after),
            out_specs=[spec, spec, pl.BlockSpec((8, LANES), lambda i: (0, 0))],
            compiler_params=pltpu.CompilerParams(vmem_limit_bytes=12 * 1024 * 1024),
            cost_estimate=pl.CostEstimate(flops=int(2.5 * COST), bytes_accessed=0, transcendentals=0),
            name="final",
        )(lengths, row_weight, own[0], keep0, got0, own[1], keep1, got1, far, vectors, *after)

    def join(body, shapes, arrays, after=(), us=0):
        return call(body, shapes, [], arrays, body.__name__, WAIT.get(body.__name__, us), after=after)

    far_q1 = qkv(1, True, [mlp_sums])
    cg11, u11, mlp_sums = call(
        functools.partial(input_kernel, 1),
        [shape(half_rows, 256), shape(half_rows, width), shape(4, width, dtype=F32)],
        [lengths, row_weight],
        [over[1], *cross[1], up_weight, dense_weight, vectors, hgrad, mlp_sums],
        "inputs",
        2,
        limit=12,
        after=[far_q1],
    )
    ctx0, jg0 = attend(0, near_q0, far_q0, cg00, cg01, [mlp_sums])
    quarter = width // 4
    part = quarter // 2
    if phased:
        u_keep, u_send, d_keep, d_send = join(
            join_1,
            [shape(quarter, width)] * 4,
            [u_keep, exchange(u_send, "wide", 0), d_keep, exchange(d_send, "wide", 1)],
            [ctx0],
        )
    ctx1, jg1 = attend(1, near_q1, far_q1, cg10, cg11, [ctx0, u_keep] if phased else [ctx0])
    if phased:
        (both,) = join(
            join_2,
            [shape(2, quarter, width)],
            [u_keep, exchange(u_send, "wide", 1), d_keep, exchange(d_send, "wide", 0)],
            [ctx1],
        )
        both_got = exchange(both, "wide", 2)
    send0, keep0, qg, close_sums = close(
        0, ctx0, jg0, (a00, a01), (u00, u01), None, [ctx1, both] if phased else [ctx1]
    )
    got0 = exchange(send0, "narrow", 0)
    send1, keep1, a_keep, a_send, b_keep, b_send, small = close(
        1, ctx1, jg1, (a10, a11), (u10, u11), [qg, close_sums, mlp_sums]
    )
    got1 = exchange(send1, "narrow", 0)
    if phased:
        tiny = shape(8, width, dtype=F32)
        a_keep, b_keep, step_send, small = join(
            last_1,
            [shape(part, width), shape(part, width), shape(quarter + 16, width), tiny],
            [a_keep, exchange(a_send, "wide", 0), b_keep, exchange(b_send, "wide", 0), small],
        )
        u_part, d_part = join(join_3, [shape(quarter, width)] * 2, [both, both_got], [a_keep])
        far = join(join_far, [shape(4, block, width)], [keep0, got0, keep1, got1], [u_part])[0]
        far_got = exchange(far, "narrow", 1)
        last, small = join(
            last_2,
            [shape(quarter + 16, width), tiny],
            [a_keep, b_keep, exchange(step_send, "wide", 1), small],
            [far],
        )
        last_got = exchange(last, "wide", 2)
        u_half, d_half = join(
            join_4,
            [shape(2 * quarter, width)] * 2,
            [u_part, exchange(u_part, "wide", 1), d_part, exchange(d_part, "wide", 0)],
            [last],
            us=10,
        )
        a_part, b_part, small = join(
            last_3, [shape(part, width), shape(part, width), tiny], [last, last_got, small], [u_half]
        )
        a_half, b_half = join(
            join_4,
            [shape(quarter, width)] * 2,
            [a_part, exchange(a_part, "wide", 1), b_part, exchange(b_part, "wide", 0)],
            us=20,
        )
        block_out, grad_tokens, sign = final(far_got, [a_half])
        up_grad, down_grad, sign = join(
            widen_kernel,
            [shape(width, inner, dtype=F32), shape(inner, width, dtype=F32), shape(8, LANES, dtype=F32)],
            [u_half, exchange(u_half, "wide", 0), d_half, exchange(d_half, "wide", 1)],
            [sign],
        )
        q_grad, dense_grad = join(
            last_kernel,
            [shape(9 * HEAD, width, dtype=F32), shape(3 * HEAD, width, dtype=F32)],
            [a_half, exchange(a_half, "wide", 0), b_half, exchange(b_half, "wide", 1)],
            [sign],
        )
    else:
        far = join(join_far, [shape(4, block, width)], [keep0, got0, keep1, got1])[0]
        far_got = exchange(far, "narrow", 1)
        block_out, grad_tokens, sign = final(far_got)

        def total(keep, send):
            return gather_back(scatter_sum(jnp.concatenate([keep, send]), "wide", bits), "wide", bits).astype(F32)

        up_grad, down_grad = total(u_keep, u_send), total(d_keep, d_send)
        a, b = total(a_keep, a_send[:quarter]), total(b_keep, b_send)
        q_grad, dense_grad = jnp.concatenate([a, b[:quarter]]), b[quarter:]
        for bit in bits:
            small = small + exchange(small, "wide", bit)

    share = width // narrow_count
    if phased:
        small = gate(small, [a_half])
    far_small = exchange(small, "narrow", 1)
    mate_small = exchange(small + far_small, "narrow", 0)
    line = shape(share, dtype=F32)
    gain_1, shift_1, gain_2, shift_2, q_bias_grad, up_bias_grad, dense_bias_grad, down_bias_grad = join(
        vector_kernel,
        [line, line, line, line, shape(9 * HEAD, dtype=F32), shape(inner, dtype=F32), line, line],
        [small, mate_small, far_small],
        [sign],
    )
    return (
        block_out,
        grad_tokens,
        gain_1,
        shift_1,
        q_grad.T,
        q_bias_grad,
        dense_grad,
        dense_bias_grad,
        gain_2,
        shift_2,
        up_grad,
        up_bias_grad,
        down_grad,
        down_bias_grad,
    )


def solution(mesh):
    placed = (
        P("wide", "narrow", None),
        P("wide"),
        P("wide"),
        P(),
        P(),
        P(None, "narrow"),
        P("narrow"),
        P("narrow", None),
        P(),
        P(),
        P(),
        P(None, "narrow"),
        P("narrow"),
        P("narrow", None),
        P(),
        P("wide", "narrow", None),
    )
    return jax.shard_map(
        shards,
        mesh=mesh,
        in_specs=placed,
        out_specs=(
            P("wide", "narrow", None),
            P("wide", "narrow", None),
            P("narrow"),
            P("narrow"),
            P(None, "narrow"),
            P("narrow"),
            P("narrow", None),
            P("narrow"),
            P("narrow"),
            P("narrow"),
            P(None, "narrow"),
            P("narrow"),
            P("narrow", None),
            P("narrow"),
        ),
        check_vma=False,
    )
```
